512 devices in a mesh: cell: 128 (over y, z, core), img: 4 (over x).
Axes of the slice: x: 4, y: 8, z: 8, core: 2. Of those that a mesh axis runs over, the one named last changes fastest.
Arguments:
- proj: float32 [4, 6, 1048576], P('img', None, 'cell'), as said below
- sh_coeffs: float32 [48, 1048576], P(None, 'cell'), may hold values from -2 to 2
- positions: float32 [3, 1048576], P(None, 'cell'), may hold values from -2 to 2
- camera: float32 [4, 3], P('img'), as said below
- send_index: int32 [4, 524288], P('img', 'cell'), may hold values from 0 to 8191
- send_count: int32 [4, 16384], P('img', 'cell'), may hold values from 1 to 32, as said below
- tile_xy: int32 [4, 2, 512], P('img', None, 'cell'), may hold values from 0 to 31
- tile_list: int32 [4, 512, 256], P('img', 'cell'), may hold values from 0 to 4095, as said below
- tile_len: int32 [4, 512], P('img', 'cell'), may hold values from 1 to 256, as said below
- pixel_grad: float32 [4, 3, 131072], P('img', None, 'cell'), may hold values from -6 to 6
Outputs:
- grad_proj: float32 [4, 6, 1048576], P('img', None, 'cell')
- grad_sh: float32 [48, 1048576], P(None, ('cell', 'img'))
The draws below stay inside these ranges and needn't reach their ends.
Inputs may be any that keep to these rules, and one draw needn't show every extreme that they name: `send_count`: for every image and owner, some renderer receives exactly 32 live slots from it. `tile_list`: an entry p * 32 + q of a tile's list always has q below send_count of owner p toward that tile's renderer. `tile_len`: every image has a tile with 256 live entries. `proj`: means lie in 0 to 4, the conic is positive definite with a and c from 0.2 to 13, opacity lies in 0.002 to 0.06. `camera`: camera heights lie in 6 to 10, other coordinates in -2 to 2.
All inputs are finite; a program needn't handle non-finite values.
Results may differ from the reference program's by a relative error of at most 0.0003.
Values sent between devices are 32-bit elements; how exact they have to be, the bound alone decides.
No kernel may reach another device: no remote copies, remote signals or barrier semaphores. Data moves between devices by JAX's collectives and lax.ppermute only.
A program may use at most 64 MiB of HBM per device.

```python
import jax
import jax.numpy as jnp
from jax import lax

G_DEV = 8192
CAP = 32
TILES_DEV = 4
DEPTH = 256
PIX = 256
GAUSS = 1048576
IMGS = 4
SLOTS = 4096
TILES = 512
N_CELL = 128


def count_table(key):
    key = jax.random.fold_in(key, 101)
    counts = jax.random.randint(key, (IMGS, N_CELL, N_CELL), 1, CAP + 1)
    chosen = jax.random.randint(jax.random.fold_in(key, 1), (IMGS, N_CELL, 1), 0, N_CELL)
    full = jnp.arange(N_CELL)[None, None, :] == chosen
    return jnp.where(full, CAP, counts)


def draw_send_count(key, part):
    table = count_table(key)
    return table.reshape(IMGS, N_CELL * N_CELL).astype(jnp.int32)


def draw_tile_list(key, part):
    table = count_table(key)
    key = jax.random.fold_in(key, 7)
    peer = jax.random.randint(jax.random.fold_in(key, 1), (IMGS, TILES, DEPTH), 0, N_CELL)
    renderer = (jnp.arange(TILES) // TILES_DEV)[None, :, None]
    image = jnp.arange(IMGS)[:, None, None]
    bound = table[image, peer, renderer]
    place = jax.random.randint(jax.random.fold_in(key, 2), (IMGS, TILES, DEPTH), 0, bound)
    return (peer * CAP + place).astype(jnp.int32)


def draw_tile_len(key, part):
    key = jax.random.fold_in(key, 11)
    upper = jax.random.randint(jax.random.fold_in(key, 1), (IMGS, N_CELL), DEPTH // 4, DEPTH + 1)
    upper = jnp.repeat(upper, TILES_DEV, axis=1)
    lengths = jax.random.randint(jax.random.fold_in(key, 2), (IMGS, TILES), 1, upper + 1)
    chosen = jax.random.randint(jax.random.fold_in(key, 3), (IMGS, 1), 0, TILES)
    return jnp.where(jnp.arange(TILES)[None, :] == chosen, DEPTH, lengths).astype(jnp.int32)


def draw_proj(key, part):
    key = jax.random.fold_in(key, 21)
    keys = jax.random.split(key, 6)
    shape = (IMGS, GAUSS)
    mean_x = jax.random.uniform(keys[0], shape, jnp.float32, 0.0, 4.0)
    mean_y = jax.random.uniform(keys[1], shape, jnp.float32, 0.0, 4.0)
    sigma_x = jnp.exp(jax.random.uniform(keys[2], shape, jnp.float32, jnp.log(0.4), jnp.log(2.0)))
    sigma_y = jnp.exp(jax.random.uniform(keys[3], shape, jnp.float32, jnp.log(0.4), jnp.log(2.0)))
    corr = jax.random.uniform(keys[4], shape, jnp.float32, -0.7, 0.7)
    opacity = jnp.exp(jax.random.uniform(keys[5], shape, jnp.float32, jnp.log(0.002), jnp.log(0.06)))
    spare = 1.0 - corr * corr
    conic_a = 1.0 / (sigma_x * sigma_x * spare)
    conic_c = 1.0 / (sigma_y * sigma_y * spare)
    conic_b = -corr / (sigma_x * sigma_y * spare)
    return jnp.stack([mean_x, mean_y, conic_a, conic_b, conic_c, opacity], axis=1)


def draw_camera(key, part):
    key = jax.random.fold_in(key, 31)
    flat = jax.random.uniform(jax.random.fold_in(key, 1), (IMGS, 2), jnp.float32, -2.0, 2.0)
    height = jax.random.uniform(jax.random.fold_in(key, 2), (IMGS, 1), jnp.float32, 6.0, 10.0)
    return jnp.concatenate([flat, height], axis=1)


def touch_ends(entries, rng, least, high):
    spot = [jax.random.randint(jax.random.fold_in(rng, axis), (), 0, length) for axis, length in enumerate(entries.shape)]
    widest = entries.shape.index(max(entries.shape))
    neighbour = spot[:widest] + [(spot[widest] + 1) % entries.shape[widest]] + spot[widest + 1:]
    return entries.at[tuple(spot)].set(least).at[tuple(neighbour)].set(high)


def levels(key, extent, shards, smallest, high):
    def one(axis_at, shards_of):
        heights = jax.random.uniform(jax.random.fold_in(jax.random.fold_in(key, 6), axis_at), (shards_of,), jnp.float32, smallest / len(shards), high / len(shards))
        return jnp.repeat(jnp.exp(heights), extent[axis_at] // shards_of).reshape((-1,) + (1,) * (len(extent) - axis_at - 1))

    gain = one(*shards[0])
    for cut in shards[1:]:
        gain = gain * one(*cut)
    return gain


def gaussian(stream_key, shape, spread, most, shards=(), kind=jnp.bfloat16):
    drawn = spread * jax.random.normal(stream_key, shape, jnp.float32)
    if shards:
        drawn = drawn * levels(stream_key, shape, shards, -0.22, 0.18)
    return jnp.clip(drawn, -most, most).astype(kind)


def setup_inputs(seed: int = 0) -> dict:
    seeds = jax.random.split(jax.random.key(seed), 11)
    proj = draw_proj(jax.random.fold_in(seeds[10], 71), 0)
    sh_coeffs = gaussian(seeds[1], (48, GAUSS), 0.3, 2.0, ((1, 128),), jnp.float32)
    positions = jnp.clip(jax.random.uniform(seeds[2], (3, GAUSS), jnp.float32, -2.0, 2.0) * levels(seeds[2], (3, GAUSS), ((1, 128),), -0.4, 0.0), -2.0, 2.0)
    camera = draw_camera(jax.random.fold_in(seeds[10], 71), 0)
    send_index = touch_ends(jax.random.randint(seeds[4], (IMGS, N_CELL * SLOTS), 0, G_DEV), jax.random.fold_in(seeds[4], 1), 0, G_DEV - 1).astype(jnp.int32)
    send_count = draw_send_count(jax.random.fold_in(seeds[10], 71), 0)
    tile_xy = touch_ends(jax.random.randint(seeds[6], (IMGS, 2, TILES), 0, 32), jax.random.fold_in(seeds[6], 1), 0, 31).astype(jnp.int32)
    tile_list = draw_tile_list(jax.random.fold_in(seeds[10], 71), 0)
    tile_len = draw_tile_len(jax.random.fold_in(seeds[10], 71), 0)
    pixel_grad = gaussian(seeds[9], (IMGS, 3, TILES * PIX), 1.0, 6.0, ((0, 4), (2, 128)), jnp.float32)
    return dict(proj=proj, sh_coeffs=sh_coeffs, positions=positions, camera=camera, send_index=send_index, send_count=send_count, tile_xy=tile_xy, tile_list=tile_list, tile_len=tile_len, pixel_grad=pixel_grad)


SH_ZERO = 0.28209479177387814
SH_ONE = 0.4886025119029199
SH_TWO = (1.0925484305920792, -1.0925484305920792, 0.31539156525252005, -1.0925484305920792, 0.5462742152960396)
SH_THREE = (-0.5900435899266435, 2.890611442640554, -0.4570457994644658, 0.3731763325901154, -0.4570457994644658, 1.445305721320277, -0.5900435899266435)

def sh_basis(positions, centre):
    offset = positions - centre[:, None]
    length = jnp.sqrt(lax.optimization_barrier(jnp.sum(offset * offset, axis=0)))
    xpos = offset[0] / length
    ypos = offset[1] / length
    zpos = offset[2] / length
    xsq = xpos * xpos
    ysq = ypos * ypos
    zsq = zpos * zpos
    terms = [jnp.full_like(xpos, SH_ZERO), -SH_ONE * ypos, SH_ONE * zpos, -SH_ONE * xpos, SH_TWO[0] * xpos * ypos, SH_TWO[1] * ypos * zpos, SH_TWO[2] * (2.0 * zsq - xsq - ysq), SH_TWO[3] * xpos * zpos, SH_TWO[4] * (xsq - ysq), SH_THREE[0] * ypos * (3.0 * xsq - ysq), SH_THREE[1] * xpos * ypos * zpos, SH_THREE[2] * ypos * (4.0 * zsq - xsq - ysq), SH_THREE[3] * zpos * (2.0 * zsq - 3.0 * xsq - 3.0 * ysq), SH_THREE[4] * xpos * (4.0 * zsq - xsq - ysq), SH_THREE[5] * zpos * (xsq - ysq), SH_THREE[6] * xpos * (xsq - 3.0 * ysq)]
    return jnp.stack(terms, axis=0)

def shade(coeffs, basis):
    return jnp.stack([lax.optimization_barrier(jnp.sum(coeffs[16 * chan:16 * chan + 16] * basis, axis=0)) for chan in range(3)], axis=0) + 0.5

def pixel_coords(tile_col, tile_row):
    local = jnp.arange(256, dtype=jnp.int32)
    upos = (tile_col.astype(jnp.float32) * 16.0 + (local % 16).astype(jnp.float32) + 0.5) / 128.0
    vpos = (tile_row.astype(jnp.float32) * 16.0 + (local // 16).astype(jnp.float32) + 0.5) / 128.0
    return (upos, vpos)

def render_tile(rows, livemask, upos, vpos):
    depth = rows.shape[1]
    delta_x = upos[:, None] - rows[0][None, :]
    delta_y = vpos[:, None] - rows[1][None, :]
    power = -0.5 * (rows[2] * delta_x * delta_x + rows[4] * delta_y * delta_y) - rows[3] * delta_x * delta_y
    alpha = rows[5] * jnp.exp(power) * livemask
    order = jnp.arange(depth, dtype=jnp.int32)
    upper = (order[:, None] < order[None, :]).astype(jnp.float32)
    log_trans = jnp.dot(jnp.log1p(-alpha), upper, precision=lax.Precision.HIGHEST, preferred_element_type=jnp.float32)
    weight = alpha * jnp.exp(log_trans)
    return jnp.dot(rows[6:9], weight.T, precision=lax.Precision.HIGHEST, preferred_element_type=jnp.float32)

def tile_grad(rows, livemask, upos, vpos, cotangent):
    _, pullback = jax.vjp(lambda values: render_tile(values, livemask, upos, vpos), rows)
    return pullback(cotangent)[0]

def reference(proj, sh_coeffs, positions, camera, send_index, send_count, tile_xy, tile_list, tile_len, pixel_grad):
    grad_list = []
    grad_sh = jnp.zeros((48, GAUSS), jnp.float32)
    renderer = jnp.arange(N_CELL, dtype=jnp.int32)[:, None]
    slot = jnp.arange(SLOTS, dtype=jnp.int32)[None, :]
    peer = slot // CAP
    place = slot % CAP
    order = jnp.arange(DEPTH, dtype=jnp.int32)
    for image in range(IMGS):
        basis = sh_basis(positions, camera[image])
        rows = jnp.concatenate([proj[image], shade(sh_coeffs, basis)], axis=0)
        local = send_index[image].reshape(N_CELL, SLOTS)[peer, renderer * CAP + place]
        live = (place < send_count[image].reshape(N_CELL, N_CELL)[peer, renderer]).astype(jnp.float32)
        global_ids = peer * G_DEV + local

        def one_tile(tile):
            owner = tile // TILES_DEV
            slots = tile_list[image, tile]
            ids = global_ids[owner][slots]
            keep = live[owner][slots]
            gathered = rows[:, ids] * keep[None, :]
            livemask = (order < tile_len[image, tile]).astype(jnp.float32)
            upos, vpos = pixel_coords(tile_xy[image, 0, tile], tile_xy[image, 1, tile])
            cotangent = lax.dynamic_slice_in_dim(pixel_grad[image], tile * PIX, PIX, 1)
            return (tile_grad(gathered, livemask, upos, vpos, cotangent) * keep[None, :], ids)
        grads, ids = lax.map(one_tile, jnp.arange(TILES, dtype=jnp.int32))
        flat = jnp.transpose(grads, (1, 0, 2)).reshape(9, TILES * DEPTH)
        total = jnp.zeros((9, GAUSS), jnp.float32).at[:, ids.reshape(-1)].add(flat)
        grad_list.append(total[:6])
        grad_sh = grad_sh + (total[6:9][:, None, :] * basis[None, :, :]).reshape(48, GAUSS)
    return (jnp.stack(grad_list, axis=0), grad_sh)
```

```python
import functools

import jax
import jax.numpy as jnp
from jax import lax
from jax.experimental import pallas as pl
from jax.experimental.pallas import tpu as pltpu
from jax.sharding import PartitionSpec as P

SH_ZERO = 0.28209479177387814
SH_ONE = 0.4886025119029199
SH_TWO = (
    1.0925484305920792,
    -1.0925484305920792,
    0.31539156525252005,
    -1.0925484305920792,
    0.5462742152960396,
)
SH_THREE = (
    -0.5900435899266435,
    2.890611442640554,
    -0.4570457994644658,
    0.3731763325901154,
    -0.4570457994644658,
    1.445305721320277,
    -0.5900435899266435,
)

F32 = jnp.float32
BF16 = jnp.bfloat16
PEERS = 128
CAP = 32
COMPS = 9
TILES = 4
DEPTH = 256
LOW = 256
HIGH = 32
PACK = 56
NOTHING = -1.0e4

LINEAR = (
    (SH_ZERO, 0, 0, 0),
    (0, 0, -SH_ONE, 0),
    (0, 0, 0, SH_ONE),
    (0, -SH_ONE, 0, 0),
    (0, SH_TWO[0], 0, 0),
    (0, 0, SH_TWO[1], 0),
    (SH_TWO[2], 0, 0, 0),
    (0, SH_TWO[3], 0, 0),
    (SH_TWO[4], 0, 0, 0),
    (0, 0, SH_THREE[0], 0),
    (0, SH_THREE[1], 0, 0),
    (0, 0, SH_THREE[2], 0),
    (0, 0, 0, SH_THREE[3]),
    (0, SH_THREE[4], 0, 0),
    (0, 0, 0, SH_THREE[5]),
    (0, SH_THREE[6], 0, 0),
)
QUADRATIC = (
    (1, 0, 0, 0, 0, 0, 0),
    (1, 0, 0, 0, 0, 0, 0),
    (1, 0, 0, 0, 0, 0, 0),
    (1, 0, 0, 0, 0, 0, 0),
    (0, 1, 0, 0, 0, 0, 0),
    (0, 0, 1, 0, 0, 0, 0),
    (0, 0, 0, -1, -1, 2, 0),
    (0, 0, 1, 0, 0, 0, 0),
    (0, 0, 0, 1, -1, 0, 0),
    (0, 0, 0, 3, -1, 0, 0),
    (0, 0, 0, 0, 0, 0, 1),
    (0, 0, 0, -1, -1, 4, 0),
    (0, 0, 0, -3, -3, 2, 0),
    (0, 0, 0, -1, -1, 4, 0),
    (0, 0, 0, 1, -1, 0, 0),
    (0, 0, 0, 1, -3, 0, 0),
)


def dot(left, right):
    return lax.dot_general(left, right, (((1,), (0,)), ((), ())), preferred_element_type=F32)


def dot_t(left, right):
    return lax.dot_general(left, right, (((1,), (1,)), ((), ())), preferred_element_type=F32)


def iota(shape, axis):
    return lax.broadcasted_iota(jnp.int32, shape, axis)


def split(value, parts):
    out = []
    for _ in range(parts - 1):
        head = value.astype(BF16).astype(F32)
        out.append(head)
        value = value - head
    out.append(value.astype(BF16).astype(F32))
    return out


def column_consts(table, half):
    rows = iota((8, 128), 0)
    out = []
    for col in range(len(table[0])):
        vals = [float(table[8 * half + i][col]) for i in range(8)]
        if not any(vals):
            out.append(None)
            continue
        acc = jnp.zeros((8, 128), F32)
        for i, val in enumerate(vals):
            if val:
                acc = jnp.where(rows == i, val, acc)
        out.append(acc)
    return out


def form(consts, values):
    total = None
    for const, value in zip(consts, values):
        if const is None:
            continue
        term = const if value is None else const * value
        total = term if total is None else total + term
    return total


def basis_consts():
    return [(column_consts(LINEAR, half), column_consts(QUADRATIC, half)) for half in range(2)]


def basis_halves(consts, xoff, yoff, zoff):
    inv = lax.rsqrt(xoff * xoff + yoff * yoff + zoff * zoff)
    xpos, ypos, zpos = xoff * inv, yoff * inv, zoff * inv
    xsq, ysq, zsq, yz = xpos * xpos, ypos * ypos, zpos * zpos, ypos * zpos
    return [
        form(lin, (None, xpos, ypos, zpos)) * form(quad, (None, ypos, zpos, xsq, ysq, zsq, yz))
        for lin, quad in consts
    ]


def slot_index(idx_ref, cnt_ref, low_scr, high_scr):
    turned = jnp.transpose(idx_ref[...].astype(F32)).astype(jnp.int32)
    slots = jnp.concatenate([turned[32 * i : 32 * i + 32] for i in range(4)], axis=1)
    rows, cols = iota((PEERS, PEERS), 0), iota((PEERS, PEERS), 1)
    perm = (rows == 4 * (cols & 31) + (cols >> 5)).astype(F32).astype(BF16)
    counts = jnp.broadcast_to(cnt_ref[...], (8, PEERS)).astype(F32).astype(BF16)
    counts = dot(counts, perm)[0:1].astype(jnp.int32)
    live = iota((CAP, PEERS), 0) < counts
    low_scr[...] = slots & (LOW - 1)
    high_scr[...] = jnp.where(live, slots >> 8, -1)


def pair_row(ref, base, pair):
    first = ref[pl.ds(base + 2 * pair, 1), :]
    second = ref[pl.ds(base + 2 * pair + 1, 1), :]
    return jnp.concatenate([first, second], axis=1)


def owner_kernel(
    cam_ref, proj_ref, sh_ref, pos_ref, idx_ref, cnt_ref, out_ref, col_scr, low_scr, high_scr, rows_scr
):
    consts = basis_consts()
    camx, camy, camz = cam_ref[0, 0], cam_ref[0, 1], cam_ref[0, 2]

    def shade(chunk, carry):
        lanes = pl.ds(pl.multiple_of(chunk * 128, 128), 128)
        xoff = jnp.broadcast_to(pos_ref[0:1, lanes], (8, 128)) - camx
        yoff = jnp.broadcast_to(pos_ref[1:2, lanes], (8, 128)) - camy
        zoff = jnp.broadcast_to(pos_ref[2:3, lanes], (8, 128)) - camz
        first, second = basis_halves(consts, xoff, yoff, zoff)
        for chan in range(3):
            terms = sh_ref[16 * chan : 16 * chan + 8, lanes] * first
            terms = terms + sh_ref[16 * chan + 8 : 16 * chan + 16, lanes] * second
            colour = jnp.sum(terms, axis=0, keepdims=True) + 0.5
            col_scr[pl.ds(64 * chan + chunk, 1), :] = colour
        return carry

    lax.fori_loop(0, 64, shade, 0, unroll=4)
    slot_index(idx_ref, cnt_ref, low_scr, high_scr)

    even = jnp.concatenate(
        [proj_ref[pl.ds(0, 192, stride=2), :], col_scr[pl.ds(0, 96, stride=2), :]], axis=0
    )
    odd = jnp.concatenate(
        [proj_ref[pl.ds(1, 192, stride=2), :], col_scr[pl.ds(1, 96, stride=2), :]], axis=0
    )
    parts = [part.astype(BF16) for part in split(jnp.concatenate([even, odd], axis=1), 3)]
    low_iota = iota((LOW, 256), 0)
    high_iota = iota((HIGH, 256), 0)

    def gather(pair, carry):
        low, high = pair_row(low_scr, 0, pair), pair_row(high_scr, 0, pair)
        hot = jnp.where(low_iota == low, 1.0, 0.0).astype(BF16)
        wide = dot(parts[0], hot) + dot(parts[1], hot) + dot(parts[2], hot)
        mask = high_iota == high
        for comp in range(COMPS):
            row = jnp.sum(
                jnp.where(mask, wide[32 * comp : 32 * comp + 32], 0.0), axis=0, keepdims=True
            )
            rows_scr[pl.ds(32 * comp + 2 * pair, 1), :] = row[:, :128]
            rows_scr[pl.ds(32 * comp + 2 * pair + 1, 1), :] = row[:, 128:]
        return carry

    lax.fori_loop(0, CAP // 2, gather, 0, unroll=2)
    rows_scr[32 * COMPS :, :] = jnp.zeros((96, 128), F32)
    for k in range(3):
        turned = jnp.transpose(rows_scr[128 * k : 128 * k + 128, :])
        for i in range(4):
            out_ref[pl.ds(3 * i + k, 32, stride=12), :] = turned[32 * i : 32 * i + 32]


def render_kernel(xy_ref, len_ref, recv_ref, list_ref, grad_ref, out_ref, turn_scr):
    table = jnp.concatenate(
        [
            jnp.transpose(recv_ref[pl.ds(0, PEERS, stride=3), :]),
            jnp.transpose(recv_ref[pl.ds(1, PEERS, stride=3), :]),
            jnp.transpose(recv_ref[pl.ds(2, PEERS, stride=3), :])[0:32],
        ],
        axis=0,
    )
    table = [part.astype(BF16) for part in split(table, 3)]

    blank = jnp.zeros((2, 256), F32)
    blocks, heads, seconds = [], [], []
    for tile in range(TILES):
        grads = jnp.concatenate(
            [
                jnp.concatenate(
                    [grad_ref[8 * c + 2 * tile + h : 8 * c + 2 * tile + h + 1, :] for h in range(2)],
                    axis=1,
                )
                for c in range(3)
            ],
            axis=0,
        )
        g0, g1, g2 = split(grads, 3)
        blocks += [g0, g1, blank, g0, g2, blank, g0, g1, blank, jnp.zeros((8, 256), F32)]
        heads.append(g0)
        seconds.append(g1)
    turned = jnp.transpose(jnp.concatenate(blocks, axis=0)).astype(BF16)

    def powers(pixel, which):
        upos = ((pixel & 15).astype(F32) - 7.5) / 128.0
        vpos = ((pixel >> 4).astype(F32) - 7.5) / 128.0
        out = jnp.where(which == 0, 1.0, 0.0)
        out = jnp.where(which == 1, upos, out)
        out = jnp.where(which == 2, vpos, out)
        out = jnp.where(which == 3, upos * upos, out)
        out = jnp.where(which == 4, vpos * vpos, out)
        return jnp.where(which == 5, upos * vpos, out).astype(BF16)

    phi = powers(iota((256, 32), 0), iota((256, 32), 1) & 7)
    phi_rows = powers(iota((16, 256), 1), iota((16, 256), 0))
    before = (iota((DEPTH, DEPTH), 0) < iota((DEPTH, DEPTH), 1)).astype(F32).astype(BF16)
    after = (iota((DEPTH, DEPTH), 0) > iota((DEPTH, DEPTH), 1)).astype(F32).astype(BF16)
    peer_iota = iota((PEERS, DEPTH), 0)
    place_iota = iota((CAP, DEPTH), 0)
    order = iota((1, DEPTH), 1)
    total = jnp.zeros((PEERS, 384), F32)

    for tile in range(TILES):
        slots = list_ref[tile : tile + 1, :]
        hot = jnp.where(peer_iota == (slots >> 5), 1.0, 0.0).astype(BF16)
        place = place_iota == (slots & (CAP - 1))
        wide = dot(table[0], hot) + dot(table[1], hot) + dot(table[2], hot)
        vals = [
            jnp.sum(jnp.where(place, wide[32 * c : 32 * c + 32], 0.0), axis=0, keepdims=True)
            for c in range(COMPS)
        ]
        mean_x, mean_y, ca, cb, cc, opac = vals[:6]
        xrel = mean_x - (xy_ref[0, tile].astype(F32) * 16.0 + 8.0) / 128.0
        yrel = mean_y - (xy_ref[1, tile].astype(F32) * 16.0 + 8.0) / 128.0
        shown = opac > 0.0
        lead_x = ca * xrel + cb * yrel
        lead_y = cc * yrel + cb * xrel
        const = -0.5 * (xrel * lead_x + yrel * lead_y) + jnp.log(jnp.where(shown, opac, 1.0))
        const = jnp.where(shown & (order < len_ref[0, tile]), const, NOTHING)
        coef = jnp.concatenate(
            [const, lead_x, lead_y, -0.5 * ca, -0.5 * cc, -cb, jnp.zeros((2, DEPTH), F32)], axis=0
        )
        coef = jnp.concatenate(split(coef, 3) + [jnp.zeros((8, DEPTH), F32)], axis=0).astype(BF16)
        alpha = jnp.exp(dot(phi, coef))
        rest = 1.0 - alpha
        logs = jnp.log(rest)
        l0 = logs.astype(BF16)
        l1 = (logs - l0.astype(F32)).astype(BF16)
        weight = alpha * jnp.exp(dot(l0, before) + dot(l1, before))

        k0, k1, k2 = split(jnp.concatenate(vals[6:9], axis=0), 3)
        right = [k0, k0, blank, k1, k0, blank, k2, k1, blank, jnp.zeros((8, DEPTH), F32)]
        right = jnp.concatenate(right, axis=0)
        pad = [jnp.zeros((32 * n, DEPTH), F32) for n in (tile, TILES - 1 - tile) ]
        pieces = ([pad[0]] if tile else []) + [right] + ([pad[1]] if tile < TILES - 1 else [])
        right = jnp.concatenate(pieces, axis=0).astype(BF16)
        flow = dot(turned, right) * weight
        s0 = flow.astype(BF16)
        s1 = (flow - s0.astype(F32)).astype(BF16)
        behind = dot(s0, after) + dot(s1, after)
        power = flow - behind * (alpha / rest)
        p0 = power.astype(BF16)
        p1 = (power - p0.astype(F32)).astype(BF16)
        moments = dot(phi_rows, p0) + dot(phi_rows, p1)
        w0 = weight.astype(BF16)
        w1 = (weight - w0.astype(F32)).astype(BF16)
        zero5 = jnp.zeros((5, 256), F32)
        sides = jnp.concatenate([heads[tile], zero5, seconds[tile], zero5], axis=0).astype(BF16)
        colours = dot(sides, w0)
        colours = colours[0:8] + colours[8:16] + dot(sides, w1)[0:8]

        m0, mu, mv, muu, mvv, muv = [moments[i : i + 1] for i in range(6)]
        grads = [
            ca * mu + cb * mv - lead_x * m0,
            cc * mv + cb * mu - lead_y * m0,
            -0.5 * (muu - 2.0 * xrel * mu + xrel * xrel * m0),
            -(muv - yrel * mu - xrel * mv + xrel * yrel * m0),
            -0.5 * (mvv - 2.0 * yrel * mv + yrel * yrel * m0),
            jnp.where(shown, m0 / jnp.where(shown, opac, 1.0), 0.0),
        ] + [colours[i : i + 1] for i in range(3)]
        fill = jnp.zeros((96, DEPTH), F32)
        heads_tails = [split(grad, 2) for grad in grads]
        for part in range(2):
            wide = jnp.concatenate(
                [jnp.where(place, both[part], 0.0) for both in heads_tails] + [fill], axis=0
            ).astype(BF16)
            total = total + dot_t(hot, wide)
    for k in range(3):
        out_ref[pl.ds(k, PEERS, stride=3), :] = total[:, 128 * k : 128 * k + 128]


def scatter_kernel(
    cam_ref, back_ref, idx_ref, cnt_ref, out_ref, col_ref, low_scr, high_scr, rows_scr, acc_scr
):
    slot_index(idx_ref, cnt_ref, low_scr, high_scr)
    for k in range(3):
        block = jnp.concatenate(
            [back_ref[pl.ds(3 * i + k, 32, stride=12), :] for i in range(4)], axis=0
        )
        rows_scr[128 * k : 128 * k + 128, :] = jnp.transpose(block)
    low_iota = iota((LOW, 256), 0)
    high_iota = iota((HIGH, 256), 0)
    acc_scr[...] = jnp.zeros(acc_scr.shape, F32)

    def scatter(step, carry):
        hots, heads, tails = [], [], []
        for sub in range(4):
            pair = 4 * step + sub
            low, high = pair_row(low_scr, 0, pair), pair_row(high_scr, 0, pair)
            hots.append(jnp.where(low_iota == low, 1.0, 0.0).astype(BF16))
            mask = high_iota == high
            both = [split(pair_row(rows_scr, 32 * comp, pair), 2) for comp in range(COMPS)]
            heads.append(
                jnp.concatenate([jnp.where(mask, b[0], 0.0) for b in both], axis=0).astype(BF16)
            )
            tails.append(
                jnp.concatenate([jnp.where(mask, b[1], 0.0) for b in both], axis=0).astype(BF16)
            )
        hot = jnp.concatenate(hots, axis=1)
        acc_scr[...] += dot_t(jnp.concatenate(heads, axis=1), hot) + dot_t(
            jnp.concatenate(tails, axis=1), hot
        )
        return carry

    lax.fori_loop(0, 4, scatter, 0)
    for par in range(2):
        out_ref[pl.ds(par, 192, stride=2), :] = acc_scr[0:192, 128 * par : 128 * par + 128]
        for share in range(4):
            for chan in range(3):
                first = 192 + 32 * chan + 8 * share
                col_ref[pl.ds(PACK * share + 16 * chan + par, 8, stride=2), :] = acc_scr[
                    first : first + 8, 128 * par : 128 * par + 128
                ]
    lanes = iota((8, 128), 1)
    row = jnp.where(lanes == 0, cam_ref[0, 0], 0.0)
    row = jnp.where(lanes == 1, cam_ref[0, 1], row)
    row = jnp.where(lanes == 2, cam_ref[0, 2], row)
    for share in range(4):
        col_ref[PACK * share + 48 : PACK * share + 56, :] = row


def coeff_kernel(share_ref, col_ref, pos_ref, out_ref):
    consts = basis_consts()
    share = share_ref[0]
    cams = []
    for image in range(4):
        row = col_ref[PACK * image + 48 : PACK * image + 56, :]
        cams.append([jnp.broadcast_to(row[:, i : i + 1], (8, 128)) for i in range(3)])

    def chunk(step, carry):
        lanes = pl.ds(pl.multiple_of(share * 2048 + step * 128, 128), 128)
        place = [jnp.broadcast_to(pos_ref[i : i + 1, lanes], (8, 128)) for i in range(3)]
        totals = [[None, None] for _ in range(3)]
        for image in range(4):
            cam = cams[image]
            halves = basis_halves(
                consts, place[0] - cam[0], place[1] - cam[1], place[2] - cam[2]
            )
            for chan in range(3):
                grad = jnp.broadcast_to(
                    col_ref[pl.ds(PACK * image + 16 * chan + step, 1), :], (8, 128)
                )
                for half in range(2):
                    term = grad * halves[half]
                    old = totals[chan][half]
                    totals[chan][half] = term if old is None else old + term
        here = pl.ds(pl.multiple_of(step * 128, 128), 128)
        for chan in range(3):
            for half in range(2):
                out_ref[16 * chan + 8 * half : 16 * chan + 8 * half + 8, here] = totals[chan][half]
        return carry

    lax.fori_loop(0, 16, chunk, 0, unroll=2)


VMEM = pl.BlockSpec(memory_space=pltpu.VMEM)
SMEM = pl.BlockSpec(memory_space=pltpu.SMEM)
PARAMS = pltpu.CompilerParams(vmem_limit_bytes=40 * 1024 * 1024)


def shape(*dims):
    return jax.ShapeDtypeStruct(dims, F32)


def owner(camera, proj, coeffs, positions, index, count):
    return pl.pallas_call(
        owner_kernel,
        out_shape=shape(384, 128),
        in_specs=[SMEM] + [VMEM] * 5,
        out_specs=VMEM,
        scratch_shapes=[
            pltpu.VMEM((192, 128), F32),
            pltpu.VMEM((CAP, PEERS), jnp.int32),
            pltpu.VMEM((CAP, PEERS), jnp.int32),
            pltpu.VMEM((384, 128), F32),
        ],
        compiler_params=PARAMS,
        name="owner_rows",
    )(camera, proj, coeffs, positions, index, count)


def render(tile_xy, tile_len, received, tile_list, pixel_grad):
    return pl.pallas_call(
        render_kernel,
        out_shape=shape(384, 128),
        in_specs=[SMEM] * 2 + [VMEM] * 3,
        out_specs=VMEM,
        scratch_shapes=[pltpu.VMEM((128, 256), F32)],
        compiler_params=PARAMS,
        name="render_tiles",
    )(tile_xy, tile_len, received, tile_list, pixel_grad)


def scatter(camera, returned, index, count):
    return pl.pallas_call(
        scatter_kernel,
        out_shape=(shape(384, 128), shape(4 * PACK, 128)),
        in_specs=[SMEM] + [VMEM] * 3,
        out_specs=(VMEM, VMEM),
        scratch_shapes=[
            pltpu.VMEM((CAP, PEERS), jnp.int32),
            pltpu.VMEM((CAP, PEERS), jnp.int32),
            pltpu.VMEM((384, 128), F32),
            pltpu.VMEM((32 * COMPS, LOW), F32),
        ],
        compiler_params=PARAMS,
        name="owner_sums",
    )(camera, returned, index, count)


def coefficients(share, colours, positions):
    return pl.pallas_call(
        coeff_kernel,
        out_shape=shape(48, 2048),
        in_specs=[SMEM] + [VMEM] * 2,
        out_specs=VMEM,
        compiler_params=PARAMS,
        name="coeff_grads",
    )(share, colours, positions)


def exchange(rows, axis, peers):
    sent = rows.reshape(peers, 1, -1)
    got = lax.all_to_all(sent, axis, split_axis=0, concat_axis=0, tiled=True)
    return got.reshape(rows.shape)


def on_device(
    proj,
    sh_coeffs,
    positions,
    camera,
    send_index,
    send_count,
    tile_xy,
    tile_list,
    tile_len,
    pixel_grad,
):
    index = send_index.reshape(CAP, PEERS)
    outgoing = owner(
        camera, proj.reshape(384, 128), sh_coeffs, positions, index, send_count
    )
    received = exchange(outgoing, "cell", PEERS)
    slot_grads = render(
        tile_xy[0], tile_len, received, tile_list[0], pixel_grad.reshape(24, 128)
    )
    returned = exchange(slot_grads, "cell", PEERS)
    grad_rows, colours = scatter(camera, returned, index, send_count)
    colours = exchange(colours, "img", 4)
    share = lax.axis_index("img").astype(jnp.int32).reshape(1)
    grad_sh = coefficients(share, colours, positions)
    return (grad_rows.reshape(proj.shape), grad_sh)


def solution(mesh):
    return jax.shard_map(
        on_device,
        mesh=mesh,
        in_specs=(
            P("img", None, "cell"),
            P(None, "cell"),
            P(None, "cell"),
            P("img", None),
            P("img", "cell"),
            P("img", "cell"),
            P("img", None, "cell"),
            P("img", "cell", None),
            P("img", "cell"),
            P("img", None, "cell"),
        ),
        out_specs=(P("img", None, "cell"), P(None, ("cell", "img"))),
        check_vma=False,
    )
```

```python
import functools

import jax
import jax.numpy as jnp
from jax import lax
from jax.experimental import pallas as pl
from jax.experimental.pallas import tpu as pltpu
from jax.sharding import PartitionSpec as P

SH_ZERO = 0.28209479177387814
SH_ONE = 0.4886025119029199
SH_TWO = (
    1.0925484305920792,
    -1.0925484305920792,
    0.31539156525252005,
    -1.0925484305920792,
    0.5462742152960396,
)
SH_THREE = (
    -0.5900435899266435,
    2.890611442640554,
    -0.4570457994644658,
    0.3731763325901154,
    -0.4570457994644658,
    1.445305721320277,
    -0.5900435899266435,
)

F32 = jnp.float32
BF16 = jnp.bfloat16
PEERS = 128
CAP = 32
COMPS = 9
TILES = 4
DEPTH = 256
LOW = 256
HIGH = 32
PACK = 56
NOTHING = -1.0e4

LINEAR = (
    (SH_ZERO, 0, 0, 0),
    (0, 0, -SH_ONE, 0),
    (0, 0, 0, SH_ONE),
    (0, -SH_ONE, 0, 0),
    (0, SH_TWO[0], 0, 0),
    (0, 0, SH_TWO[1], 0),
    (SH_TWO[2], 0, 0, 0),
    (0, SH_TWO[3], 0, 0),
    (SH_TWO[4], 0, 0, 0),
    (0, 0, SH_THREE[0], 0),
    (0, SH_THREE[1], 0, 0),
    (0, 0, SH_THREE[2], 0),
    (0, 0, 0, SH_THREE[3]),
    (0, SH_THREE[4], 0, 0),
    (0, 0, 0, SH_THREE[5]),
    (0, SH_THREE[6], 0, 0),
)
QUADRATIC = (
    (1, 0, 0, 0, 0, 0, 0),
    (1, 0, 0, 0, 0, 0, 0),
    (1, 0, 0, 0, 0, 0, 0),
    (1, 0, 0, 0, 0, 0, 0),
    (0, 1, 0, 0, 0, 0, 0),
    (0, 0, 1, 0, 0, 0, 0),
    (0, 0, 0, -1, -1, 2, 0),
    (0, 0, 1, 0, 0, 0, 0),
    (0, 0, 0, 1, -1, 0, 0),
    (0, 0, 0, 3, -1, 0, 0),
    (0, 0, 0, 0, 0, 0, 1),
    (0, 0, 0, -1, -1, 4, 0),
    (0, 0, 0, -3, -3, 2, 0),
    (0, 0, 0, -1, -1, 4, 0),
    (0, 0, 0, 1, -1, 0, 0),
    (0, 0, 0, 1, -3, 0, 0),
)


def dot(left, right):
    return lax.dot_general(left, right, (((1,), (0,)), ((), ())), preferred_element_type=F32)


def dot_t(left, right):
    return lax.dot_general(left, right, (((1,), (1,)), ((), ())), preferred_element_type=F32)


def iota(shape, axis):
    return lax.broadcasted_iota(jnp.int32, shape, axis)


def split(value, parts):
    out = []
    for _ in range(parts - 1):
        head = value.astype(BF16).astype(F32)
        out.append(head)
        value = value - head
    out.append(value.astype(BF16).astype(F32))
    return out


def column_consts(table, half):
    rows = iota((8, 128), 0)
    out = []
    for col in range(len(table[0])):
        vals = [float(table[8 * half + i][col]) for i in range(8)]
        if not any(vals):
            out.append(None)
            continue
        acc = jnp.zeros((8, 128), F32)
        for i, val in enumerate(vals):
            if val:
                acc = jnp.where(rows == i, val, acc)
        out.append(acc)
    return out


def form(consts, values):
    total = None
    for const, value in zip(consts, values):
        if const is None:
            continue
        term = const if value is None else const * value
        total = term if total is None else total + term
    return total


def basis_consts():
    return [(column_consts(LINEAR, half), column_consts(QUADRATIC, half)) for half in range(2)]


def basis_halves(consts, xoff, yoff, zoff):
    inv = lax.rsqrt(xoff * xoff + yoff * yoff + zoff * zoff)
    xpos, ypos, zpos = xoff * inv, yoff * inv, zoff * inv
    xsq, ysq, zsq, yz = xpos * xpos, ypos * ypos, zpos * zpos, ypos * zpos
    return [
        form(lin, (None, xpos, ypos, zpos)) * form(quad, (None, ypos, zpos, xsq, ysq, zsq, yz))
        for lin, quad in consts
    ]


def slot_index(idx_ref, cnt_ref, low_scr, high_scr):
    turned = jnp.transpose(idx_ref[...].astype(F32)).astype(jnp.int32)
    slots = jnp.concatenate([turned[32 * i : 32 * i + 32] for i in range(4)], axis=1)
    rows, cols = iota((PEERS, PEERS), 0), iota((PEERS, PEERS), 1)
    perm = (rows == 4 * (cols & 31) + (cols >> 5)).astype(F32).astype(BF16)
    counts = jnp.broadcast_to(cnt_ref[...], (8, PEERS)).astype(F32).astype(BF16)
    counts = dot(counts, perm)[0:1].astype(jnp.int32)
    live = iota((CAP, PEERS), 0) < counts
    low_scr[...] = slots & (LOW - 1)
    high_scr[...] = jnp.where(live, slots >> 8, -1)


def pair_row(ref, base, pair):
    first = ref[pl.ds(base + 2 * pair, 1), :]
    second = ref[pl.ds(base + 2 * pair + 1, 1), :]
    return jnp.concatenate([first, second], axis=1)


def owner_kernel(
    cam_hbm,
    proj_hbm,
    sh_hbm,
    pos_hbm,
    idx_hbm,
    cnt_hbm,
    out_ref,
    cam_ref,
    proj_ref,
    sh_ref,
    pos_ref,
    idx_ref,
    cnt_ref,
    col_scr,
    low_scr,
    high_scr,
    rows_scr,
    sems,
):
    copies = [
        pltpu.make_async_copy(src, dst, sems.at[i])
        for i, (src, dst) in enumerate(
            (
                (idx_hbm, idx_ref),
                (cnt_hbm, cnt_ref),
                (cam_hbm, cam_ref),
                (pos_hbm, pos_ref),
                (sh_hbm, sh_ref),
                (proj_hbm, proj_ref),
            )
        )
    ]
    for copy in copies:
        copy.start()
    consts = basis_consts()
    for copy in copies[:2]:
        copy.wait()
    slot_index(idx_ref, cnt_ref, low_scr, high_scr)
    for copy in copies[2:5]:
        copy.wait()
    cam = [jnp.broadcast_to(cam_ref[0:1, i : i + 1], (8, 128)) for i in range(3)]

    def shade(chunk, carry):
        lanes = pl.ds(pl.multiple_of(chunk * 128, 128), 128)
        offs = [jnp.broadcast_to(pos_ref[i : i + 1, lanes], (8, 128)) - cam[i] for i in range(3)]
        first, second = basis_halves(consts, *offs)
        for chan in range(3):
            terms = sh_ref[16 * chan : 16 * chan + 8, lanes] * first
            terms = terms + sh_ref[16 * chan + 8 : 16 * chan + 16, lanes] * second
            colour = jnp.sum(terms, axis=0, keepdims=True) + 0.5
            col_scr[pl.ds(64 * chan + chunk, 1), :] = colour
        return carry

    lax.fori_loop(0, 64, shade, 0, unroll=16)
    copies[5].wait()

    even = jnp.concatenate(
        [proj_ref[pl.ds(0, 192, stride=2), :], col_scr[pl.ds(0, 96, stride=2), :]], axis=0
    )
    odd = jnp.concatenate(
        [proj_ref[pl.ds(1, 192, stride=2), :], col_scr[pl.ds(1, 96, stride=2), :]], axis=0
    )
    parts = [part.astype(BF16) for part in split(jnp.concatenate([even, odd], axis=1), 3)]
    low_iota = iota((LOW, 256), 0)
    high_iota = iota((HIGH, 256), 0)

    for pair in range(CAP // 2):
        low, high = pair_row(low_scr, 0, pair), pair_row(high_scr, 0, pair)
        hot = jnp.where(low_iota == low, 1.0, 0.0).astype(BF16)
        wide = dot(parts[0], hot) + dot(parts[1], hot) + dot(parts[2], hot)
        mask = high_iota == high
        for comp in range(COMPS):
            row = jnp.sum(
                jnp.where(mask, wide[32 * comp : 32 * comp + 32], 0.0), axis=0, keepdims=True
            )
            rows_scr[32 * comp + 2 * pair : 32 * comp + 2 * pair + 1, :] = row[:, :128]
            rows_scr[32 * comp + 2 * pair + 1 : 32 * comp + 2 * pair + 2, :] = row[:, 128:]

    rows_scr[32 * COMPS :, :] = jnp.zeros((96, 128), F32)
    for k in range(3):
        turned = jnp.transpose(rows_scr[128 * k : 128 * k + 128, :])
        for i in range(4):
            out_ref[pl.ds(3 * i + k, 32, stride=12), :] = turned[32 * i : 32 * i + 32]


def render_kernel(
    xy_ref, len_ref, recv_ref, list_ref, grad_ref, out_ref, table_scr, coef_scr, right_scr, sums_scr
):
    for k in range(3):
        table_scr[128 * k : 128 * k + 128, :] = jnp.transpose(
            recv_ref[pl.ds(k, PEERS, stride=3), :]
        )

    slots = jnp.concatenate(
        [list_ref[t : t + 1, 128 * h : 128 * h + 128] for t in range(TILES) for h in range(2)],
        axis=0,
    )
    peer, place = slots >> 5, slots & (CAP - 1)
    row_iota = iota((8, 128), 0)

    def by_tile(ref, row):
        out = jnp.zeros((8, 128), jnp.int32)
        for t in range(TILES):
            out = jnp.where(
                row_iota >> 1 == t, jnp.broadcast_to(ref[row : row + 1, t : t + 1], (8, 128)), out
            )
        return out

    centre_x = (by_tile(xy_ref, 0).astype(F32) * 16.0 + 8.0) / 128.0
    centre_y = (by_tile(xy_ref, 1).astype(F32) * 16.0 + 8.0) / 128.0
    inside = (row_iota & 1) * 128 + iota((8, 128), 1) < by_tile(len_ref, 0)

    vals = [jnp.zeros((8, 128), F32) for _ in range(COMPS)]
    for q in range(CAP):
        mine = place == q
        for c in range(COMPS):
            row = jnp.broadcast_to(table_scr[32 * c + q : 32 * c + q + 1, :], (8, 128))
            vals[c] = jnp.where(mine, jnp.take_along_axis(row, peer, axis=1), vals[c])

    mean_x, mean_y, ca, cb, cc, opac = vals[:6]
    xrel, yrel = mean_x - centre_x, mean_y - centre_y
    shown = opac > 0.0
    lead_x = ca * xrel + cb * yrel
    lead_y = cc * yrel + cb * xrel
    const = -0.5 * (xrel * lead_x + yrel * lead_y) + jnp.log(jnp.where(shown, opac, 1.0))
    const = jnp.where(shown & inside, const, NOTHING)
    zero = jnp.zeros((8, 128), F32)
    coef = [split(v, 3) for v in (const, lead_x, lead_y, -0.5 * ca, -0.5 * cc, -cb, zero, zero)]
    for part in range(3):
        for i in range(8):
            at = 64 * part + 8 * i
            coef_scr[at : at + 8, :] = coef[i][part]
    coef_scr[192:256, :] = jnp.zeros((64, 128), F32)
    tint = [split(v, 3) for v in vals[6:9]]
    for block, (one, two) in enumerate(((0, 0), (1, 0), (2, 1))):
        for c in range(3):
            right_scr[64 * block + 8 * c : 64 * block + 8 * c + 8, :] = tint[c][one]
            right_scr[64 * block + 24 + 8 * c : 64 * block + 32 + 8 * c, :] = tint[c][two]
        right_scr[64 * block + 48 : 64 * block + 64, :] = jnp.zeros((16, 128), F32)
    right_scr[192:256, :] = jnp.zeros((64, 128), F32)

    blank = jnp.zeros((2, 256), F32)
    blocks, sides = [], []
    for tile in range(TILES):
        grads = jnp.concatenate(
            [
                jnp.concatenate(
                    [grad_ref[8 * c + 2 * tile + h : 8 * c + 2 * tile + h + 1, :] for h in range(2)],
                    axis=1,
                )
                for c in range(3)
            ],
            axis=0,
        )
        g0, g1, g2 = split(grads, 3)
        blocks += [g0, g1, blank, g0, g2, blank, g0, g1, blank, jnp.zeros((8, 256), F32)]
        zero5 = jnp.zeros((5, 256), F32)
        sides.append(jnp.concatenate([g0, zero5, g1, zero5], axis=0).astype(BF16))
    turned = jnp.transpose(jnp.concatenate(blocks, axis=0)).astype(BF16)

    pixel, which = iota((256, 32), 0), iota((256, 32), 1) & 7
    upos = ((pixel & 15).astype(F32) - 7.5) / 128.0
    vpos = ((pixel >> 4).astype(F32) - 7.5) / 128.0
    phi = jnp.where(which == 0, 1.0, 0.0)
    phi = jnp.where(which == 1, upos, phi)
    phi = jnp.where(which == 2, vpos, phi)
    phi = jnp.where(which == 3, upos * upos, phi)
    phi = jnp.where(which == 4, vpos * vpos, phi)
    phi = jnp.where(which == 5, upos * vpos, phi).astype(BF16)
    column = (iota((16, DEPTH), 0).astype(F32) - 7.5) / 128.0
    before = (iota((DEPTH, DEPTH), 0) < iota((DEPTH, DEPTH), 1)).astype(F32).astype(BF16)
    after = (iota((DEPTH, DEPTH), 0) > iota((DEPTH, DEPTH), 1)).astype(F32).astype(BF16)

    def both(ref, tile):
        return jnp.concatenate(
            [ref[pl.ds(2 * tile + h, 32, stride=8), :] for h in range(2)], axis=1
        ).astype(BF16)

    for tile in range(TILES):
        alpha = jnp.exp(dot(phi, both(coef_scr, tile)))
        logs = jnp.log(1.0 - alpha)
        l0 = logs.astype(BF16)
        l1 = (logs - l0.astype(F32)).astype(BF16)
        weight = alpha * jnp.exp(dot(l0, before) + dot(l1, before))
        flow = dot(turned[:, 32 * tile : 32 * tile + 32], both(right_scr, tile)) * weight
        s0 = flow.astype(BF16)
        s1 = (flow - s0.astype(F32)).astype(BF16)
        behind = dot(s0, after) + dot(s1, after)
        power = flow - behind * (alpha * jnp.exp(-logs))
        w0 = weight.astype(BF16)
        w1 = (weight - w0.astype(F32)).astype(BF16)
        colours = dot(sides[tile], w0)
        colours = colours[0:8] + colours[8:16] + dot(sides[tile], w1)[0:8]

        plain = linear = square = None
        for i in range(8):
            vpos = (7.5 - i) / 128.0
            top, bottom = power[16 * i : 16 * i + 16], power[240 - 16 * i : 256 - 16 * i]
            total, slope = top + bottom, (bottom - top) * vpos
            curve = total * (vpos * vpos)
            plain = total if plain is None else plain + total
            linear = slope if linear is None else linear + slope
            square = curve if square is None else square + curve
        sums = [
            plain,
            plain * column,
            linear,
            plain * (column * column),
            square,
            linear * column,
        ]
        rows = [jnp.sum(v, axis=0, keepdims=True) for v in sums]
        rows += [colours[i : i + 1] for i in range(3)]
        for i, row in enumerate(rows):
            for h in range(2):
                sums_scr[8 * i + 2 * tile + h : 8 * i + 2 * tile + h + 1, :] = row[
                    :, 128 * h : 128 * h + 128
                ]

    m0, mu, mv, muu, mvv, muv, red, green, blue = [sums_scr[8 * i : 8 * i + 8, :] for i in range(9)]
    grads = [
        ca * mu + cb * mv - lead_x * m0,
        cc * mv + cb * mu - lead_y * m0,
        -0.5 * (muu - 2.0 * xrel * mu + xrel * xrel * m0),
        -(muv - yrel * mu - xrel * mv + xrel * yrel * m0),
        -0.5 * (mvv - 2.0 * yrel * mv + yrel * yrel * m0),
        jnp.where(shown, m0 / jnp.where(shown, opac, 1.0), 0.0),
        red,
        green,
        blue,
    ]
    grads = [split(grad, 2) for grad in grads]
    peer_iota, place_iota = iota((PEERS, 128), 0), iota((CAP, 128), 0)
    hots, wides = [], []
    for r in range(8):
        hots.append(jnp.where(peer_iota == peer[r : r + 1], 1.0, 0.0).astype(BF16))
        mine = place_iota == place[r : r + 1]
        wides.append(
            jnp.concatenate(
                [
                    jnp.where(mine, grads[c][part][r : r + 1], 0.0)
                    for part in range(2)
                    for c in range(COMPS)
                ],
                axis=0,
            ).astype(BF16)
        )
    total = dot_t(jnp.concatenate(wides, axis=1), jnp.concatenate(hots, axis=1))
    total = total[: 32 * COMPS] + total[32 * COMPS :]
    total = jnp.concatenate([total, jnp.zeros((96, 128), F32)], axis=0)
    for k in range(3):
        out_ref[pl.ds(k, PEERS, stride=3), :] = jnp.transpose(total[128 * k : 128 * k + 128])


def sum_slots(comps, back_ref, idx_ref, cnt_ref, low_scr, high_scr, rows_scr):
    slot_index(idx_ref, cnt_ref, low_scr, high_scr)
    for k in sorted({comp // 4 for comp in comps}):
        block = jnp.concatenate(
            [back_ref[pl.ds(3 * i + k, 32, stride=12), :] for i in range(4)], axis=0
        )
        rows_scr[128 * k : 128 * k + 128, :] = jnp.transpose(block)
    low_iota = iota((LOW, 256), 0)
    high_iota = iota((HIGH, 256), 0)
    hots, wides = [], []
    for pair in range(CAP // 2):
        low, high = pair_row(low_scr, 0, pair), pair_row(high_scr, 0, pair)
        hots.append(jnp.where(low_iota == low, 1.0, 0.0).astype(BF16))
        mask = high_iota == high
        both = [split(pair_row(rows_scr, 32 * comp, pair), 2) for comp in comps]
        wides.append(
            jnp.concatenate(
                [jnp.where(mask, b[part], 0.0) for part in range(2) for b in both], axis=0
            ).astype(BF16)
        )
    total = None
    for i in range(0, CAP // 2, 4):
        term = dot_t(
            jnp.concatenate(wides[i : i + 4], axis=1), jnp.concatenate(hots[i : i + 4], axis=1)
        )
        total = term if total is None else total + term
    size = 32 * len(comps)
    return total[:size] + total[size:]


def colour_sum_kernel(cam_ref, back_ref, idx_ref, cnt_ref, col_ref, low_scr, high_scr, rows_scr):
    total = sum_slots((6, 7, 8), back_ref, idx_ref, cnt_ref, low_scr, high_scr, rows_scr)
    for par in range(2):
        for share in range(4):
            for chan in range(3):
                first = 32 * chan + 8 * share
                col_ref[pl.ds(PACK * share + 16 * chan + par, 8, stride=2), :] = total[
                    first : first + 8, 128 * par : 128 * par + 128
                ]
    lanes = iota((8, 128), 1)
    row = jnp.zeros((8, 128), F32)
    for i in range(3):
        row = jnp.where(lanes == i, jnp.broadcast_to(cam_ref[0:1, i : i + 1], (8, 128)), row)
    for share in range(4):
        col_ref[PACK * share + 48 : PACK * share + 56, :] = row


def row_sum_kernel(back_ref, idx_ref, cnt_ref, out_ref, low_scr, high_scr, rows_scr):
    total = sum_slots(range(6), back_ref, idx_ref, cnt_ref, low_scr, high_scr, rows_scr)
    for par in range(2):
        out_ref[pl.ds(par, 192, stride=2), :] = total[:, 128 * par : 128 * par + 128]


def coeff_kernel(share_ref, col_ref, pos_ref, out_ref):
    consts = basis_consts()
    share = share_ref[0]
    cams = []
    for image in range(4):
        row = col_ref[PACK * image + 48 : PACK * image + 56, :]
        cams.append([jnp.broadcast_to(row[:, i : i + 1], (8, 128)) for i in range(3)])

    def chunk(step, carry):
        lanes = pl.ds(pl.multiple_of(share * 2048 + step * 128, 128), 128)
        place = [jnp.broadcast_to(pos_ref[i : i + 1, lanes], (8, 128)) for i in range(3)]
        totals = [[None, None] for _ in range(3)]
        for image in range(4):
            cam = cams[image]
            halves = basis_halves(
                consts, place[0] - cam[0], place[1] - cam[1], place[2] - cam[2]
            )
            for chan in range(3):
                grad = jnp.broadcast_to(
                    col_ref[pl.ds(PACK * image + 16 * chan + step, 1), :], (8, 128)
                )
                for half in range(2):
                    term = grad * halves[half]
                    old = totals[chan][half]
                    totals[chan][half] = term if old is None else old + term
        here = pl.ds(pl.multiple_of(step * 128, 128), 128)
        for chan in range(3):
            for half in range(2):
                out_ref[16 * chan + 8 * half : 16 * chan + 8 * half + 8, here] = totals[chan][half]
        return carry

    lax.fori_loop(0, 16, chunk, 0, unroll=2)


VMEM = pl.BlockSpec(memory_space=pltpu.VMEM)
SMEM = pl.BlockSpec(memory_space=pltpu.SMEM)
HBM = pl.BlockSpec(memory_space=pltpu.HBM)
PARAMS = pltpu.CompilerParams(vmem_limit_bytes=40 * 1024 * 1024)


def shape(*dims):
    return jax.ShapeDtypeStruct(dims, F32)


def in_hbm(array):
    return pltpu.with_memory_space_constraint(array, pltpu.HBM)


def owner(camera, proj, coeffs, positions, index, count):
    return pl.pallas_call(
        owner_kernel,
        out_shape=shape(384, 128),
        in_specs=[HBM] * 6,
        out_specs=VMEM,
        scratch_shapes=[
            pltpu.VMEM((1, 3), F32),
            pltpu.VMEM((384, 128), F32),
            pltpu.VMEM((48, 8192), F32),
            pltpu.VMEM((3, 8192), F32),
            pltpu.VMEM((CAP, PEERS), jnp.int32),
            pltpu.VMEM((1, PEERS), jnp.int32),
            pltpu.VMEM((192, 128), F32),
            pltpu.VMEM((CAP, PEERS), jnp.int32),
            pltpu.VMEM((CAP, PEERS), jnp.int32),
            pltpu.VMEM((384, 128), F32),
            pltpu.SemaphoreType.DMA((6,)),
        ],
        compiler_params=PARAMS,
        name="owner_rows",
    )(*[in_hbm(x) for x in (camera, proj, coeffs, positions, index, count)])


def render(tile_xy, tile_len, received, tile_list, pixel_grad):
    return pl.pallas_call(
        render_kernel,
        out_shape=shape(384, 128),
        in_specs=[VMEM] * 5,
        out_specs=VMEM,
        scratch_shapes=[
            pltpu.VMEM((384, 128), F32),
            pltpu.VMEM((256, 128), F32),
            pltpu.VMEM((256, 128), F32),
            pltpu.VMEM((72, 128), F32),
        ],
        compiler_params=PARAMS,
        name="render_tiles",
    )(tile_xy, tile_len, received, tile_list, pixel_grad)


SLOT_SCRATCH = (
    pltpu.VMEM((CAP, PEERS), jnp.int32),
    pltpu.VMEM((CAP, PEERS), jnp.int32),
    pltpu.VMEM((384, 128), F32),
)


def sum_colours(camera, returned, index, count):
    return pl.pallas_call(
        colour_sum_kernel,
        out_shape=shape(4 * PACK, 128),
        in_specs=[VMEM] * 4,
        out_specs=VMEM,
        scratch_shapes=SLOT_SCRATCH,
        compiler_params=PARAMS,
        name="colour_sums",
    )(camera, returned, index, count)


def sum_rows(returned, index, count):
    return pl.pallas_call(
        row_sum_kernel,
        out_shape=shape(384, 128),
        in_specs=[VMEM] * 3,
        out_specs=VMEM,
        scratch_shapes=SLOT_SCRATCH,
        compiler_params=PARAMS,
        cost_estimate=pl.CostEstimate(
            flops=2 * 384 * 256 * 4096, bytes_accessed=400_000, transcendentals=0
        ),
        name="row_sums",
    )(returned, index, count)


def coefficients(share, colours, positions):
    return pl.pallas_call(
        coeff_kernel,
        out_shape=shape(48, 2048),
        in_specs=[SMEM] + [VMEM] * 2,
        out_specs=VMEM,
        compiler_params=PARAMS,
        name="coeff_grads",
    )(share, colours, positions)


def exchange(rows, axis, peers):
    sent = rows.reshape(peers, 1, -1)
    got = lax.all_to_all(sent, axis, split_axis=0, concat_axis=0, tiled=True)
    return got.reshape(rows.shape)


def on_device(
    proj,
    sh_coeffs,
    positions,
    camera,
    send_index,
    send_count,
    tile_xy,
    tile_list,
    tile_len,
    pixel_grad,
):
    index = send_index.reshape(CAP, PEERS)
    outgoing = owner(
        camera, proj.reshape(384, 128), sh_coeffs, positions, index, send_count
    )
    received = exchange(outgoing, "cell", PEERS)
    slot_grads = render(
        tile_xy[0], tile_len, received, tile_list[0], pixel_grad.reshape(24, 128)
    )
    returned = exchange(slot_grads, "cell", PEERS)
    colours = exchange(sum_colours(camera, returned, index, send_count), "img", 4)
    grad_rows = sum_rows(returned, index, send_count)
    share = lax.axis_index("img").astype(jnp.int32).reshape(1)
    grad_sh = coefficients(share, colours, positions)
    return (grad_rows.reshape(proj.shape), grad_sh)


def solution(mesh):
    return jax.shard_map(
        on_device,
        mesh=mesh,
        in_specs=(
            P("img", None, "cell"),
            P(None, "cell"),
            P(None, "cell"),
            P("img", None),
            P("img", "cell"),
            P("img", "cell"),
            P("img", None, "cell"),
            P("img", "cell", None),
            P("img", "cell"),
            P("img", None, "cell"),
        ),
        out_specs=(P("img", None, "cell"), P(None, ("cell", "img"))),
        check_vma=False,
    )
```

```python
import functools

import jax
import jax.numpy as jnp
from jax import lax
from jax.experimental import pallas as pl
from jax.experimental.pallas import tpu as pltpu
from jax.sharding import PartitionSpec as P

SH_ZERO = 0.28209479177387814
SH_ONE = 0.4886025119029199
SH_TWO = (
    1.0925484305920792,
    -1.0925484305920792,
    0.31539156525252005,
    -1.0925484305920792,
    0.5462742152960396,
)
SH_THREE = (
    -0.5900435899266435,
    2.890611442640554,
    -0.4570457994644658,
    0.3731763325901154,
    -0.4570457994644658,
    1.445305721320277,
    -0.5900435899266435,
)

F32 = jnp.float32
BF16 = jnp.bfloat16
PEERS = 128
CAP = 32
COMPS = 9
TILES = 4
DEPTH = 256
LOW = 256
HIGH = 32
PACK = 56
NOTHING = -1.0e4
EARLY = 6
ALONE = 3

LINEAR = (
    (SH_ZERO, 0, 0, 0),
    (0, 0, -SH_ONE, 0),
    (0, 0, 0, SH_ONE),
    (0, -SH_ONE, 0, 0),
    (0, SH_TWO[0], 0, 0),
    (0, 0, SH_TWO[1], 0),
    (SH_TWO[2], 0, 0, 0),
    (0, SH_TWO[3], 0, 0),
    (SH_TWO[4], 0, 0, 0),
    (0, 0, SH_THREE[0], 0),
    (0, SH_THREE[1], 0, 0),
    (0, 0, SH_THREE[2], 0),
    (0, 0, 0, SH_THREE[3]),
    (0, SH_THREE[4], 0, 0),
    (0, 0, 0, SH_THREE[5]),
    (0, SH_THREE[6], 0, 0),
)
QUADRATIC = (
    (1, 0, 0, 0, 0, 0, 0),
    (1, 0, 0, 0, 0, 0, 0),
    (1, 0, 0, 0, 0, 0, 0),
    (1, 0, 0, 0, 0, 0, 0),
    (0, 1, 0, 0, 0, 0, 0),
    (0, 0, 1, 0, 0, 0, 0),
    (0, 0, 0, -1, -1, 2, 0),
    (0, 0, 1, 0, 0, 0, 0),
    (0, 0, 0, 1, -1, 0, 0),
    (0, 0, 0, 3, -1, 0, 0),
    (0, 0, 0, 0, 0, 0, 1),
    (0, 0, 0, -1, -1, 4, 0),
    (0, 0, 0, -3, -3, 2, 0),
    (0, 0, 0, -1, -1, 4, 0),
    (0, 0, 0, 1, -1, 0, 0),
    (0, 0, 0, 1, -3, 0, 0),
)


def dot(left, right):
    return lax.dot_general(left, right, (((1,), (0,)), ((), ())), preferred_element_type=F32)


def dot_t(left, right):
    return lax.dot_general(left, right, (((1,), (1,)), ((), ())), preferred_element_type=F32)


def one_hot(rows, index):
    same = rows.astype(jnp.int16) == index.astype(jnp.int16)
    return jnp.where(same, jnp.ones((), BF16), jnp.zeros((), BF16))


def stacked(first, second, right):
    both = dot(jnp.concatenate([first, second], axis=0), right)
    return both[: first.shape[0]] + both[first.shape[0] :]


def iota(shape, axis):
    return lax.broadcasted_iota(jnp.int32, shape, axis)


def split(value, parts):
    out = []
    for _ in range(parts - 1):
        head = value.astype(BF16).astype(F32)
        out.append(head)
        value = value - head
    out.append(value.astype(BF16).astype(F32))
    return out


def column_consts(table, half):
    rows = iota((8, 128), 0)
    out = []
    for col in range(len(table[0])):
        vals = [float(table[8 * half + i][col]) for i in range(8)]
        if not any(vals):
            out.append(None)
            continue
        acc = jnp.zeros((8, 128), F32)
        for i, val in enumerate(vals):
            if val:
                acc = jnp.where(rows == i, val, acc)
        out.append(acc)
    return out


def form(consts, values):
    total = None
    for const, value in zip(consts, values):
        if const is None:
            continue
        term = const if value is None else const * value
        total = term if total is None else total + term
    return total


def basis_consts():
    return [(column_consts(LINEAR, half), column_consts(QUADRATIC, half)) for half in range(2)]


def basis_halves(consts, xoff, yoff, zoff):
    inv = lax.rsqrt(xoff * xoff + yoff * yoff + zoff * zoff)
    xpos, ypos, zpos = xoff * inv, yoff * inv, zoff * inv
    xsq, ysq, zsq, yz = xpos * xpos, ypos * ypos, zpos * zpos, ypos * zpos
    return [
        form(lin, (None, xpos, ypos, zpos)) * form(quad, (None, ypos, zpos, xsq, ysq, zsq, yz))
        for lin, quad in consts
    ]


def slot_index(idx_ref, cnt_ref, low_scr, high_scr):
    turned = jnp.transpose(idx_ref[...].astype(F32)).astype(jnp.int32)
    slots = jnp.concatenate([turned[32 * i : 32 * i + 32] for i in range(4)], axis=1)
    rows, cols = iota((PEERS, PEERS), 0), iota((PEERS, PEERS), 1)
    perm = (rows == 4 * (cols & 31) + (cols >> 5)).astype(F32).astype(BF16)
    counts = jnp.broadcast_to(cnt_ref[...], (8, PEERS)).astype(F32).astype(BF16)
    counts = dot(counts, perm)[0:1].astype(jnp.int32)
    live = iota((CAP, PEERS), 0) < counts
    low_scr[...] = slots & (LOW - 1)
    high_scr[...] = jnp.where(live, slots >> 8, -1)


def pair_row(ref, base, pair):
    first = ref[pl.ds(base + 2 * pair, 1), :]
    second = ref[pl.ds(base + 2 * pair + 1, 1), :]
    return jnp.concatenate([first, second], axis=1)


def owner_kernel(
    cam_hbm,
    proj_hbm,
    sh_hbm,
    pos_hbm,
    idx_hbm,
    cnt_hbm,
    out_ref,
    high_scr,
    hot_ref,
    cam_ref,
    proj_ref,
    sh_ref,
    pos_ref,
    idx_ref,
    cnt_ref,
    col_scr,
    low_scr,
    rows_scr,
    sems,
):
    copies = [
        pltpu.make_async_copy(src, dst, sems.at[i])
        for i, (src, dst) in enumerate(
            (
                (idx_hbm, idx_ref),
                (cnt_hbm, cnt_ref),
                (proj_hbm, proj_ref),
                (cam_hbm, cam_ref),
                (pos_hbm, pos_ref),
                (sh_hbm, sh_ref),
            )
        )
    ]
    for copy in copies:
        copy.start()
    consts = basis_consts()
    for copy in copies[:2]:
        copy.wait()
    slot_index(idx_ref, cnt_ref, low_scr, high_scr)
    low_iota = iota((LOW, 256), 0)
    high_iota = iota((HIGH, 256), 0)

    def table(ref, comps):
        return jnp.concatenate(
            [ref[pl.ds(par, 32 * comps, stride=2), :] for par in range(2)], axis=1
        )

    def pick(wide, mask, base, comps, pair):
        for comp in range(comps):
            row = jnp.sum(
                jnp.where(mask, wide[32 * comp : 32 * comp + 32], 0.0), axis=0, keepdims=True
            )
            at = 32 * (base + comp) + 2 * pair
            rows_scr[at : at + 1, :] = row[:, :128]
            rows_scr[at + 1 : at + 2, :] = row[:, 128:]

    def shade(chunk):
        lanes = slice(128 * chunk, 128 * chunk + 128)
        offs = [jnp.broadcast_to(pos_ref[i : i + 1, lanes], (8, 128)) - cam[i] for i in range(3)]
        first, second = basis_halves(consts, *offs)
        for chan in range(3):
            terms = sh_ref[16 * chan : 16 * chan + 8, lanes] * first
            terms = terms + sh_ref[16 * chan + 8 : 16 * chan + 16, lanes] * second
            colour = jnp.sum(terms, axis=0, keepdims=True) + 0.5
            at = 64 * chan + chunk
            col_scr[at : at + 1, :] = colour

    def hots(pair):
        hot = one_hot(low_iota, pair_row(low_scr, 0, pair))
        hot_ref[:, 256 * pair : 256 * pair + 256] = hot
        return hot

    def mask(pair):
        return high_iota == pair_row(high_scr, 0, pair)

    copies[2].wait()
    rows = split(table(proj_ref, 6), 3)
    rows = jnp.concatenate([rows[0], rows[1], rows[2][:160]], axis=0).astype(BF16)

    def sum_rows(wide):
        exact = wide[:160] + wide[192:352] + wide[384:544]
        return jnp.concatenate([exact, wide[160:192] + wide[352:384]], axis=0)

    cam, chunk = None, 0
    for pair in range(EARLY):
        hot = hots(pair)
        pick(sum_rows(dot(rows, hot)), mask(pair), 0, 6, pair)
        if pair == ALONE - 1:
            for copy in copies[3:]:
                copy.wait()
            cam = [jnp.broadcast_to(cam_ref[0:1, i : i + 1], (8, 128)) for i in range(3)]
        if pair >= ALONE:
            for _ in range(-(-64 // (EARLY - ALONE))):
                if chunk < 64:
                    shade(chunk)
                    chunk += 1
    tints = jnp.concatenate(split(table(col_scr, 3), 2), axis=0).astype(BF16)
    everything = jnp.concatenate([rows, tints], axis=0)
    for pair in range(EARLY, CAP // 2):
        wide = dot(everything, hots(pair))
        pick(sum_rows(wide), mask(pair), 0, 6, pair)
        pick(wide[544:640] + wide[640:736], mask(pair), 6, 3, pair)
    for pair in range(EARLY):
        wide = dot(tints, hot_ref[:, 256 * pair : 256 * pair + 256])
        pick(wide[:96] + wide[96:], mask(pair), 6, 3, pair)

    rows_scr[32 * COMPS :, :] = jnp.zeros((96, 128), F32)
    for k in range(3):
        turned = jnp.transpose(rows_scr[128 * k : 128 * k + 128, :])
        for i in range(4):
            out_ref[pl.ds(3 * i + k, 32, stride=12), :] = turned[32 * i : 32 * i + 32]


def render_kernel(
    xy_ref, len_ref, recv_ref, list_ref, grad_ref, out_ref, table_scr, coef_scr, right_scr, sums_scr
):
    for k in range(3):
        table_scr[128 * k : 128 * k + 128, :] = jnp.transpose(
            recv_ref[pl.ds(k, PEERS, stride=3), :]
        )

    slots = jnp.concatenate(
        [list_ref[t : t + 1, 128 * h : 128 * h + 128] for t in range(TILES) for h in range(2)],
        axis=0,
    )
    peer, place = slots >> 5, slots & (CAP - 1)
    row_iota = iota((8, 128), 0)

    def by_tile(ref, row):
        out = jnp.zeros((8, 128), jnp.int32)
        for t in range(TILES):
            out = jnp.where(
                row_iota >> 1 == t, jnp.broadcast_to(ref[row : row + 1, t : t + 1], (8, 128)), out
            )
        return out

    centre_x = (by_tile(xy_ref, 0).astype(F32) * 16.0 + 8.0) / 128.0
    centre_y = (by_tile(xy_ref, 1).astype(F32) * 16.0 + 8.0) / 128.0
    inside = (row_iota & 1) * 128 + iota((8, 128), 1) < by_tile(len_ref, 0)

    vals = [jnp.zeros((8, 128), F32) for _ in range(COMPS)]
    for q in range(CAP):
        mine = place == q
        for c in range(COMPS):
            row = jnp.broadcast_to(table_scr[32 * c + q : 32 * c + q + 1, :], (8, 128))
            vals[c] = jnp.where(mine, jnp.take_along_axis(row, peer, axis=1), vals[c])

    mean_x, mean_y, ca, cb, cc, opac = vals[:6]
    xrel, yrel = mean_x - centre_x, mean_y - centre_y
    shown = opac > 0.0
    lead_x = ca * xrel + cb * yrel
    lead_y = cc * yrel + cb * xrel
    const = -0.5 * (xrel * lead_x + yrel * lead_y) + jnp.log(jnp.where(shown, opac, 1.0))
    const = jnp.where(shown & inside, const, NOTHING)
    zero = jnp.zeros((8, 128), F32)
    coef = [split(v, 3) for v in (const, lead_x, lead_y, -0.5 * ca, -0.5 * cc, -cb, zero, zero)]
    for part in range(3):
        for i in range(8):
            at = 64 * part + 8 * i
            coef_scr[at : at + 8, :] = coef[i][part]
    coef_scr[192:256, :] = jnp.zeros((64, 128), F32)
    tint = [split(v, 3) for v in vals[6:9]]
    for block, (one, two) in enumerate(((0, 0), (1, 0), (2, 1))):
        for c in range(3):
            right_scr[64 * block + 8 * c : 64 * block + 8 * c + 8, :] = tint[c][one]
            right_scr[64 * block + 24 + 8 * c : 64 * block + 32 + 8 * c, :] = tint[c][two]
        right_scr[64 * block + 48 : 64 * block + 64, :] = jnp.zeros((16, 128), F32)
    right_scr[192:256, :] = jnp.zeros((64, 128), F32)

    blank = jnp.zeros((2, 256), F32)
    blocks, sides = [], []
    for tile in range(TILES):
        grads = jnp.concatenate(
            [
                jnp.concatenate(
                    [grad_ref[8 * c + 2 * tile + h : 8 * c + 2 * tile + h + 1, :] for h in range(2)],
                    axis=1,
                )
                for c in range(3)
            ],
            axis=0,
        )
        g0, g1, g2 = split(grads, 3)
        blocks += [g0, g1, blank, g0, g2, blank, g0, g1, blank, jnp.zeros((8, 256), F32)]
        zero5 = jnp.zeros((5, 256), F32)
        sides.append(jnp.concatenate([g0, zero5, g1, zero5], axis=0).astype(BF16))
    turned = jnp.transpose(jnp.concatenate(blocks, axis=0)).astype(BF16)

    pixel, which = iota((256, 32), 0), iota((256, 32), 1) & 7
    upos = ((pixel & 15).astype(F32) - 7.5) / 128.0
    vpos = ((pixel >> 4).astype(F32) - 7.5) / 128.0
    phi = jnp.where(which == 0, 1.0, 0.0)
    phi = jnp.where(which == 1, upos, phi)
    phi = jnp.where(which == 2, vpos, phi)
    phi = jnp.where(which == 3, upos * upos, phi)
    phi = jnp.where(which == 4, vpos * vpos, phi)
    phi = jnp.where(which == 5, upos * vpos, phi).astype(BF16)
    column = (iota((16, DEPTH), 0).astype(F32) - 7.5) / 128.0
    before = (iota((DEPTH, DEPTH), 0) < iota((DEPTH, DEPTH), 1)).astype(F32).astype(BF16)
    after = (iota((DEPTH, DEPTH), 0) > iota((DEPTH, DEPTH), 1)).astype(F32).astype(BF16)

    def both(ref, tile):
        return jnp.concatenate(
            [ref[pl.ds(2 * tile + h, 32, stride=8), :] for h in range(2)], axis=1
        ).astype(BF16)

    for tile in range(TILES):
        alpha = jnp.exp(dot(phi, both(coef_scr, tile)))
        logs = jnp.log(1.0 - alpha)
        l0 = logs.astype(BF16)
        l1 = (logs - l0.astype(F32)).astype(BF16)
        weight = alpha * jnp.exp(stacked(l0, l1, before))
        flow = dot(turned[:, 32 * tile : 32 * tile + 32], both(right_scr, tile)) * weight
        s0 = flow.astype(BF16)
        s1 = (flow - s0.astype(F32)).astype(BF16)
        behind = stacked(s0, s1, after)
        power = flow - behind * (alpha * jnp.exp(-logs))
        w0 = weight.astype(BF16)
        w1 = (weight - w0.astype(F32)).astype(BF16)
        colours = dot(sides[tile], w0)
        colours = colours[0:8] + colours[8:16] + dot(sides[tile], w1)[0:8]

        plain = linear = square = None
        for i in range(8):
            vpos = (7.5 - i) / 128.0
            top, bottom = power[16 * i : 16 * i + 16], power[240 - 16 * i : 256 - 16 * i]
            total, slope = top + bottom, (bottom - top) * vpos
            curve = total * (vpos * vpos)
            plain = total if plain is None else plain + total
            linear = slope if linear is None else linear + slope
            square = curve if square is None else square + curve
        sums = [
            plain,
            plain * column,
            linear,
            plain * (column * column),
            square,
            linear * column,
        ]
        rows = [jnp.sum(v, axis=0, keepdims=True) for v in sums]
        rows += [colours[i : i + 1] for i in range(3)]
        for i, row in enumerate(rows):
            for h in range(2):
                sums_scr[8 * i + 2 * tile + h : 8 * i + 2 * tile + h + 1, :] = row[
                    :, 128 * h : 128 * h + 128
                ]

    m0, mu, mv, muu, mvv, muv, red, green, blue = [sums_scr[8 * i : 8 * i + 8, :] for i in range(9)]
    grads = [
        ca * mu + cb * mv - lead_x * m0,
        cc * mv + cb * mu - lead_y * m0,
        -0.5 * (muu - 2.0 * xrel * mu + xrel * xrel * m0),
        -(muv - yrel * mu - xrel * mv + xrel * yrel * m0),
        -0.5 * (mvv - 2.0 * yrel * mv + yrel * yrel * m0),
        jnp.where(shown, m0 / jnp.where(shown, opac, 1.0), 0.0),
        red,
        green,
        blue,
    ]
    grads = [split(grad, 2) for grad in grads]
    peer_iota, place_iota = iota((PEERS, 128), 0), iota((CAP, 128), 0)
    hots, wides = [], []
    for r in range(8):
        hots.append(jnp.where(peer_iota == peer[r : r + 1], 1.0, 0.0).astype(BF16))
        mine = place_iota == place[r : r + 1]
        wides.append(
            jnp.concatenate(
                [
                    jnp.where(mine, grads[c][part][r : r + 1], 0.0)
                    for part in range(2)
                    for c in range(COMPS)
                ],
                axis=0,
            ).astype(BF16)
        )
    total = dot_t(jnp.concatenate(wides, axis=1), jnp.concatenate(hots, axis=1))
    total = total[: 32 * COMPS] + total[32 * COMPS :]
    total = jnp.concatenate([total, jnp.zeros((96, 128), F32)], axis=0)
    for k in range(3):
        out_ref[pl.ds(k, PEERS, stride=3), :] = jnp.transpose(total[128 * k : 128 * k + 128])


def sum_slots(comps, back_ref, high_ref, hot_ref, rows_scr):
    for k in sorted({comp // 4 for comp in comps}):
        block = jnp.concatenate(
            [back_ref[pl.ds(3 * i + k, 32, stride=12), :] for i in range(4)], axis=0
        )
        rows_scr[128 * k : 128 * k + 128, :] = jnp.transpose(block)
    high_iota = iota((HIGH, 256), 0)
    total = None
    for step in range(4):
        wides = []
        for pair in range(4 * step, 4 * step + 4):
            mask = high_iota == pair_row(high_ref, 0, pair)
            both = [split(pair_row(rows_scr, 32 * comp, pair), 2) for comp in comps]
            wides.append(
                jnp.concatenate(
                    [jnp.where(mask, b[part], 0.0) for part in range(2) for b in both], axis=0
                ).astype(BF16)
            )
        term = dot_t(
            jnp.concatenate(wides, axis=1), hot_ref[:, 1024 * step : 1024 * step + 1024]
        )
        total = term if total is None else total + term
    size = 32 * len(comps)
    return total[:size] + total[size:]


def colour_sum_kernel(cam_ref, back_ref, high_ref, hot_ref, col_ref, rows_scr):
    total = sum_slots((6, 7, 8), back_ref, high_ref, hot_ref, rows_scr)
    for par in range(2):
        for share in range(4):
            for chan in range(3):
                first = 32 * chan + 8 * share
                col_ref[pl.ds(PACK * share + 16 * chan + par, 8, stride=2), :] = total[
                    first : first + 8, 128 * par : 128 * par + 128
                ]
    lanes = iota((8, 128), 1)
    row = jnp.zeros((8, 128), F32)
    for i in range(3):
        row = jnp.where(lanes == i, jnp.broadcast_to(cam_ref[0:1, i : i + 1], (8, 128)), row)
    for share in range(4):
        col_ref[PACK * share + 48 : PACK * share + 56, :] = row


def row_sum_kernel(back_ref, high_ref, hot_ref, out_ref, rows_scr):
    total = sum_slots(range(6), back_ref, high_ref, hot_ref, rows_scr)
    for par in range(2):
        out_ref[pl.ds(par, 192, stride=2), :] = total[:, 128 * par : 128 * par + 128]


def coeff_kernel(share_ref, col_ref, pos_ref, out_ref):
    consts = basis_consts()
    share = share_ref[0]
    cams = []
    for image in range(4):
        row = col_ref[PACK * image + 48 : PACK * image + 56, :]
        cams.append([jnp.broadcast_to(row[:, i : i + 1], (8, 128)) for i in range(3)])

    def chunk(step, carry):
        lanes = pl.ds(pl.multiple_of(share * 2048 + step * 128, 128), 128)
        place = [jnp.broadcast_to(pos_ref[i : i + 1, lanes], (8, 128)) for i in range(3)]
        totals = [[None, None] for _ in range(3)]
        for image in range(4):
            cam = cams[image]
            halves = basis_halves(
                consts, place[0] - cam[0], place[1] - cam[1], place[2] - cam[2]
            )
            for chan in range(3):
                grad = jnp.broadcast_to(
                    col_ref[pl.ds(PACK * image + 16 * chan + step, 1), :], (8, 128)
                )
                for half in range(2):
                    term = grad * halves[half]
                    old = totals[chan][half]
                    totals[chan][half] = term if old is None else old + term
        here = pl.ds(pl.multiple_of(step * 128, 128), 128)
        for chan in range(3):
            for half in range(2):
                out_ref[16 * chan + 8 * half : 16 * chan + 8 * half + 8, here] = totals[chan][half]
        return carry

    lax.fori_loop(0, 16, chunk, 0, unroll=16)


VMEM = pl.BlockSpec(memory_space=pltpu.VMEM)
SMEM = pl.BlockSpec(memory_space=pltpu.SMEM)
HBM = pl.BlockSpec(memory_space=pltpu.HBM)
PARAMS = pltpu.CompilerParams(vmem_limit_bytes=40 * 1024 * 1024)


def shape(*dims):
    return jax.ShapeDtypeStruct(dims, F32)


def in_hbm(array):
    return pltpu.with_memory_space_constraint(array, pltpu.HBM)


def owner(camera, proj, coeffs, positions, index, count):
    return pl.pallas_call(
        owner_kernel,
        out_shape=(
            shape(384, 128),
            jax.ShapeDtypeStruct((CAP, PEERS), jnp.int32),
            jax.ShapeDtypeStruct((LOW, CAP * PEERS), BF16),
        ),
        in_specs=[HBM] * 6,
        out_specs=[VMEM] * 3,
        scratch_shapes=[
            pltpu.VMEM((1, 3), F32),
            pltpu.VMEM((384, 128), F32),
            pltpu.VMEM((48, 8192), F32),
            pltpu.VMEM((3, 8192), F32),
            pltpu.VMEM((CAP, PEERS), jnp.int32),
            pltpu.VMEM((1, PEERS), jnp.int32),
            pltpu.VMEM((192, 128), F32),
            pltpu.VMEM((CAP, PEERS), jnp.int32),
            pltpu.VMEM((384, 128), F32),
            pltpu.SemaphoreType.DMA((6,)),
        ],
        compiler_params=PARAMS,
        name="owner_rows",
    )(*[in_hbm(x) for x in (camera, proj, coeffs, positions, index, count)])


def render(tile_xy, tile_len, received, tile_list, pixel_grad):
    return pl.pallas_call(
        render_kernel,
        out_shape=shape(384, 128),
        in_specs=[VMEM] * 5,
        out_specs=VMEM,
        scratch_shapes=[
            pltpu.VMEM((384, 128), F32),
            pltpu.VMEM((256, 128), F32),
            pltpu.VMEM((256, 128), F32),
            pltpu.VMEM((72, 128), F32),
        ],
        compiler_params=PARAMS,
        name="render_tiles",
    )(tile_xy, tile_len, received, tile_list, pixel_grad)


def sum_colours(camera, returned, high, low_hot):
    return pl.pallas_call(
        colour_sum_kernel,
        out_shape=shape(4 * PACK, 128),
        in_specs=[VMEM] * 4,
        out_specs=VMEM,
        scratch_shapes=[pltpu.VMEM((384, 128), F32)],
        compiler_params=PARAMS,
        name="colour_sums",
    )(camera, returned, high, low_hot)


def sum_rows(returned, high, low_hot):
    return pl.pallas_call(
        row_sum_kernel,
        out_shape=shape(384, 128),
        in_specs=[VMEM] * 3,
        out_specs=VMEM,
        scratch_shapes=[pltpu.VMEM((384, 128), F32)],
        compiler_params=PARAMS,
        cost_estimate=pl.CostEstimate(
            flops=2 * 384 * 256 * 4096, bytes_accessed=400_000, transcendentals=0
        ),
        name="row_sums",
    )(returned, high, low_hot)


def coefficients(share, colours, positions):
    return pl.pallas_call(
        coeff_kernel,
        out_shape=shape(48, 2048),
        in_specs=[SMEM] + [VMEM] * 2,
        out_specs=VMEM,
        compiler_params=PARAMS,
        name="coeff_grads",
    )(share, colours, positions)


def exchange(rows, axis, peers):
    sent = rows.reshape(peers, 1, -1)
    got = lax.all_to_all(sent, axis, split_axis=0, concat_axis=0, tiled=True)
    return got.reshape(rows.shape)


def on_device(
    proj,
    sh_coeffs,
    positions,
    camera,
    send_index,
    send_count,
    tile_xy,
    tile_list,
    tile_len,
    pixel_grad,
):
    index = send_index.reshape(CAP, PEERS)
    outgoing, high, low_hot = owner(
        camera, proj.reshape(384, 128), sh_coeffs, positions, index, send_count
    )
    received = exchange(outgoing, "cell", PEERS)
    slot_grads = render(
        tile_xy[0], tile_len, received, tile_list[0], pixel_grad.reshape(24, 128)
    )
    returned = exchange(slot_grads, "cell", PEERS)
    colours = exchange(sum_colours(camera, returned, high, low_hot), "img", 4)
    grad_rows = sum_rows(returned, high, low_hot)
    share = lax.axis_index("img").astype(jnp.int32).reshape(1)
    grad_sh = coefficients(share, colours, positions)
    return (grad_rows.reshape(proj.shape), grad_sh)


def solution(mesh):
    return jax.shard_map(
        on_device,
        mesh=mesh,
        in_specs=(
            P("img", None, "cell"),
            P(None, "cell"),
            P(None, "cell"),
            P("img", None),
            P("img", "cell"),
            P("img", "cell"),
            P("img", None, "cell"),
            P("img", "cell", None),
            P("img", "cell"),
            P("img", None, "cell"),
        ),
        out_specs=(P("img", None, "cell"), P(None, ("cell", "img"))),
        check_vma=False,
    )
```

```python
import functools

import jax
import jax.numpy as jnp
from jax import lax
from jax.experimental import pallas as pl
from jax.experimental.pallas import tpu as pltpu
from jax.sharding import PartitionSpec as P

SH_ZERO = 0.28209479177387814
SH_ONE = 0.4886025119029199
SH_TWO = (
    1.0925484305920792,
    -1.0925484305920792,
    0.31539156525252005,
    -1.0925484305920792,
    0.5462742152960396,
)
SH_THREE = (
    -0.5900435899266435,
    2.890611442640554,
    -0.4570457994644658,
    0.3731763325901154,
    -0.4570457994644658,
    1.445305721320277,
    -0.5900435899266435,
)

F32 = jnp.float32
BF16 = jnp.bfloat16
PEERS = 128
CAP = 32
COMPS = 9
TILES = 4
DEPTH = 256
LOW = 256
HIGH = 32
PACK = 56
NOTHING = -1.0e4
LOG2E = 1.4426950408889634
EARLY = 6
ALONE = 3

LINEAR = (
    (SH_ZERO, 0, 0, 0),
    (0, 0, -SH_ONE, 0),
    (0, 0, 0, SH_ONE),
    (0, -SH_ONE, 0, 0),
    (0, SH_TWO[0], 0, 0),
    (0, 0, SH_TWO[1], 0),
    (SH_TWO[2], 0, 0, 0),
    (0, SH_TWO[3], 0, 0),
    (SH_TWO[4], 0, 0, 0),
    (0, 0, SH_THREE[0], 0),
    (0, SH_THREE[1], 0, 0),
    (0, 0, SH_THREE[2], 0),
    (0, 0, 0, SH_THREE[3]),
    (0, SH_THREE[4], 0, 0),
    (0, 0, 0, SH_THREE[5]),
    (0, SH_THREE[6], 0, 0),
)
QUADRATIC = (
    (1, 0, 0, 0, 0, 0, 0),
    (1, 0, 0, 0, 0, 0, 0),
    (1, 0, 0, 0, 0, 0, 0),
    (1, 0, 0, 0, 0, 0, 0),
    (0, 1, 0, 0, 0, 0, 0),
    (0, 0, 1, 0, 0, 0, 0),
    (0, 0, 0, -1, -1, 2, 0),
    (0, 0, 1, 0, 0, 0, 0),
    (0, 0, 0, 1, -1, 0, 0),
    (0, 0, 0, 3, -1, 0, 0),
    (0, 0, 0, 0, 0, 0, 1),
    (0, 0, 0, -1, -1, 4, 0),
    (0, 0, 0, -3, -3, 2, 0),
    (0, 0, 0, -1, -1, 4, 0),
    (0, 0, 0, 1, -1, 0, 0),
    (0, 0, 0, 1, -3, 0, 0),
)


def dot(left, right):
    return lax.dot_general(left, right, (((1,), (0,)), ((), ())), preferred_element_type=F32)


def dot_t(left, right):
    return lax.dot_general(left, right, (((1,), (1,)), ((), ())), preferred_element_type=F32)


def one_hot(rows, index):
    same = rows.astype(jnp.int16) == index.astype(jnp.int16)
    return jnp.where(same, jnp.ones((), BF16), jnp.zeros((), BF16))


def stacked(first, second, right):
    both = dot(jnp.concatenate([first, second], axis=0), right)
    return both[: first.shape[0]] + both[first.shape[0] :]


def iota(shape, axis):
    return lax.broadcasted_iota(jnp.int32, shape, axis)


def split(value, parts):
    out = []
    for _ in range(parts - 1):
        head = value.astype(BF16).astype(F32)
        out.append(head)
        value = value - head
    out.append(value.astype(BF16).astype(F32))
    return out


def column_consts(table, half):
    rows = iota((8, 128), 0)
    out = []
    for col in range(len(table[0])):
        vals = [float(table[8 * half + i][col]) for i in range(8)]
        if not any(vals):
            out.append(None)
            continue
        acc = jnp.zeros((8, 128), F32)
        for i, val in enumerate(vals):
            if val:
                acc = jnp.where(rows == i, val, acc)
        out.append(acc)
    return out


def form(consts, values):
    total = None
    for const, value in zip(consts, values):
        if const is None:
            continue
        term = const if value is None else const * value
        total = term if total is None else total + term
    return total


def basis_consts():
    return [(column_consts(LINEAR, half), column_consts(QUADRATIC, half)) for half in range(2)]


def basis_halves(consts, xoff, yoff, zoff):
    inv = lax.rsqrt(xoff * xoff + yoff * yoff + zoff * zoff)
    xpos, ypos, zpos = xoff * inv, yoff * inv, zoff * inv
    xsq, ysq, zsq, yz = xpos * xpos, ypos * ypos, zpos * zpos, ypos * zpos
    return [
        form(lin, (None, xpos, ypos, zpos)) * form(quad, (None, ypos, zpos, xsq, ysq, zsq, yz))
        for lin, quad in consts
    ]


def slot_index(idx_ref, cnt_ref, low_scr, high_scr):
    turned = jnp.transpose(idx_ref[...].astype(F32)).astype(jnp.int32)
    slots = jnp.concatenate([turned[32 * i : 32 * i + 32] for i in range(4)], axis=1)
    rows, cols = iota((PEERS, PEERS), 0), iota((PEERS, PEERS), 1)
    perm = (rows == 4 * (cols & 31) + (cols >> 5)).astype(F32).astype(BF16)
    counts = jnp.broadcast_to(cnt_ref[...], (8, PEERS)).astype(F32).astype(BF16)
    counts = dot(counts, perm)[0:1].astype(jnp.int32)
    live = iota((CAP, PEERS), 0) < counts
    low_scr[...] = slots & (LOW - 1)
    high_scr[...] = jnp.where(live, slots >> 8, -1)


def pair_row(ref, base, pair):
    first = ref[pl.ds(base + 2 * pair, 1), :]
    second = ref[pl.ds(base + 2 * pair + 1, 1), :]
    return jnp.concatenate([first, second], axis=1)


def returned_row(ref, base, pair):
    first = ref[pl.ds(base + pair, 1), :]
    second = ref[pl.ds(base + CAP // 2 + pair, 1), :]
    return jnp.concatenate([first, second], axis=1)


def owner_kernel(
    cam_hbm,
    proj_hbm,
    sh_hbm,
    pos_hbm,
    idx_hbm,
    cnt_hbm,
    out_ref,
    high_scr,
    hot_ref,
    cam_ref,
    proj_ref,
    sh_ref,
    pos_ref,
    idx_ref,
    cnt_ref,
    col_scr,
    low_scr,
    rows_scr,
    sems,
):
    copies = [
        pltpu.make_async_copy(src, dst, sems.at[i])
        for i, (src, dst) in enumerate(
            (
                (idx_hbm, idx_ref),
                (cnt_hbm, cnt_ref),
                (proj_hbm, proj_ref),
                (cam_hbm, cam_ref),
                (pos_hbm, pos_ref),
                (sh_hbm, sh_ref),
            )
        )
    ]
    for copy in copies:
        copy.start()
    consts = basis_consts()
    for copy in copies[:2]:
        copy.wait()
    slot_index(idx_ref, cnt_ref, low_scr, high_scr)
    low_iota = iota((LOW, 256), 0)
    high_iota = iota((HIGH, 256), 0)

    def table(ref, comps):
        return jnp.concatenate(
            [ref[pl.ds(par, 32 * comps, stride=2), :] for par in range(2)], axis=1
        )

    def pick(wide, mask, base, comps, pair):
        for comp in range(comps):
            row = jnp.sum(
                jnp.where(mask, wide[32 * comp : 32 * comp + 32], 0.0), axis=0, keepdims=True
            )
            at = 32 * (base + comp) + 2 * pair
            rows_scr[at : at + 1, :] = row[:, :128]
            rows_scr[at + 1 : at + 2, :] = row[:, 128:]

    def shade(chunk):
        lanes = slice(128 * chunk, 128 * chunk + 128)
        offs = [jnp.broadcast_to(pos_ref[i : i + 1, lanes], (8, 128)) - cam[i] for i in range(3)]
        first, second = basis_halves(consts, *offs)
        for chan in range(3):
            terms = sh_ref[16 * chan : 16 * chan + 8, lanes] * first
            terms = terms + sh_ref[16 * chan + 8 : 16 * chan + 16, lanes] * second
            colour = jnp.sum(terms, axis=0, keepdims=True) + 0.5
            at = 64 * chan + chunk
            col_scr[at : at + 1, :] = colour

    def hots(pair):
        hot = one_hot(low_iota, pair_row(low_scr, 0, pair))
        hot_ref[:, 256 * pair : 256 * pair + 256] = hot
        return hot

    def mask(pair):
        return high_iota == pair_row(high_scr, 0, pair)

    copies[2].wait()
    rows = split(table(proj_ref, 6), 3)
    rows = jnp.concatenate([rows[0], rows[1], rows[2][:160]], axis=0).astype(BF16)

    def sum_rows(wide):
        exact = wide[:160] + wide[192:352] + wide[384:544]
        return jnp.concatenate([exact, wide[160:192] + wide[352:384]], axis=0)

    cam, chunk = None, 0
    for pair in range(EARLY):
        hot = hots(pair)
        pick(sum_rows(dot(rows, hot)), mask(pair), 0, 6, pair)
        if pair == ALONE - 1:
            for copy in copies[3:]:
                copy.wait()
            cam = [jnp.broadcast_to(cam_ref[0:1, i : i + 1], (8, 128)) for i in range(3)]
        if pair >= ALONE:
            for _ in range(-(-64 // (EARLY - ALONE))):
                if chunk < 64:
                    shade(chunk)
                    chunk += 1
    tints = jnp.concatenate(split(table(col_scr, 3), 2), axis=0).astype(BF16)
    everything = jnp.concatenate([rows, tints], axis=0)
    for pair in range(EARLY, CAP // 2):
        wide = dot(everything, hots(pair))
        pick(sum_rows(wide), mask(pair), 0, 6, pair)
        pick(wide[544:640] + wide[640:736], mask(pair), 6, 3, pair)
    for pair in range(EARLY):
        wide = dot(tints, hot_ref[:, 256 * pair : 256 * pair + 256])
        pick(wide[:96] + wide[96:], mask(pair), 6, 3, pair)

    rows_scr[32 * COMPS :, :] = jnp.zeros((96, 128), F32)
    for k in range(3):
        turned = jnp.transpose(rows_scr[128 * k : 128 * k + 128, :])
        for i in range(4):
            out_ref[pl.ds(3 * i + k, 32, stride=12), :] = turned[32 * i : 32 * i + 32]


def render_kernel(
    xy_ref, len_ref, recv_ref, list_ref, grad_ref, out_ref, table_scr, coef_scr, right_scr, sums_scr
):
    for k in range(3):
        table_scr[128 * k : 128 * k + 128, :] = jnp.transpose(
            recv_ref[pl.ds(k, PEERS, stride=3), :]
        )

    slots = jnp.concatenate(
        [list_ref[t : t + 1, 128 * h : 128 * h + 128] for t in range(TILES) for h in range(2)],
        axis=0,
    )
    peer, place = slots >> 5, slots & (CAP - 1)
    row_iota = iota((8, 128), 0)

    def by_tile(ref, row):
        out = jnp.zeros((8, 128), jnp.int32)
        for t in range(TILES):
            out = jnp.where(
                row_iota >> 1 == t, jnp.broadcast_to(ref[row : row + 1, t : t + 1], (8, 128)), out
            )
        return out

    centre_x = (by_tile(xy_ref, 0).astype(F32) * 16.0 + 8.0) / 128.0
    centre_y = (by_tile(xy_ref, 1).astype(F32) * 16.0 + 8.0) / 128.0
    inside = (row_iota & 1) * 128 + iota((8, 128), 1) < by_tile(len_ref, 0)

    vals = [jnp.zeros((8, 128), F32) for _ in range(COMPS)]
    for q in range(CAP):
        mine = place == q
        for c in range(COMPS):
            row = jnp.broadcast_to(table_scr[32 * c + q : 32 * c + q + 1, :], (8, 128))
            vals[c] = jnp.where(mine, jnp.take_along_axis(row, peer, axis=1), vals[c])

    mean_x, mean_y, ca, cb, cc, opac = vals[:6]
    xrel, yrel = mean_x - centre_x, mean_y - centre_y
    shown = opac > 0.0
    lead_x = ca * xrel + cb * yrel
    lead_y = cc * yrel + cb * xrel
    const = -0.5 * (xrel * lead_x + yrel * lead_y) + jnp.log(jnp.where(shown, opac, 1.0))
    const = jnp.where(shown & inside, const, NOTHING)
    for i, value in enumerate((const, lead_x, lead_y, -0.5 * ca, -0.5 * cc, -cb)):
        coef_scr[8 * i : 8 * i + 8, :] = LOG2E * value
    tint = [split(v, 3) for v in vals[6:9]]
    for block, (one, two) in enumerate(((0, 0), (1, 0), (2, 1))):
        for c in range(3):
            right_scr[64 * block + 8 * c : 64 * block + 8 * c + 8, :] = tint[c][one]
            right_scr[64 * block + 24 + 8 * c : 64 * block + 32 + 8 * c, :] = tint[c][two]
        right_scr[64 * block + 48 : 64 * block + 64, :] = jnp.zeros((16, 128), F32)
    right_scr[192:256, :] = jnp.zeros((64, 128), F32)

    blank = jnp.zeros((2, 256), F32)
    blocks, sides = [], []
    for tile in range(TILES):
        grads = jnp.concatenate(
            [
                jnp.concatenate(
                    [grad_ref[8 * c + 2 * tile + h : 8 * c + 2 * tile + h + 1, :] for h in range(2)],
                    axis=1,
                )
                for c in range(3)
            ],
            axis=0,
        )
        g0, g1, g2 = split(grads, 3)
        blocks += [g0, g1, blank, g0, g2, blank, g0, g1, blank, jnp.zeros((8, 256), F32)]
        zero5 = jnp.zeros((5, 256), F32)
        sides.append(jnp.concatenate([g0, zero5, g1, zero5], axis=0).astype(BF16))
    turned = jnp.transpose(jnp.concatenate(blocks, axis=0)).astype(BF16)

    column = (iota((16, DEPTH), 0).astype(F32) - 7.5) / 128.0
    before = (iota((DEPTH, DEPTH), 0) < iota((DEPTH, DEPTH), 1)).astype(F32).astype(BF16)
    after = (iota((DEPTH, DEPTH), 0) > iota((DEPTH, DEPTH), 1)).astype(F32).astype(BF16)

    def both(ref, tile):
        return jnp.concatenate(
            [ref[pl.ds(2 * tile + h, 32, stride=8), :] for h in range(2)], axis=1
        ).astype(BF16)

    side = [column[8 * g : 8 * g + 8, :128] for g in range(2)]

    def exponents(tile):
        halves = []
        for h in range(2):
            at = 2 * tile + h
            rows = [
                jnp.broadcast_to(coef_scr[8 * i + at : 8 * i + at + 1, :], (8, 128))
                for i in range(6)
            ]
            along = [rows[0] + u * (rows[1] + u * rows[3]) for u in side]
            across = [rows[2] + u * rows[5] for u in side]
            blocks = []
            for i in range(16):
                vpos = (i - 7.5) / 128.0
                bend = vpos * rows[4]
                blocks += [along[g] + vpos * (across[g] + bend) for g in range(2)]
            halves.append(jnp.concatenate(blocks, axis=0))
        return jnp.concatenate(halves, axis=1)

    def front(tile):
        alpha = jnp.exp2(exponents(tile))
        logs = jnp.log(1.0 - alpha)
        l0 = logs.astype(BF16)
        return alpha, logs, l0, (logs - l0.astype(F32)).astype(BF16)

    def middle(tile, alpha, logs, l0, l1):
        weight = alpha * jnp.exp(stacked(l0, l1, before))
        flow = dot(turned[:, 32 * tile : 32 * tile + 32], both(right_scr, tile)) * weight
        s0 = flow.astype(BF16)
        return weight, flow, s0, (flow - s0.astype(F32)).astype(BF16)

    def back(tile, alpha, logs, weight, flow, s0, s1):
        power = flow - stacked(s0, s1, after) * (alpha * jnp.exp(-logs))
        w0 = weight.astype(BF16)
        w1 = (weight - w0.astype(F32)).astype(BF16)
        colours = dot(sides[tile], w0)
        colours = colours[0:8] + colours[8:16] + dot(sides[tile], w1)[0:8]

        plain = linear = square = None
        for i in range(8):
            vpos = (7.5 - i) / 128.0
            top, bottom = power[16 * i : 16 * i + 16], power[240 - 16 * i : 256 - 16 * i]
            total, slope = top + bottom, (bottom - top) * vpos
            curve = total * (vpos * vpos)
            plain = total if plain is None else plain + total
            linear = slope if linear is None else linear + slope
            square = curve if square is None else square + curve
        sums = [
            plain,
            plain * column,
            linear,
            plain * (column * column),
            square,
            linear * column,
        ]
        rows = [jnp.sum(v, axis=0, keepdims=True) for v in sums]
        rows += [colours[i : i + 1] for i in range(3)]
        for i, row in enumerate(rows):
            for h in range(2):
                sums_scr[8 * i + 2 * tile + h : 8 * i + 2 * tile + h + 1, :] = row[
                    :, 128 * h : 128 * h + 128
                ]

    for first in range(0, TILES, 2):
        group = (first, first + 1)
        fronts = [front(tile) for tile in group]
        middles = [middle(tile, *fronts[tile - first]) for tile in group]
        for tile in group:
            back(tile, *fronts[tile - first][:2], *middles[tile - first])

    m0, mu, mv, muu, mvv, muv, red, green, blue = [sums_scr[8 * i : 8 * i + 8, :] for i in range(9)]
    grads = [
        ca * mu + cb * mv - lead_x * m0,
        cc * mv + cb * mu - lead_y * m0,
        -0.5 * (muu - 2.0 * xrel * mu + xrel * xrel * m0),
        -(muv - yrel * mu - xrel * mv + xrel * yrel * m0),
        -0.5 * (mvv - 2.0 * yrel * mv + yrel * yrel * m0),
        jnp.where(shown, m0 / jnp.where(shown, opac, 1.0), 0.0),
        red,
        green,
        blue,
    ]
    grads = [split(grad, 2) for grad in grads]
    column_iota, place_iota = iota((2 * PEERS, 128), 0), iota((CAP // 2, 128), 0)
    column_of, row_of = peer + PEERS * (place & 1), place >> 1
    hots, wides = [], []
    for r in range(8):
        hots.append(one_hot(column_iota, column_of[r : r + 1]))
        mine = place_iota == row_of[r : r + 1]
        wides.append(
            jnp.concatenate(
                [
                    jnp.where(mine, grads[c][part][r : r + 1], 0.0)
                    for part in range(2)
                    for c in range(COMPS)
                ],
                axis=0,
            ).astype(BF16)
        )
    total = dot_t(jnp.concatenate(wides, axis=1), jnp.concatenate(hots, axis=1))
    half = 16 * COMPS
    total = total[:half] + total[half:]
    total = jnp.concatenate(
        [
            total[16 * c : 16 * c + 16, PEERS * bit : PEERS * bit + PEERS]
            for c in range(COMPS)
            for bit in range(2)
        ]
        + [jnp.zeros((96, 128), F32)],
        axis=0,
    )
    for k in range(3):
        out_ref[pl.ds(k, PEERS, stride=3), :] = jnp.transpose(total[128 * k : 128 * k + 128])


def sum_slots(comps, back_ref, high_ref, hot_ref, rows_scr):
    for k in sorted({comp // 4 for comp in comps}):
        block = jnp.concatenate(
            [back_ref[pl.ds(3 * i + k, 32, stride=12), :] for i in range(4)], axis=0
        )
        rows_scr[128 * k : 128 * k + 128, :] = jnp.transpose(block)
    high_iota = iota((HIGH, 256), 0)
    total = None
    for step in range(4):
        wides = []
        for pair in range(4 * step, 4 * step + 4):
            mask = high_iota == pair_row(high_ref, 0, pair)
            both = [split(returned_row(rows_scr, 32 * comp, pair), 2) for comp in comps]
            wides.append(
                jnp.concatenate(
                    [jnp.where(mask, b[part], 0.0) for part in range(2) for b in both], axis=0
                ).astype(BF16)
            )
        term = dot_t(
            jnp.concatenate(wides, axis=1), hot_ref[:, 1024 * step : 1024 * step + 1024]
        )
        total = term if total is None else total + term
    size = 32 * len(comps)
    return total[:size] + total[size:]


def colour_sum_kernel(cam_ref, back_ref, high_ref, hot_ref, col_ref, rows_scr):
    total = sum_slots((6, 7, 8), back_ref, high_ref, hot_ref, rows_scr)
    for par in range(2):
        for share in range(4):
            for chan in range(3):
                first = 32 * chan + 8 * share
                col_ref[pl.ds(PACK * share + 16 * chan + par, 8, stride=2), :] = total[
                    first : first + 8, 128 * par : 128 * par + 128
                ]
    lanes = iota((8, 128), 1)
    row = jnp.zeros((8, 128), F32)
    for i in range(3):
        row = jnp.where(lanes == i, jnp.broadcast_to(cam_ref[0:1, i : i + 1], (8, 128)), row)
    for share in range(4):
        col_ref[PACK * share + 48 : PACK * share + 56, :] = row


def row_sum_kernel(back_ref, high_ref, hot_ref, out_ref, rows_scr):
    total = sum_slots(range(6), back_ref, high_ref, hot_ref, rows_scr)
    for par in range(2):
        out_ref[pl.ds(par, 192, stride=2), :] = total[:, 128 * par : 128 * par + 128]


def coeff_kernel(share_ref, col_ref, pos_ref, out_ref):
    consts = basis_consts()
    share = share_ref[0]
    cams = []
    for image in range(4):
        row = col_ref[PACK * image + 48 : PACK * image + 56, :]
        cams.append([jnp.broadcast_to(row[:, i : i + 1], (8, 128)) for i in range(3)])

    def chunk(step, carry):
        lanes = pl.ds(pl.multiple_of(share * 2048 + step * 128, 128), 128)
        place = [jnp.broadcast_to(pos_ref[i : i + 1, lanes], (8, 128)) for i in range(3)]
        totals = [[None, None] for _ in range(3)]
        for image in range(4):
            cam = cams[image]
            halves = basis_halves(
                consts, place[0] - cam[0], place[1] - cam[1], place[2] - cam[2]
            )
            for chan in range(3):
                grad = jnp.broadcast_to(
                    col_ref[pl.ds(PACK * image + 16 * chan + step, 1), :], (8, 128)
                )
                for half in range(2):
                    term = grad * halves[half]
                    old = totals[chan][half]
                    totals[chan][half] = term if old is None else old + term
        here = pl.ds(pl.multiple_of(step * 128, 128), 128)
        for chan in range(3):
            for half in range(2):
                out_ref[16 * chan + 8 * half : 16 * chan + 8 * half + 8, here] = totals[chan][half]
        return carry

    lax.fori_loop(0, 16, chunk, 0, unroll=16)


VMEM = pl.BlockSpec(memory_space=pltpu.VMEM)
SMEM = pl.BlockSpec(memory_space=pltpu.SMEM)
HBM = pl.BlockSpec(memory_space=pltpu.HBM)
PARAMS = pltpu.CompilerParams(vmem_limit_bytes=40 * 1024 * 1024)


def shape(*dims):
    return jax.ShapeDtypeStruct(dims, F32)


def in_hbm(array):
    return pltpu.with_memory_space_constraint(array, pltpu.HBM)


def owner(camera, proj, coeffs, positions, index, count):
    return pl.pallas_call(
        owner_kernel,
        out_shape=(
            shape(384, 128),
            jax.ShapeDtypeStruct((CAP, PEERS), jnp.int32),
            jax.ShapeDtypeStruct((LOW, CAP * PEERS), BF16),
        ),
        in_specs=[HBM] * 6,
        out_specs=[VMEM] * 3,
        scratch_shapes=[
            pltpu.VMEM((1, 3), F32),
            pltpu.VMEM((384, 128), F32),
            pltpu.VMEM((48, 8192), F32),
            pltpu.VMEM((3, 8192), F32),
            pltpu.VMEM((CAP, PEERS), jnp.int32),
            pltpu.VMEM((1, PEERS), jnp.int32),
            pltpu.VMEM((192, 128), F32),
            pltpu.VMEM((CAP, PEERS), jnp.int32),
            pltpu.VMEM((384, 128), F32),
            pltpu.SemaphoreType.DMA((6,)),
        ],
        compiler_params=PARAMS,
        name="owner_rows",
    )(*[in_hbm(x) for x in (camera, proj, coeffs, positions, index, count)])


def render(tile_xy, tile_len, received, tile_list, pixel_grad):
    return pl.pallas_call(
        render_kernel,
        out_shape=shape(384, 128),
        in_specs=[VMEM] * 5,
        out_specs=VMEM,
        scratch_shapes=[
            pltpu.VMEM((384, 128), F32),
            pltpu.VMEM((48, 128), F32),
            pltpu.VMEM((256, 128), F32),
            pltpu.VMEM((72, 128), F32),
        ],
        compiler_params=PARAMS,
        name="render_tiles",
    )(tile_xy, tile_len, received, tile_list, pixel_grad)


def sum_colours(camera, returned, high, low_hot):
    return pl.pallas_call(
        colour_sum_kernel,
        out_shape=shape(4 * PACK, 128),
        in_specs=[VMEM] * 4,
        out_specs=VMEM,
        scratch_shapes=[pltpu.VMEM((384, 128), F32)],
        compiler_params=PARAMS,
        name="colour_sums",
    )(camera, returned, high, low_hot)


def sum_rows(returned, high, low_hot):
    return pl.pallas_call(
        row_sum_kernel,
        out_shape=shape(384, 128),
        in_specs=[VMEM] * 3,
        out_specs=VMEM,
        scratch_shapes=[pltpu.VMEM((384, 128), F32)],
        compiler_params=PARAMS,
        cost_estimate=pl.CostEstimate(
            flops=2 * 384 * 256 * 4096, bytes_accessed=400_000, transcendentals=0
        ),
        name="row_sums",
    )(returned, high, low_hot)


def coefficients(share, colours, positions):
    return pl.pallas_call(
        coeff_kernel,
        out_shape=shape(48, 2048),
        in_specs=[SMEM] + [VMEM] * 2,
        out_specs=VMEM,
        compiler_params=PARAMS,
        name="coeff_grads",
    )(share, colours, positions)


def exchange(rows, axis, peers):
    sent = rows.reshape(peers, 1, -1)
    got = lax.all_to_all(sent, axis, split_axis=0, concat_axis=0, tiled=True)
    return got.reshape(rows.shape)


def on_device(
    proj,
    sh_coeffs,
    positions,
    camera,
    send_index,
    send_count,
    tile_xy,
    tile_list,
    tile_len,
    pixel_grad,
):
    index = send_index.reshape(CAP, PEERS)
    outgoing, high, low_hot = owner(
        camera, proj.reshape(384, 128), sh_coeffs, positions, index, send_count
    )
    received = exchange(outgoing, "cell", PEERS)
    slot_grads = render(
        tile_xy[0], tile_len, received, tile_list[0], pixel_grad.reshape(24, 128)
    )
    returned = exchange(slot_grads, "cell", PEERS)
    colours = exchange(sum_colours(camera, returned, high, low_hot), "img", 4)
    grad_rows = sum_rows(returned, high, low_hot)
    share = lax.axis_index("img").astype(jnp.int32).reshape(1)
    grad_sh = coefficients(share, colours, positions)
    return (grad_rows.reshape(proj.shape), grad_sh)


def solution(mesh):
    return jax.shard_map(
        on_device,
        mesh=mesh,
        in_specs=(
            P("img", None, "cell"),
            P(None, "cell"),
            P(None, "cell"),
            P("img", None),
            P("img", "cell"),
            P("img", "cell"),
            P("img", None, "cell"),
            P("img", "cell", None),
            P("img", "cell"),
            P("img", None, "cell"),
        ),
        out_specs=(P("img", None, "cell"), P(None, ("cell", "img"))),
        check_vma=False,
    )
```

```python
import functools

import jax
import jax.numpy as jnp
from jax import lax
from jax.experimental import pallas as pl
from jax.experimental.pallas import tpu as pltpu
from jax.sharding import PartitionSpec as P

SH_ZERO = 0.28209479177387814
SH_ONE = 0.4886025119029199
SH_TWO = (
    1.0925484305920792,
    -1.0925484305920792,
    0.31539156525252005,
    -1.0925484305920792,
    0.5462742152960396,
)
SH_THREE = (
    -0.5900435899266435,
    2.890611442640554,
    -0.4570457994644658,
    0.3731763325901154,
    -0.4570457994644658,
    1.445305721320277,
    -0.5900435899266435,
)

F32 = jnp.float32
BF16 = jnp.bfloat16
PEERS = 128
CAP = 32
COMPS = 9
TILES = 4
DEPTH = 256
LOW = 256
HIGH = 32
PACK = 56
NOTHING = -1.0e4
LOG2E = 1.4426950408889634
EARLY = 6
ALONE = 3

LINEAR = (
    (SH_ZERO, 0, 0, 0),
    (0, 0, -SH_ONE, 0),
    (0, 0, 0, SH_ONE),
    (0, -SH_ONE, 0, 0),
    (0, SH_TWO[0], 0, 0),
    (0, 0, SH_TWO[1], 0),
    (SH_TWO[2], 0, 0, 0),
    (0, SH_TWO[3], 0, 0),
    (SH_TWO[4], 0, 0, 0),
    (0, 0, SH_THREE[0], 0),
    (0, SH_THREE[1], 0, 0),
    (0, 0, SH_THREE[2], 0),
    (0, 0, 0, SH_THREE[3]),
    (0, SH_THREE[4], 0, 0),
    (0, 0, 0, SH_THREE[5]),
    (0, SH_THREE[6], 0, 0),
)
QUADRATIC = (
    (1, 0, 0, 0, 0, 0, 0),
    (1, 0, 0, 0, 0, 0, 0),
    (1, 0, 0, 0, 0, 0, 0),
    (1, 0, 0, 0, 0, 0, 0),
    (0, 1, 0, 0, 0, 0, 0),
    (0, 0, 1, 0, 0, 0, 0),
    (0, 0, 0, -1, -1, 2, 0),
    (0, 0, 1, 0, 0, 0, 0),
    (0, 0, 0, 1, -1, 0, 0),
    (0, 0, 0, 3, -1, 0, 0),
    (0, 0, 0, 0, 0, 0, 1),
    (0, 0, 0, -1, -1, 4, 0),
    (0, 0, 0, -3, -3, 2, 0),
    (0, 0, 0, -1, -1, 4, 0),
    (0, 0, 0, 1, -1, 0, 0),
    (0, 0, 0, 1, -3, 0, 0),
)


def dot(left, right):
    return lax.dot_general(left, right, (((1,), (0,)), ((), ())), preferred_element_type=F32)


def dot_t(left, right):
    return lax.dot_general(left, right, (((1,), (1,)), ((), ())), preferred_element_type=F32)


def one_hot(rows, index):
    same = rows.astype(jnp.int16) == index.astype(jnp.int16)
    return jnp.where(same, jnp.ones((), BF16), jnp.zeros((), BF16))


def stacked(first, second, right):
    both = dot(jnp.concatenate([first, second], axis=0), right)
    return both[: first.shape[0]] + both[first.shape[0] :]


def iota(shape, axis):
    return lax.broadcasted_iota(jnp.int32, shape, axis)


def split(value, parts):
    out = []
    for _ in range(parts - 1):
        head = value.astype(BF16).astype(F32)
        out.append(head)
        value = value - head
    out.append(value.astype(BF16).astype(F32))
    return out


def column_consts(table, half):
    rows = iota((8, 128), 0)
    out = []
    for col in range(len(table[0])):
        vals = [float(table[8 * half + i][col]) for i in range(8)]
        if not any(vals):
            out.append(None)
            continue
        acc = jnp.zeros((8, 128), F32)
        for i, val in enumerate(vals):
            if val:
                acc = jnp.where(rows == i, val, acc)
        out.append(acc)
    return out


def form(consts, values):
    total = None
    for const, value in zip(consts, values):
        if const is None:
            continue
        term = const if value is None else const * value
        total = term if total is None else total + term
    return total


def basis_consts():
    return [(column_consts(LINEAR, half), column_consts(QUADRATIC, half)) for half in range(2)]


def basis_halves(consts, xoff, yoff, zoff):
    inv = lax.rsqrt(xoff * xoff + yoff * yoff + zoff * zoff)
    xpos, ypos, zpos = xoff * inv, yoff * inv, zoff * inv
    xsq, ysq, zsq, yz = xpos * xpos, ypos * ypos, zpos * zpos, ypos * zpos
    return [
        form(lin, (None, xpos, ypos, zpos)) * form(quad, (None, ypos, zpos, xsq, ysq, zsq, yz))
        for lin, quad in consts
    ]


def slot_index(idx_ref, cnt_ref, low_scr, high_scr):
    turned = jnp.transpose(idx_ref[...].astype(F32)).astype(jnp.int32)
    slots = jnp.concatenate([turned[32 * i : 32 * i + 32] for i in range(4)], axis=1)
    rows, cols = iota((PEERS, PEERS), 0), iota((PEERS, PEERS), 1)
    perm = (rows == 4 * (cols & 31) + (cols >> 5)).astype(F32).astype(BF16)
    counts = jnp.broadcast_to(cnt_ref[...], (8, PEERS)).astype(F32).astype(BF16)
    counts = dot(counts, perm)[0:1].astype(jnp.int32)
    live = iota((CAP, PEERS), 0) < counts
    low_scr[...] = slots & (LOW - 1)
    high_scr[...] = jnp.where(live, slots >> 8, -1)


def pair_row(ref, base, pair):
    first = ref[pl.ds(base + 2 * pair, 1), :]
    second = ref[pl.ds(base + 2 * pair + 1, 1), :]
    return jnp.concatenate([first, second], axis=1)


def returned_row(ref, base, pair):
    first = ref[pl.ds(base + pair, 1), :]
    second = ref[pl.ds(base + CAP // 2 + pair, 1), :]
    return jnp.concatenate([first, second], axis=1)


def owner_kernel(
    cam_hbm,
    proj_hbm,
    sh_hbm,
    pos_hbm,
    idx_hbm,
    cnt_hbm,
    out_ref,
    high_scr,
    hot_ref,
    cam_ref,
    proj_ref,
    sh_ref,
    pos_ref,
    idx_ref,
    cnt_ref,
    col_scr,
    low_scr,
    rows_scr,
    sems,
):
    copies = [
        pltpu.make_async_copy(src, dst, sems.at[i])
        for i, (src, dst) in enumerate(
            (
                (idx_hbm, idx_ref),
                (cnt_hbm, cnt_ref),
                (proj_hbm, proj_ref),
                (cam_hbm, cam_ref),
                (pos_hbm, pos_ref),
                (sh_hbm.at[:, pl.ds(0, 4096)], sh_ref.at[:, pl.ds(0, 4096)]),
                (sh_hbm.at[:, pl.ds(4096, 4096)], sh_ref.at[:, pl.ds(4096, 4096)]),
            )
        )
    ]
    for copy in copies:
        copy.start()
    consts = basis_consts()
    for copy in copies[:2]:
        copy.wait()
    slot_index(idx_ref, cnt_ref, low_scr, high_scr)
    low_iota = iota((LOW, 256), 0)
    high_iota = iota((HIGH, 256), 0)

    def table(ref, comps):
        return jnp.concatenate(
            [ref[pl.ds(par, 32 * comps, stride=2), :] for par in range(2)], axis=1
        )

    def pick(wide, mask, base, comps, pair):
        for comp in range(comps):
            row = jnp.sum(
                jnp.where(mask, wide[32 * comp : 32 * comp + 32], 0.0), axis=0, keepdims=True
            )
            at = 32 * (base + comp) + 2 * pair
            rows_scr[at : at + 1, :] = row[:, :128]
            rows_scr[at + 1 : at + 2, :] = row[:, 128:]

    def shade(chunk):
        lanes = slice(128 * chunk, 128 * chunk + 128)
        offs = [jnp.broadcast_to(pos_ref[i : i + 1, lanes], (8, 128)) - cam[i] for i in range(3)]
        first, second = basis_halves(consts, *offs)
        for chan in range(3):
            terms = sh_ref[16 * chan : 16 * chan + 8, lanes] * first
            terms = terms + sh_ref[16 * chan + 8 : 16 * chan + 16, lanes] * second
            colour = jnp.sum(terms, axis=0, keepdims=True) + 0.5
            at = 64 * chan + chunk
            col_scr[at : at + 1, :] = colour

    def hots(pair):
        hot = one_hot(low_iota, pair_row(low_scr, 0, pair))
        hot_ref[:, 256 * pair : 256 * pair + 256] = hot
        return hot

    def mask(pair):
        return high_iota == pair_row(high_scr, 0, pair)

    copies[2].wait()
    rows = split(table(proj_ref, 6), 3)
    rows = jnp.concatenate([rows[0], rows[1], rows[2][:160]], axis=0).astype(BF16)

    def sum_rows(wide):
        exact = wide[:160] + wide[192:352] + wide[384:544]
        return jnp.concatenate([exact, wide[160:192] + wide[352:384]], axis=0)

    cam, chunk = None, 0
    for pair in range(EARLY):
        hot = hots(pair)
        pick(sum_rows(dot(rows, hot)), mask(pair), 0, 6, pair)
        if pair == ALONE - 1:
            for copy in copies[3:6]:
                copy.wait()
            cam = [jnp.broadcast_to(cam_ref[0:1, i : i + 1], (8, 128)) for i in range(3)]
        if pair >= ALONE:
            for _ in range(-(-64 // (EARLY - ALONE))):
                if chunk == 32:
                    copies[6].wait()
                if chunk < 64:
                    shade(chunk)
                    chunk += 1
    tints = jnp.concatenate(split(table(col_scr, 3), 2), axis=0).astype(BF16)
    everything = jnp.concatenate([rows, tints], axis=0)
    for pair in range(EARLY, CAP // 2):
        wide = dot(everything, hots(pair))
        pick(sum_rows(wide), mask(pair), 0, 6, pair)
        pick(wide[544:640] + wide[640:736], mask(pair), 6, 3, pair)
    for pair in range(EARLY):
        wide = dot(tints, hot_ref[:, 256 * pair : 256 * pair + 256])
        pick(wide[:96] + wide[96:], mask(pair), 6, 3, pair)

    rows_scr[32 * COMPS :, :] = jnp.zeros((96, 128), F32)
    for k in range(3):
        turned = jnp.transpose(rows_scr[128 * k : 128 * k + 128, :])
        for i in range(4):
            out_ref[pl.ds(3 * i + k, 32, stride=12), :] = turned[32 * i : 32 * i + 32]


def render_kernel(
    xy_ref, len_ref, recv_ref, list_ref, grad_ref, out_ref, table_scr, coef_scr, right_scr, sums_scr
):
    for k in range(3):
        table_scr[128 * k : 128 * k + 128, :] = jnp.transpose(
            recv_ref[pl.ds(k, PEERS, stride=3), :]
        )

    slots = jnp.concatenate(
        [list_ref[t : t + 1, 128 * h : 128 * h + 128] for t in range(TILES) for h in range(2)],
        axis=0,
    )
    peer, place = slots >> 5, slots & (CAP - 1)
    row_iota = iota((8, 128), 0)

    def by_tile(ref, row):
        out = jnp.zeros((8, 128), jnp.int32)
        for t in range(TILES):
            out = jnp.where(
                row_iota >> 1 == t, jnp.broadcast_to(ref[row : row + 1, t : t + 1], (8, 128)), out
            )
        return out

    centre_x = (by_tile(xy_ref, 0).astype(F32) * 16.0 + 8.0) / 128.0
    centre_y = (by_tile(xy_ref, 1).astype(F32) * 16.0 + 8.0) / 128.0
    inside = (row_iota & 1) * 128 + iota((8, 128), 1) < by_tile(len_ref, 0)

    vals = [jnp.zeros((8, 128), F32) for _ in range(COMPS)]
    for q in range(CAP):
        mine = place == q
        for c in range(COMPS):
            row = jnp.broadcast_to(table_scr[32 * c + q : 32 * c + q + 1, :], (8, 128))
            vals[c] = jnp.where(mine, jnp.take_along_axis(row, peer, axis=1), vals[c])

    mean_x, mean_y, ca, cb, cc, opac = vals[:6]
    xrel, yrel = mean_x - centre_x, mean_y - centre_y
    shown = opac > 0.0
    lead_x = ca * xrel + cb * yrel
    lead_y = cc * yrel + cb * xrel
    const = -0.5 * (xrel * lead_x + yrel * lead_y) + jnp.log(jnp.where(shown, opac, 1.0))
    const = jnp.where(shown & inside, const, NOTHING)
    for i, value in enumerate((const, lead_x, lead_y, -0.5 * ca, -0.5 * cc, -cb)):
        coef_scr[8 * i : 8 * i + 8, :] = LOG2E * value
    tint = [split(v, 3) for v in vals[6:9]]
    for block, (one, two) in enumerate(((0, 0), (1, 0), (2, 1))):
        for c in range(3):
            right_scr[64 * block + 8 * c : 64 * block + 8 * c + 8, :] = tint[c][one]
            right_scr[64 * block + 24 + 8 * c : 64 * block + 32 + 8 * c, :] = tint[c][two]
        right_scr[64 * block + 48 : 64 * block + 64, :] = jnp.zeros((16, 128), F32)
    right_scr[192:256, :] = jnp.zeros((64, 128), F32)

    blank = jnp.zeros((2, 256), F32)
    blocks, sides = [], []
    for tile in range(TILES):
        grads = jnp.concatenate(
            [
                jnp.concatenate(
                    [grad_ref[8 * c + 2 * tile + h : 8 * c + 2 * tile + h + 1, :] for h in range(2)],
                    axis=1,
                )
                for c in range(3)
            ],
            axis=0,
        )
        g0, g1, g2 = split(grads, 3)
        blocks += [g0, g1, blank, g0, g2, blank, g0, g1, blank, jnp.zeros((8, 256), F32)]
        zero5 = jnp.zeros((5, 256), F32)
        sides.append(jnp.concatenate([g0, zero5, g1, zero5], axis=0).astype(BF16))
    turned = jnp.transpose(jnp.concatenate(blocks, axis=0)).astype(BF16)

    column = (iota((16, DEPTH), 0).astype(F32) - 7.5) / 128.0
    before = (iota((DEPTH, DEPTH), 0) < iota((DEPTH, DEPTH), 1)).astype(F32).astype(BF16)
    after = (iota((DEPTH, DEPTH), 0) > iota((DEPTH, DEPTH), 1)).astype(F32).astype(BF16)

    def both(ref, tile):
        return jnp.concatenate(
            [ref[pl.ds(2 * tile + h, 32, stride=8), :] for h in range(2)], axis=1
        ).astype(BF16)

    side = [column[8 * g : 8 * g + 8, :128] for g in range(2)]

    def exponents(tile):
        halves = []
        for h in range(2):
            at = 2 * tile + h
            rows = [
                jnp.broadcast_to(coef_scr[8 * i + at : 8 * i + at + 1, :], (8, 128))
                for i in range(6)
            ]
            along = [rows[0] + u * (rows[1] + u * rows[3]) for u in side]
            across = [rows[2] + u * rows[5] for u in side]
            blocks = []
            for i in range(16):
                vpos = (i - 7.5) / 128.0
                bend = vpos * rows[4]
                blocks += [along[g] + vpos * (across[g] + bend) for g in range(2)]
            halves.append(jnp.concatenate(blocks, axis=0))
        return jnp.concatenate(halves, axis=1)

    def front(tile):
        alpha = jnp.exp2(exponents(tile))
        logs = jnp.log(1.0 - alpha)
        l0 = logs.astype(BF16)
        return alpha, logs, l0, (logs - l0.astype(F32)).astype(BF16)

    def middle(tile, alpha, logs, l0, l1):
        weight = alpha * jnp.exp(stacked(l0, l1, before))
        flow = dot(turned[:, 32 * tile : 32 * tile + 32], both(right_scr, tile)) * weight
        s0 = flow.astype(BF16)
        return weight, flow, s0, (flow - s0.astype(F32)).astype(BF16)

    def back(tile, alpha, logs, weight, flow, s0, s1):
        power = flow - stacked(s0, s1, after) * (alpha * jnp.exp(-logs))
        w0 = weight.astype(BF16)
        w1 = (weight - w0.astype(F32)).astype(BF16)
        colours = dot(sides[tile], w0)
        colours = colours[0:8] + colours[8:16] + dot(sides[tile], w1)[0:8]

        plain = linear = square = None
        for i in range(8):
            vpos = (7.5 - i) / 128.0
            top, bottom = power[16 * i : 16 * i + 16], power[240 - 16 * i : 256 - 16 * i]
            total, slope = top + bottom, (bottom - top) * vpos
            curve = total * (vpos * vpos)
            plain = total if plain is None else plain + total
            linear = slope if linear is None else linear + slope
            square = curve if square is None else square + curve
        sums = [
            plain,
            plain * column,
            linear,
            plain * (column * column),
            square,
            linear * column,
        ]
        rows = [jnp.sum(v, axis=0, keepdims=True) for v in sums]
        rows += [colours[i : i + 1] for i in range(3)]
        for i, row in enumerate(rows):
            for h in range(2):
                sums_scr[8 * i + 2 * tile + h : 8 * i + 2 * tile + h + 1, :] = row[
                    :, 128 * h : 128 * h + 128
                ]

    for first in range(0, TILES, 2):
        group = (first, first + 1)
        fronts = [front(tile) for tile in group]
        middles = [middle(tile, *fronts[tile - first]) for tile in group]
        for tile in group:
            back(tile, *fronts[tile - first][:2], *middles[tile - first])

    m0, mu, mv, muu, mvv, muv, red, green, blue = [sums_scr[8 * i : 8 * i + 8, :] for i in range(9)]
    grads = [
        ca * mu + cb * mv - lead_x * m0,
        cc * mv + cb * mu - lead_y * m0,
        -0.5 * (muu - 2.0 * xrel * mu + xrel * xrel * m0),
        -(muv - yrel * mu - xrel * mv + xrel * yrel * m0),
        -0.5 * (mvv - 2.0 * yrel * mv + yrel * yrel * m0),
        jnp.where(shown, m0 / jnp.where(shown, opac, 1.0), 0.0),
        red,
        green,
        blue,
    ]
    grads = [split(grad, 2) for grad in grads]
    column_iota, place_iota = iota((2 * PEERS, 128), 0), iota((CAP // 2, 128), 0)
    column_of, row_of = peer + PEERS * (place & 1), place >> 1
    hots, wides = [], []
    for r in range(8):
        hots.append(one_hot(column_iota, column_of[r : r + 1]))
        mine = place_iota == row_of[r : r + 1]
        wides.append(
            jnp.concatenate(
                [
                    jnp.where(mine, grads[c][part][r : r + 1], 0.0)
                    for part in range(2)
                    for c in range(COMPS)
                ],
                axis=0,
            ).astype(BF16)
        )
    total = dot_t(jnp.concatenate(wides, axis=1), jnp.concatenate(hots, axis=1))
    half = 16 * COMPS
    total = total[:half] + total[half:]
    total = jnp.concatenate(
        [
            total[16 * c : 16 * c + 16, PEERS * bit : PEERS * bit + PEERS]
            for c in range(COMPS)
            for bit in range(2)
        ]
        + [jnp.zeros((96, 128), F32)],
        axis=0,
    )
    for k in range(3):
        out_ref[pl.ds(k, PEERS, stride=3), :] = jnp.transpose(total[128 * k : 128 * k + 128])


def sum_slots(comps, back_ref, high_ref, hot_ref, rows_scr):
    for k in sorted({comp // 4 for comp in comps}):
        block = jnp.concatenate(
            [back_ref[pl.ds(3 * i + k, 32, stride=12), :] for i in range(4)], axis=0
        )
        rows_scr[128 * k : 128 * k + 128, :] = jnp.transpose(block)
    high_iota = iota((HIGH, 256), 0)
    total = None
    for step in range(4):
        wides = []
        for pair in range(4 * step, 4 * step + 4):
            mask = high_iota == pair_row(high_ref, 0, pair)
            both = [split(returned_row(rows_scr, 32 * comp, pair), 2) for comp in comps]
            wides.append(
                jnp.concatenate(
                    [jnp.where(mask, b[part], 0.0) for part in range(2) for b in both], axis=0
                ).astype(BF16)
            )
        term = dot_t(
            jnp.concatenate(wides, axis=1), hot_ref[:, 1024 * step : 1024 * step + 1024]
        )
        total = term if total is None else total + term
    size = 32 * len(comps)
    return total[:size] + total[size:]


def sum_kernel(cam_ref, back_ref, high_ref, hot_ref, out_ref, col_ref, rows_scr):
    total = sum_slots(range(COMPS), back_ref, high_ref, hot_ref, rows_scr)
    for par in range(2):
        out_ref[pl.ds(par, 192, stride=2), :] = total[:192, 128 * par : 128 * par + 128]
        for share in range(4):
            for chan in range(3):
                first = 192 + 32 * chan + 8 * share
                col_ref[pl.ds(PACK * share + 16 * chan + par, 8, stride=2), :] = total[
                    first : first + 8, 128 * par : 128 * par + 128
                ]
    lanes = iota((8, 128), 1)
    row = jnp.zeros((8, 128), F32)
    for i in range(3):
        row = jnp.where(lanes == i, jnp.broadcast_to(cam_ref[0:1, i : i + 1], (8, 128)), row)
    for share in range(4):
        col_ref[PACK * share + 48 : PACK * share + 56, :] = jnp.where(
            lanes == 3, float(share), row
        )


def coeff_kernel(col_ref, pos_ref, rows_ref, out_hbm, rows_hbm, out_scr, sems):
    keep = pltpu.make_async_copy(rows_ref, rows_hbm, sems.at[2])
    keep.start()
    consts = basis_consts()
    share = jnp.max(col_ref[48:49, 3:4]).astype(jnp.int32)
    cams = []
    for image in range(4):
        row = col_ref[PACK * image + 48 : PACK * image + 56, :]
        cams.append([jnp.broadcast_to(row[:, i : i + 1], (8, 128)) for i in range(3)])

    def chunk(step):
        lanes = pl.ds(pl.multiple_of(share * 2048 + step * 128, 128), 128)
        place = [jnp.broadcast_to(pos_ref[i : i + 1, lanes], (8, 128)) for i in range(3)]
        totals = [[None, None] for _ in range(3)]
        for image in range(4):
            cam = cams[image]
            halves = basis_halves(
                consts, place[0] - cam[0], place[1] - cam[1], place[2] - cam[2]
            )
            for chan in range(3):
                at = PACK * image + 16 * chan + step
                grad = jnp.broadcast_to(col_ref[at : at + 1, :], (8, 128))
                for half in range(2):
                    term = grad * halves[half]
                    old = totals[chan][half]
                    totals[chan][half] = term if old is None else old + term
        for chan in range(3):
            for half in range(2):
                at = 16 * chan + 8 * half
                out_scr[at : at + 8, 128 * step : 128 * step + 128] = totals[chan][half]

    copies = []
    for half in range(2):
        for step in range(8 * half, 8 * half + 8):
            chunk(step)
        lanes = pl.ds(1024 * half, 1024)
        copies.append(
            pltpu.make_async_copy(out_scr.at[:, lanes], out_hbm.at[:, lanes], sems.at[half])
        )
        copies[-1].start()
    keep.wait()
    for copy in copies:
        copy.wait()


VMEM = pl.BlockSpec(memory_space=pltpu.VMEM)
HBM = pl.BlockSpec(memory_space=pltpu.HBM)
PARAMS = pltpu.CompilerParams(vmem_limit_bytes=40 * 1024 * 1024)


def shape(*dims):
    return jax.ShapeDtypeStruct(dims, F32)


def in_hbm(array):
    return pltpu.with_memory_space_constraint(array, pltpu.HBM)


def owner(camera, proj, coeffs, positions, index, count):
    return pl.pallas_call(
        owner_kernel,
        out_shape=(
            shape(384, 128),
            jax.ShapeDtypeStruct((CAP, PEERS), jnp.int32),
            jax.ShapeDtypeStruct((LOW, CAP * PEERS), BF16),
        ),
        in_specs=[HBM] * 6,
        out_specs=[VMEM] * 3,
        scratch_shapes=[
            pltpu.VMEM((1, 3), F32),
            pltpu.VMEM((384, 128), F32),
            pltpu.VMEM((48, 8192), F32),
            pltpu.VMEM((3, 8192), F32),
            pltpu.VMEM((CAP, PEERS), jnp.int32),
            pltpu.VMEM((1, PEERS), jnp.int32),
            pltpu.VMEM((192, 128), F32),
            pltpu.VMEM((CAP, PEERS), jnp.int32),
            pltpu.VMEM((384, 128), F32),
            pltpu.SemaphoreType.DMA((7,)),
        ],
        compiler_params=PARAMS,
        name="owner_rows",
    )(*[in_hbm(x) for x in (camera, proj, coeffs, positions, index, count)])


def render(tile_xy, tile_len, received, tile_list, pixel_grad):
    return pl.pallas_call(
        render_kernel,
        out_shape=shape(384, 128),
        in_specs=[VMEM] * 5,
        out_specs=VMEM,
        scratch_shapes=[
            pltpu.VMEM((384, 128), F32),
            pltpu.VMEM((48, 128), F32),
            pltpu.VMEM((256, 128), F32),
            pltpu.VMEM((72, 128), F32),
        ],
        compiler_params=PARAMS,
        name="render_tiles",
    )(tile_xy, tile_len, received, tile_list, pixel_grad)


def sum_returned(camera, returned, high, low_hot):
    return pl.pallas_call(
        sum_kernel,
        out_shape=(shape(384, 128), shape(4 * PACK, 128)),
        in_specs=[VMEM] * 4,
        out_specs=[VMEM] * 2,
        scratch_shapes=[pltpu.VMEM((384, 128), F32)],
        compiler_params=PARAMS,
        name="owner_sums",
    )(camera, returned, high, low_hot)


def coefficients(colours, positions, rows):
    return pl.pallas_call(
        coeff_kernel,
        out_shape=(shape(48, 2048), shape(384, 128)),
        in_specs=[VMEM] * 3,
        out_specs=[HBM] * 2,
        scratch_shapes=[pltpu.VMEM((48, 2048), F32), pltpu.SemaphoreType.DMA((3,))],
        compiler_params=PARAMS,
        name="coeff_grads",
    )(colours, positions, rows)


def exchange(rows, axis, peers):
    sent = rows.reshape(peers, 1, -1)
    got = lax.all_to_all(sent, axis, split_axis=0, concat_axis=0, tiled=True)
    return got.reshape(rows.shape)


def on_device(
    proj,
    sh_coeffs,
    positions,
    camera,
    send_index,
    send_count,
    tile_xy,
    tile_list,
    tile_len,
    pixel_grad,
):
    index = send_index.reshape(CAP, PEERS)
    outgoing, high, low_hot = owner(
        camera, proj.reshape(384, 128), sh_coeffs, positions, index, send_count
    )
    received = exchange(outgoing, "cell", PEERS)
    slot_grads = render(
        tile_xy[0], tile_len, received, tile_list[0], pixel_grad.reshape(24, 128)
    )
    returned = exchange(slot_grads, "cell", PEERS)
    grad_rows, colours = sum_returned(camera, returned, high, low_hot)
    colours = exchange(colours, "img", 4)
    grad_sh, grad_rows = coefficients(colours, positions, grad_rows)
    return (grad_rows.reshape(proj.shape), grad_sh)


def solution(mesh):
    return jax.shard_map(
        on_device,
        mesh=mesh,
        in_specs=(
            P("img", None, "cell"),
            P(None, "cell"),
            P(None, "cell"),
            P("img", None),
            P("img", "cell"),
            P("img", "cell"),
            P("img", None, "cell"),
            P("img", "cell", None),
            P("img", "cell"),
            P("img", None, "cell"),
        ),
        out_specs=(P("img", None, "cell"), P(None, ("cell", "img"))),
        check_vma=False,
    )
```

```python
import functools

import jax
import jax.numpy as jnp
from jax import lax
from jax.experimental import pallas as pl
from jax.experimental.pallas import tpu as pltpu
from jax.sharding import PartitionSpec as P

SH_ZERO = 0.28209479177387814
SH_ONE = 0.4886025119029199
SH_TWO = (
    1.0925484305920792,
    -1.0925484305920792,
    0.31539156525252005,
    -1.0925484305920792,
    0.5462742152960396,
)
SH_THREE = (
    -0.5900435899266435,
    2.890611442640554,
    -0.4570457994644658,
    0.3731763325901154,
    -0.4570457994644658,
    1.445305721320277,
    -0.5900435899266435,
)

F32 = jnp.float32
BF16 = jnp.bfloat16
PEERS = 128
CAP = 32
COMPS = 9
TILES = 4
DEPTH = 256
LOW = 256
HIGH = 32
PACK = 56
NOTHING = -1.0e4
LOG2E = 1.4426950408889634
EARLY = 6
LANED = 2
ALONE = 3

LINEAR = (
    (SH_ZERO, 0, 0, 0),
    (0, 0, -SH_ONE, 0),
    (0, 0, 0, SH_ONE),
    (0, -SH_ONE, 0, 0),
    (0, SH_TWO[0], 0, 0),
    (0, 0, SH_TWO[1], 0),
    (SH_TWO[2], 0, 0, 0),
    (0, SH_TWO[3], 0, 0),
    (SH_TWO[4], 0, 0, 0),
    (0, 0, SH_THREE[0], 0),
    (0, SH_THREE[1], 0, 0),
    (0, 0, SH_THREE[2], 0),
    (0, 0, 0, SH_THREE[3]),
    (0, SH_THREE[4], 0, 0),
    (0, 0, 0, SH_THREE[5]),
    (0, SH_THREE[6], 0, 0),
)
QUADRATIC = (
    (1, 0, 0, 0, 0, 0, 0),
    (1, 0, 0, 0, 0, 0, 0),
    (1, 0, 0, 0, 0, 0, 0),
    (1, 0, 0, 0, 0, 0, 0),
    (0, 1, 0, 0, 0, 0, 0),
    (0, 0, 1, 0, 0, 0, 0),
    (0, 0, 0, -1, -1, 2, 0),
    (0, 0, 1, 0, 0, 0, 0),
    (0, 0, 0, 1, -1, 0, 0),
    (0, 0, 0, 3, -1, 0, 0),
    (0, 0, 0, 0, 0, 0, 1),
    (0, 0, 0, -1, -1, 4, 0),
    (0, 0, 0, -3, -3, 2, 0),
    (0, 0, 0, -1, -1, 4, 0),
    (0, 0, 0, 1, -1, 0, 0),
    (0, 0, 0, 1, -3, 0, 0),
)


def dot(left, right):
    return lax.dot_general(left, right, (((1,), (0,)), ((), ())), preferred_element_type=F32)


def dot_t(left, right):
    return lax.dot_general(left, right, (((1,), (1,)), ((), ())), preferred_element_type=F32)


def one_hot(rows, index):
    same = rows.astype(jnp.int16) == index.astype(jnp.int16)
    return jnp.where(same, jnp.ones((), BF16), jnp.zeros((), BF16))


def stacked(first, second, right):
    both = dot(jnp.concatenate([first, second], axis=0), right)
    return both[: first.shape[0]] + both[first.shape[0] :]


def iota(shape, axis):
    return lax.broadcasted_iota(jnp.int32, shape, axis)


def split(value, parts):
    out = []
    for _ in range(parts - 1):
        head = value.astype(BF16).astype(F32)
        out.append(head)
        value = value - head
    out.append(value.astype(BF16).astype(F32))
    return out


def column_consts(table, half):
    rows = iota((8, 128), 0)
    out = []
    for col in range(len(table[0])):
        vals = [float(table[8 * half + i][col]) for i in range(8)]
        if not any(vals):
            out.append(None)
            continue
        acc = jnp.zeros((8, 128), F32)
        for i, val in enumerate(vals):
            if val:
                acc = jnp.where(rows == i, val, acc)
        out.append(acc)
    return out


def form(consts, values):
    total = None
    for const, value in zip(consts, values):
        if const is None:
            continue
        term = const if value is None else const * value
        total = term if total is None else total + term
    return total


def basis_consts():
    return [(column_consts(LINEAR, half), column_consts(QUADRATIC, half)) for half in range(2)]


def basis_halves(consts, xoff, yoff, zoff):
    inv = lax.rsqrt(xoff * xoff + yoff * yoff + zoff * zoff)
    xpos, ypos, zpos = xoff * inv, yoff * inv, zoff * inv
    xsq, ysq, zsq, yz = xpos * xpos, ypos * ypos, zpos * zpos, ypos * zpos
    return [
        form(lin, (None, xpos, ypos, zpos)) * form(quad, (None, ypos, zpos, xsq, ysq, zsq, yz))
        for lin, quad in consts
    ]


def column_sums(blocks):
    rows = iota((8, 128), 0)
    low = rows < 4
    blocks = [
        jnp.where(low, blocks[i], blocks[i + 4])
        + pltpu.roll(jnp.where(low, blocks[i + 4], blocks[i]), 4, 0)
        for i in range(4)
    ]
    for step in (2, 1):
        low = (rows & step) == 0
        blocks = [
            jnp.where(low, blocks[i], blocks[i + step])
            + jnp.where(
                low, pltpu.roll(blocks[i], 8 - step, 0), pltpu.roll(blocks[i + step], step, 0)
            )
            for i in range(step)
        ]
    return blocks[0]


def slot_index(idx_ref, cnt_ref, low_scr, high_scr):
    turned = jnp.transpose(idx_ref[...].astype(F32)).astype(jnp.int32)
    slots = jnp.concatenate([turned[32 * i : 32 * i + 32] for i in range(4)], axis=1)
    rows, cols = iota((PEERS, PEERS), 0), iota((PEERS, PEERS), 1)
    perm = (rows == 4 * (cols & 31) + (cols >> 5)).astype(F32).astype(BF16)
    counts = jnp.broadcast_to(cnt_ref[...], (8, PEERS)).astype(F32).astype(BF16)
    counts = dot(counts, perm)[0:1].astype(jnp.int32)
    live = iota((CAP, PEERS), 0) < counts
    low_scr[...] = slots & (LOW - 1)
    high_scr[...] = jnp.where(live, slots >> 8, -1)


def pair_row(ref, base, pair):
    first = ref[pl.ds(base + 2 * pair, 1), :]
    second = ref[pl.ds(base + 2 * pair + 1, 1), :]
    return jnp.concatenate([first, second], axis=1)


def returned_row(ref, base, pair):
    first = ref[pl.ds(base + pair, 1), :]
    second = ref[pl.ds(base + CAP // 2 + pair, 1), :]
    return jnp.concatenate([first, second], axis=1)


def owner_kernel(
    cam_hbm,
    proj_hbm,
    sh_hbm,
    pos_hbm,
    idx_hbm,
    cnt_hbm,
    out_ref,
    high_scr,
    hot_ref,
    cam_ref,
    proj_ref,
    sh_ref,
    pos_ref,
    idx_ref,
    cnt_ref,
    col_scr,
    low_scr,
    rows_scr,
    sems,
):
    copies = [
        pltpu.make_async_copy(src, dst, sems.at[i])
        for i, (src, dst) in enumerate(
            (
                (idx_hbm, idx_ref),
                (cnt_hbm, cnt_ref),
                (proj_hbm, proj_ref),
                (cam_hbm, cam_ref),
                (pos_hbm, pos_ref),
                (sh_hbm.at[:, pl.ds(0, 4096)], sh_ref.at[:, pl.ds(0, 4096)]),
                (sh_hbm.at[:, pl.ds(4096, 4096)], sh_ref.at[:, pl.ds(4096, 4096)]),
            )
        )
    ]
    for copy in copies:
        copy.start()
    consts = basis_consts()
    for copy in copies[:2]:
        copy.wait()
    slot_index(idx_ref, cnt_ref, low_scr, high_scr)
    low_iota = iota((LOW, 256), 0)
    high_iota = iota((HIGH, 256), 0)

    def table(ref, comps):
        return jnp.concatenate(
            [ref[pl.ds(par, 32 * comps, stride=2), :] for par in range(2)], axis=1
        )

    partial = {}

    def pick(wide, mask, base, comps, pair):
        for comp in range(base, base + comps):
            at = 32 * (comp - base)
            kept = jnp.where(mask, wide[at : at + 32], 0.0)
            kept = (kept[0:8] + kept[8:16]) + (kept[16:24] + kept[24:32])
            for h in range(2):
                partial[comp, 2 * pair + h] = kept[:, 128 * h : 128 * h + 128]
            first = 8 * (pair // 4)
            if all((comp, first + i) in partial for i in range(8)):
                rows_scr[32 * comp + first : 32 * comp + first + 8, :] = column_sums(
                    [partial.pop((comp, first + i)) for i in range(8)]
                )

    def shade(chunk):
        lanes = slice(128 * chunk, 128 * chunk + 128)
        offs = [jnp.broadcast_to(pos_ref[i : i + 1, lanes], (8, 128)) - cam[i] for i in range(3)]
        first, second = basis_halves(consts, *offs)
        for chan in range(3):
            terms = sh_ref[16 * chan : 16 * chan + 8, lanes] * first
            partial["shade", chan, chunk] = (
                terms + sh_ref[16 * chan + 8 : 16 * chan + 16, lanes] * second
            )
            if chunk % 8 == 7:
                at = 64 * chan + chunk - 7
                col_scr[at : at + 8, :] = 0.5 + column_sums(
                    [partial.pop(("shade", chan, chunk - 7 + i)) for i in range(8)]
                )

    def hots(pair):
        hot = one_hot(low_iota, pair_row(low_scr, 0, pair))
        hot_ref[:, 256 * pair : 256 * pair + 256] = hot
        return hot

    def mask(pair):
        return high_iota == pair_row(high_scr, 0, pair)

    copies[2].wait()
    rows = split(table(proj_ref, 6)[32 * LANED :], 3)
    size = 192 - 32 * LANED
    exact = size - 32
    rows = jnp.concatenate([rows[0], rows[1], rows[2][:exact]], axis=0).astype(BF16)
    both = 2 * size + exact

    def sum_rows(wide):
        first = wide[:exact] + wide[size : size + exact] + wide[2 * size : both]
        return jnp.concatenate([first, wide[exact:size] + wide[size + exact : 2 * size]], axis=0)

    lanes_of = [(high_scr[8 * b : 8 * b + 8, :] << 1) | (low_scr[8 * b : 8 * b + 8, :] >> 7) for b in range(4)]
    dead = [high_scr[8 * b : 8 * b + 8, :] < 0 for b in range(4)]
    lanes_of = [jnp.where(d, -1, v) for d, v in zip(dead, lanes_of)]
    within = [low_scr[8 * b : 8 * b + 8, :] & 127 for b in range(4)]
    found = [[jnp.zeros((8, 128), F32) for _ in range(4)] for _ in range(LANED)]

    def lane_gather(block):
        mine = [v == block for v in lanes_of]
        for comp in range(LANED):
            at = 64 * comp + block
            row = jnp.broadcast_to(proj_ref[at : at + 1, :], (8, 128))
            for b in range(4):
                value = jnp.take_along_axis(row, within[b], axis=1)
                found[comp][b] = jnp.where(mine[b], value, found[comp][b])

    cam, chunk = None, 0
    for pair in range(EARLY):
        hot = hots(pair)
        pick(sum_rows(dot(rows, hot)), mask(pair), LANED, 6 - LANED, pair)
        for block in range(4 * pair, 4 * pair + 4):
            lane_gather(block)
        if pair == ALONE - 1:
            for copy in copies[3:6]:
                copy.wait()
            cam = [jnp.broadcast_to(cam_ref[0:1, i : i + 1], (8, 128)) for i in range(3)]
        if pair >= ALONE:
            for _ in range(-(-64 // (EARLY - ALONE))):
                if chunk == 32:
                    copies[6].wait()
                if chunk < 64:
                    shade(chunk)
                    chunk += 1
    tints = jnp.concatenate(split(table(col_scr, 3), 2), axis=0).astype(BF16)
    everything = jnp.concatenate([rows, tints], axis=0)
    for pair in range(EARLY, CAP // 2):
        wide = dot(everything, hots(pair))
        pick(sum_rows(wide), mask(pair), LANED, 6 - LANED, pair)
        pick(wide[both : both + 96] + wide[both + 96 :], mask(pair), 6, 3, pair)
        for block in range(4 * pair, 4 * pair + 4):
            lane_gather(block)
    for pair in range(EARLY):
        wide = dot(tints, hot_ref[:, 256 * pair : 256 * pair + 256])
        pick(wide[:96] + wide[96:], mask(pair), 6, 3, pair)

    for comp in range(LANED):
        for b in range(4):
            rows_scr[32 * comp + 8 * b : 32 * comp + 8 * b + 8, :] = found[comp][b]
    rows_scr[32 * COMPS :, :] = jnp.zeros((96, 128), F32)
    for k in range(3):
        turned = jnp.transpose(rows_scr[128 * k : 128 * k + 128, :])
        for i in range(4):
            out_ref[pl.ds(3 * i + k, 32, stride=12), :] = turned[32 * i : 32 * i + 32]


def render_kernel(
    xy_ref, len_ref, recv_ref, list_ref, grad_ref, out_ref, table_scr, coef_scr, right_scr, sums_scr
):
    for k in range(3):
        table_scr[128 * k : 128 * k + 128, :] = jnp.transpose(
            recv_ref[pl.ds(k, PEERS, stride=3), :]
        )

    slots = jnp.concatenate(
        [list_ref[t : t + 1, 128 * h : 128 * h + 128] for t in range(TILES) for h in range(2)],
        axis=0,
    )
    peer, place = slots >> 5, slots & (CAP - 1)
    row_iota = iota((8, 128), 0)

    def by_tile(ref, row):
        out = jnp.zeros((8, 128), jnp.int32)
        for t in range(TILES):
            out = jnp.where(
                row_iota >> 1 == t, jnp.broadcast_to(ref[row : row + 1, t : t + 1], (8, 128)), out
            )
        return out

    centre_x = (by_tile(xy_ref, 0).astype(F32) * 16.0 + 8.0) / 128.0
    centre_y = (by_tile(xy_ref, 1).astype(F32) * 16.0 + 8.0) / 128.0
    inside = (row_iota & 1) * 128 + iota((8, 128), 1) < by_tile(len_ref, 0)

    vals = [jnp.zeros((8, 128), F32) for _ in range(COMPS)]
    for q in range(CAP):
        mine = place == q
        for c in range(COMPS):
            row = jnp.broadcast_to(table_scr[32 * c + q : 32 * c + q + 1, :], (8, 128))
            vals[c] = jnp.where(mine, jnp.take_along_axis(row, peer, axis=1), vals[c])

    mean_x, mean_y, ca, cb, cc, opac = vals[:6]
    xrel, yrel = mean_x - centre_x, mean_y - centre_y
    shown = opac > 0.0
    lead_x = ca * xrel + cb * yrel
    lead_y = cc * yrel + cb * xrel
    const = -0.5 * (xrel * lead_x + yrel * lead_y) + jnp.log(jnp.where(shown, opac, 1.0))
    const = jnp.where(shown & inside, const, NOTHING)
    for i, value in enumerate((const, lead_x, lead_y, -0.5 * ca, -0.5 * cc, -cb)):
        coef_scr[8 * i : 8 * i + 8, :] = LOG2E * value
    tint = [split(v, 3) for v in vals[6:9]]
    for block, (one, two) in enumerate(((0, 0), (1, 0), (2, 1))):
        for c in range(3):
            right_scr[64 * block + 8 * c : 64 * block + 8 * c + 8, :] = tint[c][one]
            right_scr[64 * block + 24 + 8 * c : 64 * block + 32 + 8 * c, :] = tint[c][two]
        right_scr[64 * block + 48 : 64 * block + 64, :] = jnp.zeros((16, 128), F32)
    right_scr[192:256, :] = jnp.zeros((64, 128), F32)

    blank = jnp.zeros((2, 256), F32)
    blocks, sides = [], []
    for tile in range(TILES):
        grads = jnp.concatenate(
            [
                jnp.concatenate(
                    [grad_ref[8 * c + 2 * tile + h : 8 * c + 2 * tile + h + 1, :] for h in range(2)],
                    axis=1,
                )
                for c in range(3)
            ],
            axis=0,
        )
        g0, g1, g2 = split(grads, 3)
        blocks += [g0, g1, blank, g0, g2, blank, g0, g1, blank, jnp.zeros((8, 256), F32)]
        zero5 = jnp.zeros((5, 256), F32)
        sides.append(jnp.concatenate([g0, zero5, g1, zero5], axis=0).astype(BF16))
    turned = jnp.transpose(jnp.concatenate(blocks, axis=0)).astype(BF16)

    column = (iota((16, DEPTH), 0).astype(F32) - 7.5) / 128.0
    before = (iota((DEPTH, DEPTH), 0) < iota((DEPTH, DEPTH), 1)).astype(F32).astype(BF16)
    after = (iota((DEPTH, DEPTH), 0) > iota((DEPTH, DEPTH), 1)).astype(F32).astype(BF16)

    def both(ref, tile):
        return jnp.concatenate(
            [ref[pl.ds(2 * tile + h, 32, stride=8), :] for h in range(2)], axis=1
        ).astype(BF16)

    side = [column[8 * g : 8 * g + 8, :128] for g in range(2)]

    def exponents(tile):
        halves = []
        for h in range(2):
            at = 2 * tile + h
            rows = [
                jnp.broadcast_to(coef_scr[8 * i + at : 8 * i + at + 1, :], (8, 128))
                for i in range(6)
            ]
            along = [rows[0] + u * (rows[1] + u * rows[3]) for u in side]
            across = [rows[2] + u * rows[5] for u in side]
            blocks = []
            for i in range(16):
                vpos = (i - 7.5) / 128.0
                bend = vpos * rows[4]
                blocks += [along[g] + vpos * (across[g] + bend) for g in range(2)]
            halves.append(jnp.concatenate(blocks, axis=0))
        return jnp.concatenate(halves, axis=1)

    def front(tile):
        alpha = jnp.exp2(exponents(tile))
        logs = jnp.log(1.0 - alpha)
        l0 = logs.astype(BF16)
        return alpha, logs, l0, (logs - l0.astype(F32)).astype(BF16)

    def middle(tile, alpha, logs, l0, l1):
        weight = alpha * jnp.exp(stacked(l0, l1, before))
        flow = dot(turned[:, 32 * tile : 32 * tile + 32], both(right_scr, tile)) * weight
        s0 = flow.astype(BF16)
        return weight, flow, s0, (flow - s0.astype(F32)).astype(BF16)

    def back(tile, alpha, logs, weight, flow, s0, s1):
        power = flow - stacked(s0, s1, after) * (alpha * jnp.exp(-logs))
        w0 = weight.astype(BF16)
        w1 = (weight - w0.astype(F32)).astype(BF16)
        colours = dot(sides[tile], w0)
        colours = colours[0:8] + colours[8:16] + dot(sides[tile], w1)[0:8]

        plain = linear = square = None
        for i in range(8):
            vpos = (7.5 - i) / 128.0
            top, bottom = power[16 * i : 16 * i + 16], power[240 - 16 * i : 256 - 16 * i]
            total, slope = top + bottom, (bottom - top) * vpos
            curve = total * (vpos * vpos)
            plain = total if plain is None else plain + total
            linear = slope if linear is None else linear + slope
            square = curve if square is None else square + curve
        sums = [
            plain,
            plain * column,
            linear,
            plain * (column * column),
            square,
            linear * column,
        ]
        rows = [jnp.sum(v, axis=0, keepdims=True) for v in sums]
        rows += [colours[i : i + 1] for i in range(3)]
        for i, row in enumerate(rows):
            for h in range(2):
                sums_scr[8 * i + 2 * tile + h : 8 * i + 2 * tile + h + 1, :] = row[
                    :, 128 * h : 128 * h + 128
                ]

    for first in range(0, TILES, 2):
        group = (first, first + 1)
        fronts = [front(tile) for tile in group]
        middles = [middle(tile, *fronts[tile - first]) for tile in group]
        for tile in group:
            back(tile, *fronts[tile - first][:2], *middles[tile - first])

    m0, mu, mv, muu, mvv, muv, red, green, blue = [sums_scr[8 * i : 8 * i + 8, :] for i in range(9)]
    grads = [
        ca * mu + cb * mv - lead_x * m0,
        cc * mv + cb * mu - lead_y * m0,
        -0.5 * (muu - 2.0 * xrel * mu + xrel * xrel * m0),
        -(muv - yrel * mu - xrel * mv + xrel * yrel * m0),
        -0.5 * (mvv - 2.0 * yrel * mv + yrel * yrel * m0),
        jnp.where(shown, m0 / jnp.where(shown, opac, 1.0), 0.0),
        red,
        green,
        blue,
    ]
    grads = [split(grad, 2) for grad in grads]
    column_iota, place_iota = iota((2 * PEERS, 128), 0), iota((CAP // 2, 128), 0)
    column_of, row_of = peer + PEERS * (place & 1), place >> 1
    hots, wides = [], []
    for r in range(8):
        hots.append(one_hot(column_iota, column_of[r : r + 1]))
        mine = place_iota == row_of[r : r + 1]
        wides.append(
            jnp.concatenate(
                [
                    jnp.where(mine, grads[c][part][r : r + 1], 0.0)
                    for part in range(2)
                    for c in range(COMPS)
                ],
                axis=0,
            ).astype(BF16)
        )
    total = dot_t(jnp.concatenate(wides, axis=1), jnp.concatenate(hots, axis=1))
    half = 16 * COMPS
    total = total[:half] + total[half:]
    total = jnp.concatenate(
        [
            total[16 * c : 16 * c + 16, PEERS * bit : PEERS * bit + PEERS]
            for c in range(COMPS)
            for bit in range(2)
        ]
        + [jnp.zeros((96, 128), F32)],
        axis=0,
    )
    for k in range(3):
        out_ref[pl.ds(k, PEERS, stride=3), :] = jnp.transpose(total[128 * k : 128 * k + 128])


def sum_slots(comps, back_ref, high_ref, hot_ref, rows_scr):
    for k in sorted({comp // 4 for comp in comps}):
        block = jnp.concatenate(
            [back_ref[pl.ds(3 * i + k, 32, stride=12), :] for i in range(4)], axis=0
        )
        rows_scr[128 * k : 128 * k + 128, :] = jnp.transpose(block)
    high_iota = iota((HIGH, 256), 0)
    total = None
    for step in range(4):
        wides = []
        for pair in range(4 * step, 4 * step + 4):
            mask = high_iota == pair_row(high_ref, 0, pair)
            both = [split(returned_row(rows_scr, 32 * comp, pair), 2) for comp in comps]
            wides.append(
                jnp.concatenate(
                    [jnp.where(mask, b[part], 0.0) for part in range(2) for b in both], axis=0
                ).astype(BF16)
            )
        term = dot_t(
            jnp.concatenate(wides, axis=1), hot_ref[:, 1024 * step : 1024 * step + 1024]
        )
        total = term if total is None else total + term
    size = 32 * len(comps)
    return total[:size] + total[size:]


def sum_kernel(cam_ref, back_ref, high_ref, hot_ref, out_ref, col_ref, rows_scr):
    total = sum_slots(range(COMPS), back_ref, high_ref, hot_ref, rows_scr)
    for par in range(2):
        out_ref[pl.ds(par, 192, stride=2), :] = total[:192, 128 * par : 128 * par + 128]
        for share in range(4):
            for chan in range(3):
                first = 192 + 32 * chan + 8 * share
                col_ref[pl.ds(PACK * share + 16 * chan + par, 8, stride=2), :] = total[
                    first : first + 8, 128 * par : 128 * par + 128
                ]
    lanes = iota((8, 128), 1)
    row = jnp.zeros((8, 128), F32)
    for i in range(3):
        row = jnp.where(lanes == i, jnp.broadcast_to(cam_ref[0:1, i : i + 1], (8, 128)), row)
    for share in range(4):
        col_ref[PACK * share + 48 : PACK * share + 56, :] = jnp.where(
            lanes == 3, float(share), row
        )


def coeff_kernel(col_ref, pos_ref, rows_ref, out_hbm, rows_hbm, out_scr, sems):
    keep = pltpu.make_async_copy(rows_ref, rows_hbm, sems.at[2])
    keep.start()
    consts = basis_consts()
    share = jnp.max(col_ref[48:49, 3:4]).astype(jnp.int32)
    cams = []
    for image in range(4):
        row = col_ref[PACK * image + 48 : PACK * image + 56, :]
        cams.append([jnp.broadcast_to(row[:, i : i + 1], (8, 128)) for i in range(3)])

    def chunk(step):
        lanes = pl.ds(pl.multiple_of(share * 2048 + step * 128, 128), 128)
        place = [jnp.broadcast_to(pos_ref[i : i + 1, lanes], (8, 128)) for i in range(3)]
        totals = [[None, None] for _ in range(3)]
        for image in range(4):
            cam = cams[image]
            halves = basis_halves(
                consts, place[0] - cam[0], place[1] - cam[1], place[2] - cam[2]
            )
            for chan in range(3):
                at = PACK * image + 16 * chan + step
                grad = jnp.broadcast_to(col_ref[at : at + 1, :], (8, 128))
                for half in range(2):
                    term = grad * halves[half]
                    old = totals[chan][half]
                    totals[chan][half] = term if old is None else old + term
        for chan in range(3):
            for half in range(2):
                at = 16 * chan + 8 * half
                out_scr[at : at + 8, 128 * step : 128 * step + 128] = totals[chan][half]

    copies = []
    for half in range(2):
        for step in range(8 * half, 8 * half + 8):
            chunk(step)
        lanes = pl.ds(1024 * half, 1024)
        copies.append(
            pltpu.make_async_copy(out_scr.at[:, lanes], out_hbm.at[:, lanes], sems.at[half])
        )
        copies[-1].start()
    keep.wait()
    for copy in copies:
        copy.wait()


VMEM = pl.BlockSpec(memory_space=pltpu.VMEM)
HBM = pl.BlockSpec(memory_space=pltpu.HBM)
PARAMS = pltpu.CompilerParams(vmem_limit_bytes=40 * 1024 * 1024)


def shape(*dims):
    return jax.ShapeDtypeStruct(dims, F32)


def in_hbm(array):
    return pltpu.with_memory_space_constraint(array, pltpu.HBM)


def owner(camera, proj, coeffs, positions, index, count):
    return pl.pallas_call(
        owner_kernel,
        out_shape=(
            shape(384, 128),
            jax.ShapeDtypeStruct((CAP, PEERS), jnp.int32),
            jax.ShapeDtypeStruct((LOW, CAP * PEERS), BF16),
        ),
        in_specs=[HBM] * 6,
        out_specs=[VMEM] * 3,
        scratch_shapes=[
            pltpu.VMEM((1, 3), F32),
            pltpu.VMEM((384, 128), F32),
            pltpu.VMEM((48, 8192), F32),
            pltpu.VMEM((3, 8192), F32),
            pltpu.VMEM((CAP, PEERS), jnp.int32),
            pltpu.VMEM((1, PEERS), jnp.int32),
            pltpu.VMEM((192, 128), F32),
            pltpu.VMEM((CAP, PEERS), jnp.int32),
            pltpu.VMEM((384, 128), F32),
            pltpu.SemaphoreType.DMA((7,)),
        ],
        compiler_params=PARAMS,
        name="owner_rows",
    )(*[in_hbm(x) for x in (camera, proj, coeffs, positions, index, count)])


def render(tile_xy, tile_len, received, tile_list, pixel_grad):
    return pl.pallas_call(
        render_kernel,
        out_shape=shape(384, 128),
        in_specs=[VMEM] * 5,
        out_specs=VMEM,
        scratch_shapes=[
            pltpu.VMEM((384, 128), F32),
            pltpu.VMEM((48, 128), F32),
            pltpu.VMEM((256, 128), F32),
            pltpu.VMEM((72, 128), F32),
        ],
        compiler_params=PARAMS,
        name="render_tiles",
    )(tile_xy, tile_len, received, tile_list, pixel_grad)


def sum_returned(camera, returned, high, low_hot):
    return pl.pallas_call(
        sum_kernel,
        out_shape=(shape(384, 128), shape(4 * PACK, 128)),
        in_specs=[VMEM] * 4,
        out_specs=[VMEM] * 2,
        scratch_shapes=[pltpu.VMEM((384, 128), F32)],
        compiler_params=PARAMS,
        name="owner_sums",
    )(camera, returned, high, low_hot)


def coefficients(colours, positions, rows):
    return pl.pallas_call(
        coeff_kernel,
        out_shape=(shape(48, 2048), shape(384, 128)),
        in_specs=[VMEM] * 3,
        out_specs=[HBM] * 2,
        scratch_shapes=[pltpu.VMEM((48, 2048), F32), pltpu.SemaphoreType.DMA((3,))],
        compiler_params=PARAMS,
        name="coeff_grads",
    )(colours, positions, rows)


def exchange(rows, axis, peers):
    sent = rows.reshape(peers, 1, -1)
    got = lax.all_to_all(sent, axis, split_axis=0, concat_axis=0, tiled=True)
    return got.reshape(rows.shape)


def on_device(
    proj,
    sh_coeffs,
    positions,
    camera,
    send_index,
    send_count,
    tile_xy,
    tile_list,
    tile_len,
    pixel_grad,
):
    index = send_index.reshape(CAP, PEERS)
    outgoing, high, low_hot = owner(
        camera, proj.reshape(384, 128), sh_coeffs, positions, index, send_count
    )
    received = exchange(outgoing, "cell", PEERS)
    slot_grads = render(
        tile_xy[0], tile_len, received, tile_list[0], pixel_grad.reshape(24, 128)
    )
    returned = exchange(slot_grads, "cell", PEERS)
    grad_rows, colours = sum_returned(camera, returned, high, low_hot)
    colours = exchange(colours, "img", 4)
    grad_sh, grad_rows = coefficients(colours, positions, grad_rows)
    return (grad_rows.reshape(proj.shape), grad_sh)


def solution(mesh):
    return jax.shard_map(
        on_device,
        mesh=mesh,
        in_specs=(
            P("img", None, "cell"),
            P(None, "cell"),
            P(None, "cell"),
            P("img", None),
            P("img", "cell"),
            P("img", "cell"),
            P("img", None, "cell"),
            P("img", "cell", None),
            P("img", "cell"),
            P("img", None, "cell"),
        ),
        out_specs=(P("img", None, "cell"), P(None, ("cell", "img"))),
        check_vma=False,
    )
```

```python
import functools

import jax
import jax.numpy as jnp
from jax import lax
from jax.experimental import pallas as pl
from jax.experimental.pallas import tpu as pltpu
from jax.sharding import PartitionSpec as P

SH_ZERO = 0.28209479177387814
SH_ONE = 0.4886025119029199
SH_TWO = (
    1.0925484305920792,
    -1.0925484305920792,
    0.31539156525252005,
    -1.0925484305920792,
    0.5462742152960396,
)
SH_THREE = (
    -0.5900435899266435,
    2.890611442640554,
    -0.4570457994644658,
    0.3731763325901154,
    -0.4570457994644658,
    1.445305721320277,
    -0.5900435899266435,
)

F32 = jnp.float32
BF16 = jnp.bfloat16
PEERS = 128
CAP = 32
COMPS = 9
TILES = 4
DEPTH = 256
LOW = 256
HIGH = 32
PACK = 56
NOTHING = -1.0e4
LOG2E = 1.4426950408889634
EARLY = 6
LANED = 2
ALONE = 3

LINEAR = (
    (SH_ZERO, 0, 0, 0),
    (0, 0, -SH_ONE, 0),
    (0, 0, 0, SH_ONE),
    (0, -SH_ONE, 0, 0),
    (0, SH_TWO[0], 0, 0),
    (0, 0, SH_TWO[1], 0),
    (SH_TWO[2], 0, 0, 0),
    (0, SH_TWO[3], 0, 0),
    (SH_TWO[4], 0, 0, 0),
    (0, 0, SH_THREE[0], 0),
    (0, SH_THREE[1], 0, 0),
    (0, 0, SH_THREE[2], 0),
    (0, 0, 0, SH_THREE[3]),
    (0, SH_THREE[4], 0, 0),
    (0, 0, 0, SH_THREE[5]),
    (0, SH_THREE[6], 0, 0),
)
QUADRATIC = (
    (1, 0, 0, 0, 0, 0, 0),
    (1, 0, 0, 0, 0, 0, 0),
    (1, 0, 0, 0, 0, 0, 0),
    (1, 0, 0, 0, 0, 0, 0),
    (0, 1, 0, 0, 0, 0, 0),
    (0, 0, 1, 0, 0, 0, 0),
    (0, 0, 0, -1, -1, 2, 0),
    (0, 0, 1, 0, 0, 0, 0),
    (0, 0, 0, 1, -1, 0, 0),
    (0, 0, 0, 3, -1, 0, 0),
    (0, 0, 0, 0, 0, 0, 1),
    (0, 0, 0, -1, -1, 4, 0),
    (0, 0, 0, -3, -3, 2, 0),
    (0, 0, 0, -1, -1, 4, 0),
    (0, 0, 0, 1, -1, 0, 0),
    (0, 0, 0, 1, -3, 0, 0),
)


def dot(left, right):
    return lax.dot_general(left, right, (((1,), (0,)), ((), ())), preferred_element_type=F32)


def dot_t(left, right):
    return lax.dot_general(left, right, (((1,), (1,)), ((), ())), preferred_element_type=F32)


def one_hot(rows, index):
    same = rows.astype(jnp.int16) == index.astype(jnp.int16)
    return jnp.where(same, jnp.ones((), BF16), jnp.zeros((), BF16))


def stacked(first, second, right):
    both = dot(jnp.concatenate([first, second], axis=0), right)
    return both[: first.shape[0]] + both[first.shape[0] :]


def iota(shape, axis):
    return lax.broadcasted_iota(jnp.int32, shape, axis)


def split(value, parts):
    out = []
    for _ in range(parts - 1):
        head = value.astype(BF16).astype(F32)
        out.append(head)
        value = value - head
    out.append(value.astype(BF16).astype(F32))
    return out


def column_consts(table, half):
    rows = iota((8, 128), 0)
    out = []
    for col in range(len(table[0])):
        vals = [float(table[8 * half + i][col]) for i in range(8)]
        if not any(vals):
            out.append(None)
            continue
        acc = jnp.zeros((8, 128), F32)
        for i, val in enumerate(vals):
            if val:
                acc = jnp.where(rows == i, val, acc)
        out.append(acc)
    return out


def form(consts, values):
    total = None
    for const, value in zip(consts, values):
        if const is None:
            continue
        term = const if value is None else const * value
        total = term if total is None else total + term
    return total


def basis_consts():
    return [(column_consts(LINEAR, half), column_consts(QUADRATIC, half)) for half in range(2)]


def unit_terms(place, cam):
    offs = [at - centre for at, centre in zip(place, cam)]
    inv = lax.rsqrt(offs[0] * offs[0] + offs[1] * offs[1] + offs[2] * offs[2])
    xpos, ypos, zpos = [off * inv for off in offs]
    return xpos, ypos, zpos, xpos * xpos, ypos * ypos, zpos * zpos, ypos * zpos


def basis_halves(consts, terms):
    xpos, ypos, zpos, xsq, ysq, zsq, yz = terms
    return [
        form(lin, (None, xpos, ypos, zpos)) * form(quad, (None, ypos, zpos, xsq, ysq, zsq, yz))
        for lin, quad in consts
    ]


def repeated(ref, row):
    return jnp.broadcast_to(ref[row : row + 1, :], (8, 128))


def column_sums(blocks):
    rows = iota((8, 128), 0)
    low = rows < 4
    blocks = [
        jnp.where(low, blocks[i], blocks[i + 4])
        + pltpu.roll(jnp.where(low, blocks[i + 4], blocks[i]), 4, 0)
        for i in range(4)
    ]
    for step in (2, 1):
        low = (rows & step) == 0
        blocks = [
            jnp.where(low, blocks[i], blocks[i + step])
            + jnp.where(
                low, pltpu.roll(blocks[i], 8 - step, 0), pltpu.roll(blocks[i + step], step, 0)
            )
            for i in range(step)
        ]
    return blocks[0]


def slot_index(idx_ref, cnt_ref, low_scr, high_scr):
    turned = jnp.transpose(idx_ref[...].astype(F32)).astype(jnp.int32)
    slots = jnp.concatenate([turned[32 * i : 32 * i + 32] for i in range(4)], axis=1)
    rows, cols = iota((PEERS, PEERS), 0), iota((PEERS, PEERS), 1)
    perm = (rows == 4 * (cols & 31) + (cols >> 5)).astype(F32).astype(BF16)
    counts = jnp.broadcast_to(cnt_ref[...], (8, PEERS)).astype(F32).astype(BF16)
    counts = dot(counts, perm)[0:1].astype(jnp.int32)
    live = iota((CAP, PEERS), 0) < counts
    low_scr[...] = slots & (LOW - 1)
    high_scr[...] = jnp.where(live, slots >> 8, -1)


def pair_row(ref, base, pair):
    first = ref[pl.ds(base + 2 * pair, 1), :]
    second = ref[pl.ds(base + 2 * pair + 1, 1), :]
    return jnp.concatenate([first, second], axis=1)


def returned_row(ref, base, pair):
    first = ref[pl.ds(base + pair, 1), :]
    second = ref[pl.ds(base + CAP // 2 + pair, 1), :]
    return jnp.concatenate([first, second], axis=1)


def owner_kernel(
    cam_hbm,
    proj_hbm,
    sh_hbm,
    pos_hbm,
    idx_hbm,
    cnt_hbm,
    out_ref,
    high_scr,
    hot_ref,
    cam_ref,
    proj_ref,
    sh_ref,
    pos_ref,
    idx_ref,
    cnt_ref,
    col_scr,
    low_scr,
    rows_scr,
    sems,
):
    copies = [
        pltpu.make_async_copy(src, dst, sems.at[i])
        for i, (src, dst) in enumerate(
            (
                (idx_hbm, idx_ref),
                (cnt_hbm, cnt_ref),
                (proj_hbm, proj_ref),
                (cam_hbm, cam_ref),
                (pos_hbm, pos_ref),
                (sh_hbm.at[:, pl.ds(0, 4096)], sh_ref.at[:, pl.ds(0, 4096)]),
                (sh_hbm.at[:, pl.ds(4096, 4096)], sh_ref.at[:, pl.ds(4096, 4096)]),
            )
        )
    ]
    for copy in copies:
        copy.start()
    consts = basis_consts()
    for copy in copies[:2]:
        copy.wait()
    slot_index(idx_ref, cnt_ref, low_scr, high_scr)
    low_iota = iota((LOW, 256), 0)
    high_iota = iota((HIGH, 256), 0)

    def table(ref, comps):
        return jnp.concatenate(
            [ref[pl.ds(par, 32 * comps, stride=2), :] for par in range(2)], axis=1
        )

    partial = {}

    def pick(wide, mask, base, comps, pair):
        for comp in range(base, base + comps):
            at = 32 * (comp - base)
            kept = jnp.where(mask, wide[at : at + 32], 0.0)
            kept = (kept[0:8] + kept[8:16]) + (kept[16:24] + kept[24:32])
            for h in range(2):
                partial[comp, 2 * pair + h] = kept[:, 128 * h : 128 * h + 128]
            first = 8 * (pair // 4)
            if all((comp, first + i) in partial for i in range(8)):
                rows_scr[32 * comp + first : 32 * comp + first + 8, :] = column_sums(
                    [partial.pop((comp, first + i)) for i in range(8)]
                )

    def shade(chunk):
        lanes = slice(128 * chunk, 128 * chunk + 128)
        place = [jnp.broadcast_to(pos_ref[i : i + 1, lanes], (8, 128)) for i in range(3)]
        first, second = basis_halves(consts, unit_terms(place, cam))
        for chan in range(3):
            terms = sh_ref[16 * chan : 16 * chan + 8, lanes] * first
            partial["shade", chan, chunk] = (
                terms + sh_ref[16 * chan + 8 : 16 * chan + 16, lanes] * second
            )
            if chunk % 8 == 7:
                at = 64 * chan + chunk - 7
                col_scr[at : at + 8, :] = 0.5 + column_sums(
                    [partial.pop(("shade", chan, chunk - 7 + i)) for i in range(8)]
                )

    def hots(pair):
        hot = one_hot(low_iota, pair_row(low_scr, 0, pair))
        hot_ref[:, 256 * pair : 256 * pair + 256] = hot
        return hot

    def mask(pair):
        return high_iota == pair_row(high_scr, 0, pair)

    copies[2].wait()
    rows = split(table(proj_ref, 6)[32 * LANED :], 3)
    size = 192 - 32 * LANED
    exact = size - 32
    rows = jnp.concatenate([rows[0], rows[1], rows[2][:exact]], axis=0).astype(BF16)
    both = 2 * size + exact

    def sum_rows(wide):
        first = wide[:exact] + wide[size : size + exact] + wide[2 * size : both]
        return jnp.concatenate([first, wide[exact:size] + wide[size + exact : 2 * size]], axis=0)

    lanes_of = [(high_scr[8 * b : 8 * b + 8, :] << 1) | (low_scr[8 * b : 8 * b + 8, :] >> 7) for b in range(4)]
    dead = [high_scr[8 * b : 8 * b + 8, :] < 0 for b in range(4)]
    lanes_of = [jnp.where(d, -1, v) for d, v in zip(dead, lanes_of)]
    within = [low_scr[8 * b : 8 * b + 8, :] & 127 for b in range(4)]
    found = [[jnp.zeros((8, 128), F32) for _ in range(4)] for _ in range(LANED)]

    def lane_gather(block):
        mine = [v == block for v in lanes_of]
        for comp in range(LANED):
            at = 64 * comp + block
            row = jnp.broadcast_to(proj_ref[at : at + 1, :], (8, 128))
            for b in range(4):
                value = jnp.take_along_axis(row, within[b], axis=1)
                found[comp][b] = jnp.where(mine[b], value, found[comp][b])

    cam, chunk = None, 0
    for pair in range(EARLY):
        hot = hots(pair)
        pick(sum_rows(dot(rows, hot)), mask(pair), LANED, 6 - LANED, pair)
        for block in range(4 * pair, 4 * pair + 4):
            lane_gather(block)
        if pair == ALONE - 1:
            for copy in copies[3:6]:
                copy.wait()
            cam = [jnp.broadcast_to(cam_ref[0:1, i : i + 1], (8, 128)) for i in range(3)]
        if pair >= ALONE:
            for _ in range(-(-64 // (EARLY - ALONE))):
                if chunk == 32:
                    copies[6].wait()
                if chunk < 64:
                    shade(chunk)
                    chunk += 1
    tints = jnp.concatenate(split(table(col_scr, 3), 2), axis=0).astype(BF16)
    everything = jnp.concatenate([rows, tints], axis=0)
    for pair in range(EARLY, CAP // 2):
        wide = dot(everything, hots(pair))
        pick(sum_rows(wide), mask(pair), LANED, 6 - LANED, pair)
        pick(wide[both : both + 96] + wide[both + 96 :], mask(pair), 6, 3, pair)
        for block in range(4 * pair, 4 * pair + 4):
            lane_gather(block)
    for pair in range(EARLY):
        wide = dot(tints, hot_ref[:, 256 * pair : 256 * pair + 256])
        pick(wide[:96] + wide[96:], mask(pair), 6, 3, pair)

    for comp in range(LANED):
        for b in range(4):
            rows_scr[32 * comp + 8 * b : 32 * comp + 8 * b + 8, :] = found[comp][b]
    rows_scr[32 * COMPS :, :] = jnp.zeros((96, 128), F32)
    for k in range(3):
        turned = jnp.transpose(rows_scr[128 * k : 128 * k + 128, :])
        for i in range(4):
            out_ref[pl.ds(3 * i + k, 32, stride=12), :] = turned[32 * i : 32 * i + 32]


def render_kernel(
    xy_ref, len_ref, recv_ref, list_ref, grad_ref, out_ref, table_scr, coef_scr, right_scr, sums_scr
):
    for k in range(3):
        table_scr[128 * k : 128 * k + 128, :] = jnp.transpose(
            recv_ref[pl.ds(k, PEERS, stride=3), :]
        )

    slots = jnp.concatenate(
        [list_ref[t : t + 1, 128 * h : 128 * h + 128] for t in range(TILES) for h in range(2)],
        axis=0,
    )
    peer, place = slots >> 5, slots & (CAP - 1)
    row_iota = iota((8, 128), 0)

    def by_tile(ref, row):
        out = jnp.zeros((8, 128), jnp.int32)
        for t in range(TILES):
            out = jnp.where(
                row_iota >> 1 == t, jnp.broadcast_to(ref[row : row + 1, t : t + 1], (8, 128)), out
            )
        return out

    centre_x = (by_tile(xy_ref, 0).astype(F32) * 16.0 + 8.0) / 128.0
    centre_y = (by_tile(xy_ref, 1).astype(F32) * 16.0 + 8.0) / 128.0
    inside = (row_iota & 1) * 128 + iota((8, 128), 1) < by_tile(len_ref, 0)

    vals = [jnp.zeros((8, 128), F32) for _ in range(COMPS)]
    for q in range(CAP):
        mine = place == q
        for c in range(COMPS):
            row = jnp.broadcast_to(table_scr[32 * c + q : 32 * c + q + 1, :], (8, 128))
            vals[c] = jnp.where(mine, jnp.take_along_axis(row, peer, axis=1), vals[c])

    mean_x, mean_y, ca, cb, cc, opac = vals[:6]
    xrel, yrel = mean_x - centre_x, mean_y - centre_y
    shown = opac > 0.0
    lead_x = ca * xrel + cb * yrel
    lead_y = cc * yrel + cb * xrel
    const = -0.5 * (xrel * lead_x + yrel * lead_y) + jnp.log(jnp.where(shown, opac, 1.0))
    const = jnp.where(shown & inside, const, NOTHING)
    for i, value in enumerate((const, lead_x, lead_y, -0.5 * ca, -0.5 * cc, -cb)):
        coef_scr[8 * i : 8 * i + 8, :] = LOG2E * value
    tint = [split(v, 3) for v in vals[6:9]]
    for block, (one, two) in enumerate(((0, 0), (1, 0), (2, 1))):
        for c in range(3):
            right_scr[64 * block + 8 * c : 64 * block + 8 * c + 8, :] = tint[c][one]
            right_scr[64 * block + 24 + 8 * c : 64 * block + 32 + 8 * c, :] = tint[c][two]
        right_scr[64 * block + 48 : 64 * block + 64, :] = jnp.zeros((16, 128), F32)
    right_scr[192:256, :] = jnp.zeros((64, 128), F32)

    blank = jnp.zeros((2, 256), F32)
    blocks, sides = [], []
    for tile in range(TILES):
        grads = jnp.concatenate(
            [
                jnp.concatenate(
                    [grad_ref[8 * c + 2 * tile + h : 8 * c + 2 * tile + h + 1, :] for h in range(2)],
                    axis=1,
                )
                for c in range(3)
            ],
            axis=0,
        )
        g0, g1, g2 = split(grads, 3)
        blocks += [g0, g1, blank, g0, g2, blank, g0, g1, blank, jnp.zeros((8, 256), F32)]
        zero5 = jnp.zeros((5, 256), F32)
        sides.append(jnp.concatenate([g0, zero5, g1, zero5], axis=0).astype(BF16))
    turned = jnp.transpose(jnp.concatenate(blocks, axis=0)).astype(BF16)

    column = (iota((16, DEPTH), 0).astype(F32) - 7.5) / 128.0
    before = (iota((DEPTH, DEPTH), 0) < iota((DEPTH, DEPTH), 1)).astype(F32).astype(BF16)
    after = (iota((DEPTH, DEPTH), 0) > iota((DEPTH, DEPTH), 1)).astype(F32).astype(BF16)

    def both(ref, tile):
        return jnp.concatenate(
            [ref[pl.ds(2 * tile + h, 32, stride=8), :] for h in range(2)], axis=1
        ).astype(BF16)

    side = [column[8 * g : 8 * g + 8, :128] for g in range(2)]

    def exponents(tile):
        halves = []
        for h in range(2):
            at = 2 * tile + h
            rows = [
                jnp.broadcast_to(coef_scr[8 * i + at : 8 * i + at + 1, :], (8, 128))
                for i in range(6)
            ]
            along = [rows[0] + u * (rows[1] + u * rows[3]) for u in side]
            across = [rows[2] + u * rows[5] for u in side]
            blocks = []
            for i in range(16):
                vpos = (i - 7.5) / 128.0
                bend = vpos * rows[4]
                blocks += [along[g] + vpos * (across[g] + bend) for g in range(2)]
            halves.append(jnp.concatenate(blocks, axis=0))
        return jnp.concatenate(halves, axis=1)

    def front(tile):
        alpha = jnp.exp2(exponents(tile))
        logs = jnp.log(1.0 - alpha)
        l0 = logs.astype(BF16)
        return alpha, l0, (logs - l0.astype(F32)).astype(BF16)

    def middle(tile, alpha, l0, l1):
        weight = alpha * jnp.exp(stacked(l0, l1, before))
        flow = dot(turned[:, 32 * tile : 32 * tile + 32], both(right_scr, tile)) * weight
        s0 = flow.astype(BF16)
        return weight, flow, s0, (flow - s0.astype(F32)).astype(BF16)

    def back(tile, alpha, weight, flow, s0, s1):
        power = flow - stacked(s0, s1, after) * (alpha / (1.0 - alpha))
        w0 = weight.astype(BF16)
        w1 = (weight - w0.astype(F32)).astype(BF16)
        colours = dot(sides[tile], w0)
        colours = colours[0:8] + colours[8:16] + dot(sides[tile], w1)[0:8]

        plain = linear = square = None
        for i in range(8):
            vpos = (7.5 - i) / 128.0
            top, bottom = power[16 * i : 16 * i + 16], power[240 - 16 * i : 256 - 16 * i]
            total, slope = top + bottom, (bottom - top) * vpos
            curve = total * (vpos * vpos)
            plain = total if plain is None else plain + total
            linear = slope if linear is None else linear + slope
            square = curve if square is None else square + curve
        sums = [
            plain,
            plain * column,
            linear,
            plain * (column * column),
            square,
            linear * column,
        ]
        rows = [jnp.sum(v, axis=0, keepdims=True) for v in sums]
        rows += [colours[i : i + 1] for i in range(3)]
        for i, row in enumerate(rows):
            for h in range(2):
                sums_scr[8 * i + 2 * tile + h : 8 * i + 2 * tile + h + 1, :] = row[
                    :, 128 * h : 128 * h + 128
                ]

    for first in range(0, TILES, 2):
        group = (first, first + 1)
        fronts = [front(tile) for tile in group]
        middles = [middle(tile, *fronts[tile - first]) for tile in group]
        for tile in group:
            back(tile, fronts[tile - first][0], *middles[tile - first])

    m0, mu, mv, muu, mvv, muv, red, green, blue = [sums_scr[8 * i : 8 * i + 8, :] for i in range(9)]
    grads = [
        ca * mu + cb * mv - lead_x * m0,
        cc * mv + cb * mu - lead_y * m0,
        -0.5 * (muu - 2.0 * xrel * mu + xrel * xrel * m0),
        -(muv - yrel * mu - xrel * mv + xrel * yrel * m0),
        -0.5 * (mvv - 2.0 * yrel * mv + yrel * yrel * m0),
        jnp.where(shown, m0 / jnp.where(shown, opac, 1.0), 0.0),
        red,
        green,
        blue,
    ]
    grads = [split(grad, 2) for grad in grads]
    column_iota, place_iota = iota((2 * PEERS, 128), 0), iota((CAP // 2, 128), 0)
    column_of, row_of = peer + PEERS * (place & 1), place >> 1
    hots, wides = [], []
    for r in range(8):
        hots.append(one_hot(column_iota, column_of[r : r + 1]))
        mine = place_iota == row_of[r : r + 1]
        wides.append(
            jnp.concatenate(
                [
                    jnp.where(mine, grads[c][part][r : r + 1], 0.0)
                    for part in range(2)
                    for c in range(COMPS)
                ],
                axis=0,
            ).astype(BF16)
        )
    total = dot_t(jnp.concatenate(wides, axis=1), jnp.concatenate(hots, axis=1))
    half = 16 * COMPS
    total = total[:half] + total[half:]
    total = jnp.concatenate(
        [
            total[16 * c : 16 * c + 16, PEERS * bit : PEERS * bit + PEERS]
            for c in range(COMPS)
            for bit in range(2)
        ]
        + [jnp.zeros((96, 128), F32)],
        axis=0,
    )
    for k in range(3):
        out_ref[pl.ds(k, PEERS, stride=3), :] = jnp.transpose(total[128 * k : 128 * k + 128])


def sum_slots(comps, back_ref, high_ref, hot_ref, rows_scr):
    for k in sorted({comp // 4 for comp in comps}):
        block = jnp.concatenate(
            [back_ref[pl.ds(3 * i + k, 32, stride=12), :] for i in range(4)], axis=0
        )
        rows_scr[128 * k : 128 * k + 128, :] = jnp.transpose(block)
    high_iota = iota((HIGH, 256), 0)
    total = None
    for step in range(4):
        wides = []
        for pair in range(4 * step, 4 * step + 4):
            mask = high_iota == pair_row(high_ref, 0, pair)
            both = [split(returned_row(rows_scr, 32 * comp, pair), 2) for comp in comps]
            wides.append(
                jnp.concatenate(
                    [jnp.where(mask, b[part], 0.0) for part in range(2) for b in both], axis=0
                ).astype(BF16)
            )
        term = dot_t(
            jnp.concatenate(wides, axis=1), hot_ref[:, 1024 * step : 1024 * step + 1024]
        )
        total = term if total is None else total + term
    size = 32 * len(comps)
    return total[:size] + total[size:]


def sum_kernel(cam_ref, back_ref, high_ref, hot_ref, out_ref, col_ref, rows_scr):
    total = sum_slots(range(COMPS), back_ref, high_ref, hot_ref, rows_scr)
    for par in range(2):
        out_ref[pl.ds(par, 192, stride=2), :] = total[:192, 128 * par : 128 * par + 128]
        for share in range(4):
            for chan in range(3):
                first = 192 + 32 * chan + 8 * share
                col_ref[pl.ds(PACK * share + 16 * chan + par, 8, stride=2), :] = total[
                    first : first + 8, 128 * par : 128 * par + 128
                ]
    lanes = iota((8, 128), 1)
    row = jnp.zeros((8, 128), F32)
    for i in range(3):
        row = jnp.where(lanes == i, jnp.broadcast_to(cam_ref[0:1, i : i + 1], (8, 128)), row)
    for share in range(4):
        col_ref[PACK * share + 48 : PACK * share + 56, :] = jnp.where(
            lanes == 3, float(share), row
        )


def coeff_kernel(col_ref, pos_ref, rows_ref, out_hbm, rows_hbm, out_scr, unit_scr, sems):
    keep = pltpu.make_async_copy(rows_ref, rows_hbm, sems.at[4])
    keep.start()
    consts = basis_consts()
    share = jnp.max(col_ref[48:49, 3:4]).astype(jnp.int32)
    for i in range(3):
        for at in range(16):
            lanes = pl.ds(pl.multiple_of(share * 2048 + at * 128, 128), 128)
            unit_scr[16 * i + at : 16 * i + at + 1, :] = pos_ref[i : i + 1, lanes]
    place = [unit_scr[16 * i : 16 * i + 16, :] for i in range(3)]
    for image in range(4):
        row = col_ref[PACK * image + 48 : PACK * image + 49, :]
        cam = [jnp.broadcast_to(row[:, i : i + 1], (16, 128)) for i in range(3)]
        for i, term in enumerate(unit_terms(place, cam)):
            at = 112 * image + 16 * i
            unit_scr[at : at + 16, :] = term

    def chunk(step):
        totals = [[None, None] for _ in range(3)]
        for image in range(4):
            halves = basis_halves(
                consts, [repeated(unit_scr, 112 * image + 16 * i + step) for i in range(7)]
            )
            for chan in range(3):
                grad = repeated(col_ref, PACK * image + 16 * chan + step)
                for half in range(2):
                    term = grad * halves[half]
                    old = totals[chan][half]
                    totals[chan][half] = term if old is None else old + term
        for chan in range(3):
            for half in range(2):
                at = 16 * chan + 8 * half
                out_scr[at : at + 8, 128 * step : 128 * step + 128] = totals[chan][half]

    copies = []
    for piece in range(4):
        for step in range(4 * piece, 4 * piece + 4):
            chunk(step)
        lanes = pl.ds(512 * piece, 512)
        copies.append(
            pltpu.make_async_copy(out_scr.at[:, lanes], out_hbm.at[:, lanes], sems.at[piece])
        )
        copies[-1].start()
    keep.wait()
    for copy in copies:
        copy.wait()


VMEM = pl.BlockSpec(memory_space=pltpu.VMEM)
HBM = pl.BlockSpec(memory_space=pltpu.HBM)
PARAMS = pltpu.CompilerParams(vmem_limit_bytes=40 * 1024 * 1024)


def shape(*dims):
    return jax.ShapeDtypeStruct(dims, F32)


def in_hbm(array):
    return pltpu.with_memory_space_constraint(array, pltpu.HBM)


def owner(camera, proj, coeffs, positions, index, count):
    return pl.pallas_call(
        owner_kernel,
        out_shape=(
            shape(384, 128),
            jax.ShapeDtypeStruct((CAP, PEERS), jnp.int32),
            jax.ShapeDtypeStruct((LOW, CAP * PEERS), BF16),
        ),
        in_specs=[HBM] * 6,
        out_specs=[VMEM] * 3,
        scratch_shapes=[
            pltpu.VMEM((1, 3), F32),
            pltpu.VMEM((384, 128), F32),
            pltpu.VMEM((48, 8192), F32),
            pltpu.VMEM((3, 8192), F32),
            pltpu.VMEM((CAP, PEERS), jnp.int32),
            pltpu.VMEM((1, PEERS), jnp.int32),
            pltpu.VMEM((192, 128), F32),
            pltpu.VMEM((CAP, PEERS), jnp.int32),
            pltpu.VMEM((384, 128), F32),
            pltpu.SemaphoreType.DMA((7,)),
        ],
        compiler_params=PARAMS,
        name="owner_rows",
    )(*[in_hbm(x) for x in (camera, proj, coeffs, positions, index, count)])


def render(tile_xy, tile_len, received, tile_list, pixel_grad):
    return pl.pallas_call(
        render_kernel,
        out_shape=shape(384, 128),
        in_specs=[VMEM] * 5,
        out_specs=VMEM,
        scratch_shapes=[
            pltpu.VMEM((384, 128), F32),
            pltpu.VMEM((48, 128), F32),
            pltpu.VMEM((256, 128), F32),
            pltpu.VMEM((72, 128), F32),
        ],
        compiler_params=PARAMS,
        name="render_tiles",
    )(tile_xy, tile_len, received, tile_list, pixel_grad)


def sum_returned(camera, returned, high, low_hot):
    return pl.pallas_call(
        sum_kernel,
        out_shape=(shape(384, 128), shape(4 * PACK, 128)),
        in_specs=[VMEM] * 4,
        out_specs=[VMEM] * 2,
        scratch_shapes=[pltpu.VMEM((384, 128), F32)],
        compiler_params=PARAMS,
        name="owner_sums",
    )(camera, returned, high, low_hot)


def coefficients(colours, positions, rows):
    return pl.pallas_call(
        coeff_kernel,
        out_shape=(shape(48, 2048), shape(384, 128)),
        in_specs=[VMEM] * 3,
        out_specs=[HBM] * 2,
        scratch_shapes=[
            pltpu.VMEM((48, 2048), F32),
            pltpu.VMEM((448, 128), F32),
            pltpu.SemaphoreType.DMA((5,)),
        ],
        compiler_params=PARAMS,
        name="coeff_grads",
    )(colours, positions, rows)


def exchange(rows, axis, peers):
    sent = rows.reshape(peers, 1, -1)
    got = lax.all_to_all(sent, axis, split_axis=0, concat_axis=0, tiled=True)
    return got.reshape(rows.shape)


def on_device(
    proj,
    sh_coeffs,
    positions,
    camera,
    send_index,
    send_count,
    tile_xy,
    tile_list,
    tile_len,
    pixel_grad,
):
    index = send_index.reshape(CAP, PEERS)
    outgoing, high, low_hot = owner(
        camera, proj.reshape(384, 128), sh_coeffs, positions, index, send_count
    )
    received = exchange(outgoing, "cell", PEERS)
    slot_grads = render(
        tile_xy[0], tile_len, received, tile_list[0], pixel_grad.reshape(24, 128)
    )
    returned = exchange(slot_grads, "cell", PEERS)
    grad_rows, colours = sum_returned(camera, returned, high, low_hot)
    colours = exchange(colours, "img", 4)
    grad_sh, grad_rows = coefficients(colours, positions, grad_rows)
    return (grad_rows.reshape(proj.shape), grad_sh)


def solution(mesh):
    return jax.shard_map(
        on_device,
        mesh=mesh,
        in_specs=(
            P("img", None, "cell"),
            P(None, "cell"),
            P(None, "cell"),
            P("img", None),
            P("img", "cell"),
            P("img", "cell"),
            P("img", None, "cell"),
            P("img", "cell", None),
            P("img", "cell"),
            P("img", None, "cell"),
        ),
        out_specs=(P("img", None, "cell"), P(None, ("cell", "img"))),
        check_vma=False,
    )
```

```python
import functools

import jax
import jax.numpy as jnp
from jax import lax
from jax.experimental import pallas as pl
from jax.experimental.pallas import tpu as pltpu
from jax.sharding import PartitionSpec as P

SH_ZERO = 0.28209479177387814
SH_ONE = 0.4886025119029199
SH_TWO = (
    1.0925484305920792,
    -1.0925484305920792,
    0.31539156525252005,
    -1.0925484305920792,
    0.5462742152960396,
)
SH_THREE = (
    -0.5900435899266435,
    2.890611442640554,
    -0.4570457994644658,
    0.3731763325901154,
    -0.4570457994644658,
    1.445305721320277,
    -0.5900435899266435,
)

F32 = jnp.float32
BF16 = jnp.bfloat16
PEERS = 128
CAP = 32
COMPS = 9
TILES = 4
DEPTH = 256
LOW = 256
HIGH = 32
PACK = 56
NOTHING = -1.0e4
CELL = ("y2", "y1", "y0", "z2", "z1", "z0", "core")
ORDER = ("y0", "y1", "y2", "z0", "z1", "z2", "core")
LOG2E = 1.4426950408889634
EARLY = 6
LANED = 2
ALONE = 3

LINEAR = (
    (SH_ZERO, 0, 0, 0),
    (0, 0, -SH_ONE, 0),
    (0, 0, 0, SH_ONE),
    (0, -SH_ONE, 0, 0),
    (0, SH_TWO[0], 0, 0),
    (0, 0, SH_TWO[1], 0),
    (SH_TWO[2], 0, 0, 0),
    (0, SH_TWO[3], 0, 0),
    (SH_TWO[4], 0, 0, 0),
    (0, 0, SH_THREE[0], 0),
    (0, SH_THREE[1], 0, 0),
    (0, 0, SH_THREE[2], 0),
    (0, 0, 0, SH_THREE[3]),
    (0, SH_THREE[4], 0, 0),
    (0, 0, 0, SH_THREE[5]),
    (0, SH_THREE[6], 0, 0),
)
QUADRATIC = (
    (1, 0, 0, 0, 0, 0, 0),
    (1, 0, 0, 0, 0, 0, 0),
    (1, 0, 0, 0, 0, 0, 0),
    (1, 0, 0, 0, 0, 0, 0),
    (0, 1, 0, 0, 0, 0, 0),
    (0, 0, 1, 0, 0, 0, 0),
    (0, 0, 0, -1, -1, 2, 0),
    (0, 0, 1, 0, 0, 0, 0),
    (0, 0, 0, 1, -1, 0, 0),
    (0, 0, 0, 3, -1, 0, 0),
    (0, 0, 0, 0, 0, 0, 1),
    (0, 0, 0, -1, -1, 4, 0),
    (0, 0, 0, -3, -3, 2, 0),
    (0, 0, 0, -1, -1, 4, 0),
    (0, 0, 0, 1, -1, 0, 0),
    (0, 0, 0, 1, -3, 0, 0),
)


def dot(left, right):
    return lax.dot_general(left, right, (((1,), (0,)), ((), ())), preferred_element_type=F32)


def dot_t(left, right):
    return lax.dot_general(left, right, (((1,), (1,)), ((), ())), preferred_element_type=F32)


def one_hot(rows, index):
    same = rows.astype(jnp.int16) == index.astype(jnp.int16)
    return jnp.where(same, jnp.ones((), BF16), jnp.zeros((), BF16))


def stacked(first, second, right):
    both = dot(jnp.concatenate([first, second], axis=0), right)
    return both[: first.shape[0]] + both[first.shape[0] :]


def iota(shape, axis):
    return lax.broadcasted_iota(jnp.int32, shape, axis)


def split(value, parts):
    out = []
    for _ in range(parts - 1):
        head = value.astype(BF16).astype(F32)
        out.append(head)
        value = value - head
    out.append(value.astype(BF16).astype(F32))
    return out


def column_consts(table, half):
    rows = iota((8, 128), 0)
    out = []
    for col in range(len(table[0])):
        vals = [float(table[8 * half + i][col]) for i in range(8)]
        if not any(vals):
            out.append(None)
            continue
        acc = jnp.zeros((8, 128), F32)
        for i, val in enumerate(vals):
            if val:
                acc = jnp.where(rows == i, val, acc)
        out.append(acc)
    return out


def form(consts, values):
    total = None
    for const, value in zip(consts, values):
        if const is None:
            continue
        term = const if value is None else const * value
        total = term if total is None else total + term
    return total


def basis_consts():
    return [(column_consts(LINEAR, half), column_consts(QUADRATIC, half)) for half in range(2)]


def unit_terms(place, cam):
    offs = [at - centre for at, centre in zip(place, cam)]
    inv = lax.rsqrt(offs[0] * offs[0] + offs[1] * offs[1] + offs[2] * offs[2])
    xpos, ypos, zpos = [off * inv for off in offs]
    return xpos, ypos, zpos, xpos * xpos, ypos * ypos, zpos * zpos, ypos * zpos


def basis_halves(consts, terms):
    xpos, ypos, zpos, xsq, ysq, zsq, yz = terms
    return [
        form(lin, (None, xpos, ypos, zpos)) * form(quad, (None, ypos, zpos, xsq, ysq, zsq, yz))
        for lin, quad in consts
    ]


def repeated(ref, row):
    return jnp.broadcast_to(ref[row : row + 1, :], (8, 128))


def column_sums(blocks):
    rows = iota((8, 128), 0)
    low = rows < 4
    blocks = [
        jnp.where(low, blocks[i], blocks[i + 4])
        + pltpu.roll(jnp.where(low, blocks[i + 4], blocks[i]), 4, 0)
        for i in range(4)
    ]
    for step in (2, 1):
        low = (rows & step) == 0
        blocks = [
            jnp.where(low, blocks[i], blocks[i + step])
            + jnp.where(
                low, pltpu.roll(blocks[i], 8 - step, 0), pltpu.roll(blocks[i + step], step, 0)
            )
            for i in range(step)
        ]
    return blocks[0]


def flipped(value, bits):
    out = jnp.zeros_like(value)
    for i in range(bits):
        out = out | (((value >> i) & 1) << (bits - 1 - i))
    return out


def rank_of(peer):
    return (flipped(peer >> 4, 3) << 4) | (flipped((peer >> 1) & 7, 3) << 1) | (peer & 1)


def slot_index(idx_ref, cnt_ref, low_scr, high_scr):
    order = [int(f"{row:05b}"[::-1], 2) for row in range(32)]
    turned = jnp.concatenate([idx_ref[row : row + 1, :] for row in order], axis=0)
    turned = jnp.transpose(turned.astype(F32)).astype(jnp.int32)
    slots = jnp.concatenate([turned[32 * i : 32 * i + 32] for i in range(4)], axis=1)
    rows, cols = iota((PEERS, PEERS), 0), iota((PEERS, PEERS), 1)
    perm = (rows == 4 * flipped(cols & 31, 5) + (cols >> 5)).astype(F32).astype(BF16)
    counts = jnp.broadcast_to(cnt_ref[...], (8, PEERS)).astype(F32).astype(BF16)
    counts = dot(counts, perm)[0:1].astype(jnp.int32)
    live = iota((CAP, PEERS), 0) < counts
    low_scr[...] = slots & (LOW - 1)
    high_scr[...] = jnp.where(live, slots >> 8, -1)


def peer_blocks(k):
    for part in range(4):
        for group in range(4):
            rank = ((part >> 1) << 3) | (group << 1) | (part & 1)
            yield 32 * part + 8 * group, pl.ds(3 * rank + k, 8, stride=48)


def pair_row(ref, base, pair):
    first = ref[pl.ds(base + 2 * pair, 1), :]
    second = ref[pl.ds(base + 2 * pair + 1, 1), :]
    return jnp.concatenate([first, second], axis=1)


def returned_row(ref, base, pair):
    first = ref[pl.ds(base + pair, 1), :]
    second = ref[pl.ds(base + CAP // 2 + pair, 1), :]
    return jnp.concatenate([first, second], axis=1)


def owner_kernel(
    cam_hbm,
    proj_hbm,
    sh_hbm,
    pos_hbm,
    idx_hbm,
    cnt_hbm,
    out_ref,
    high_scr,
    hot_ref,
    cam_ref,
    proj_ref,
    sh_ref,
    pos_ref,
    idx_ref,
    cnt_ref,
    col_scr,
    low_scr,
    rows_scr,
    sems,
):
    copies = [
        pltpu.make_async_copy(src, dst, sems.at[i])
        for i, (src, dst) in enumerate(
            (
                (idx_hbm, idx_ref),
                (cnt_hbm, cnt_ref),
                (proj_hbm, proj_ref),
                (cam_hbm, cam_ref),
                (pos_hbm, pos_ref),
                (sh_hbm.at[:, pl.ds(0, 4096)], sh_ref.at[:, pl.ds(0, 4096)]),
                (sh_hbm.at[:, pl.ds(4096, 4096)], sh_ref.at[:, pl.ds(4096, 4096)]),
            )
        )
    ]
    for copy in copies:
        copy.start()
    consts = basis_consts()
    for copy in copies[:2]:
        copy.wait()
    slot_index(idx_ref, cnt_ref, low_scr, high_scr)
    low_iota = iota((LOW, 256), 0)
    high_iota = iota((HIGH, 256), 0)

    def table(ref, comps):
        return jnp.concatenate(
            [ref[pl.ds(par, 32 * comps, stride=2), :] for par in range(2)], axis=1
        )

    partial = {}

    def pick(wide, mask, base, comps, pair):
        for comp in range(base, base + comps):
            at = 32 * (comp - base)
            kept = jnp.where(mask, wide[at : at + 32], 0.0)
            kept = (kept[0:8] + kept[8:16]) + (kept[16:24] + kept[24:32])
            for h in range(2):
                partial[comp, 2 * pair + h] = kept[:, 128 * h : 128 * h + 128]
            first = 8 * (pair // 4)
            if all((comp, first + i) in partial for i in range(8)):
                rows_scr[32 * comp + first : 32 * comp + first + 8, :] = column_sums(
                    [partial.pop((comp, first + i)) for i in range(8)]
                )

    def shade(chunk):
        lanes = slice(128 * chunk, 128 * chunk + 128)
        place = [jnp.broadcast_to(pos_ref[i : i + 1, lanes], (8, 128)) for i in range(3)]
        first, second = basis_halves(consts, unit_terms(place, cam))
        for chan in range(3):
            terms = sh_ref[16 * chan : 16 * chan + 8, lanes] * first
            partial["shade", chan, chunk] = (
                terms + sh_ref[16 * chan + 8 : 16 * chan + 16, lanes] * second
            )
            if chunk % 8 == 7:
                at = 64 * chan + chunk - 7
                col_scr[at : at + 8, :] = 0.5 + column_sums(
                    [partial.pop(("shade", chan, chunk - 7 + i)) for i in range(8)]
                )

    def hots(pair):
        hot = one_hot(low_iota, pair_row(low_scr, 0, pair))
        hot_ref[:, 256 * pair : 256 * pair + 256] = hot
        return hot

    def mask(pair):
        return high_iota == pair_row(high_scr, 0, pair)

    copies[2].wait()
    rows = split(table(proj_ref, 6)[32 * LANED :], 3)
    size = 192 - 32 * LANED
    exact = size - 32
    rows = jnp.concatenate([rows[0], rows[1], rows[2][:exact]], axis=0).astype(BF16)
    both = 2 * size + exact

    def sum_rows(wide):
        first = wide[:exact] + wide[size : size + exact] + wide[2 * size : both]
        return jnp.concatenate([first, wide[exact:size] + wide[size + exact : 2 * size]], axis=0)

    lanes_of = [(high_scr[8 * b : 8 * b + 8, :] << 1) | (low_scr[8 * b : 8 * b + 8, :] >> 7) for b in range(4)]
    dead = [high_scr[8 * b : 8 * b + 8, :] < 0 for b in range(4)]
    lanes_of = [jnp.where(d, -1, v) for d, v in zip(dead, lanes_of)]
    within = [low_scr[8 * b : 8 * b + 8, :] & 127 for b in range(4)]
    found = [[jnp.zeros((8, 128), F32) for _ in range(4)] for _ in range(LANED)]

    def lane_gather(block):
        mine = [v == block for v in lanes_of]
        for comp in range(LANED):
            at = 64 * comp + block
            row = jnp.broadcast_to(proj_ref[at : at + 1, :], (8, 128))
            for b in range(4):
                value = jnp.take_along_axis(row, within[b], axis=1)
                found[comp][b] = jnp.where(mine[b], value, found[comp][b])

    cam, chunk = None, 0
    for pair in range(EARLY):
        hot = hots(pair)
        pick(sum_rows(dot(rows, hot)), mask(pair), LANED, 6 - LANED, pair)
        for block in range(4 * pair, 4 * pair + 4):
            lane_gather(block)
        if pair == ALONE - 1:
            for copy in copies[3:6]:
                copy.wait()
            cam = [jnp.broadcast_to(cam_ref[0:1, i : i + 1], (8, 128)) for i in range(3)]
        if pair >= ALONE:
            for _ in range(-(-64 // (EARLY - ALONE))):
                if chunk == 32:
                    copies[6].wait()
                if chunk < 64:
                    shade(chunk)
                    chunk += 1
    tints = jnp.concatenate(split(table(col_scr, 3), 2), axis=0).astype(BF16)
    everything = jnp.concatenate([rows, tints], axis=0)
    for pair in range(EARLY, CAP // 2):
        wide = dot(everything, hots(pair))
        pick(sum_rows(wide), mask(pair), LANED, 6 - LANED, pair)
        pick(wide[both : both + 96] + wide[both + 96 :], mask(pair), 6, 3, pair)
        for block in range(4 * pair, 4 * pair + 4):
            lane_gather(block)
    for pair in range(EARLY):
        wide = dot(tints, hot_ref[:, 256 * pair : 256 * pair + 256])
        pick(wide[:96] + wide[96:], mask(pair), 6, 3, pair)

    for comp in range(LANED):
        for b in range(4):
            rows_scr[32 * comp + 8 * b : 32 * comp + 8 * b + 8, :] = found[comp][b]
    rows_scr[32 * COMPS :, :] = jnp.zeros((96, 128), F32)
    for k in range(3):
        turned = jnp.transpose(rows_scr[128 * k : 128 * k + 128, :])
        for at, rows in peer_blocks(k):
            out_ref[rows, :] = turned[at : at + 8]


def render_kernel(
    xy_ref, len_ref, recv_ref, list_ref, grad_ref, out_ref, table_scr, coef_scr, right_scr, sums_scr
):
    for k in range(3):
        table_scr[128 * k : 128 * k + 128, :] = jnp.transpose(
            recv_ref[pl.ds(k, PEERS, stride=3), :]
        )

    slots = jnp.concatenate(
        [list_ref[t : t + 1, 128 * h : 128 * h + 128] for t in range(TILES) for h in range(2)],
        axis=0,
    )
    peer, place = rank_of(slots >> 5), slots & (CAP - 1)
    row_iota = iota((8, 128), 0)

    def by_tile(ref, row):
        out = jnp.zeros((8, 128), jnp.int32)
        for t in range(TILES):
            out = jnp.where(
                row_iota >> 1 == t, jnp.broadcast_to(ref[row : row + 1, t : t + 1], (8, 128)), out
            )
        return out

    centre_x = (by_tile(xy_ref, 0).astype(F32) * 16.0 + 8.0) / 128.0
    centre_y = (by_tile(xy_ref, 1).astype(F32) * 16.0 + 8.0) / 128.0
    inside = (row_iota & 1) * 128 + iota((8, 128), 1) < by_tile(len_ref, 0)

    vals = [jnp.zeros((8, 128), F32) for _ in range(COMPS)]
    for q in range(CAP):
        mine = place == q
        for c in range(COMPS):
            row = jnp.broadcast_to(table_scr[32 * c + q : 32 * c + q + 1, :], (8, 128))
            vals[c] = jnp.where(mine, jnp.take_along_axis(row, peer, axis=1), vals[c])

    mean_x, mean_y, ca, cb, cc, opac = vals[:6]
    xrel, yrel = mean_x - centre_x, mean_y - centre_y
    shown = opac > 0.0
    lead_x = ca * xrel + cb * yrel
    lead_y = cc * yrel + cb * xrel
    const = -0.5 * (xrel * lead_x + yrel * lead_y) + jnp.log(jnp.where(shown, opac, 1.0))
    const = jnp.where(shown & inside, const, NOTHING)
    for i, value in enumerate((const, lead_x, lead_y, -0.5 * ca, -0.5 * cc, -cb)):
        coef_scr[8 * i : 8 * i + 8, :] = LOG2E * value
    tint = [split(v, 3) for v in vals[6:9]]
    for block, (one, two) in enumerate(((0, 0), (1, 0), (2, 1))):
        for c in range(3):
            right_scr[64 * block + 8 * c : 64 * block + 8 * c + 8, :] = tint[c][one]
            right_scr[64 * block + 24 + 8 * c : 64 * block + 32 + 8 * c, :] = tint[c][two]
        right_scr[64 * block + 48 : 64 * block + 64, :] = jnp.zeros((16, 128), F32)
    right_scr[192:256, :] = jnp.zeros((64, 128), F32)

    blank = jnp.zeros((2, 256), F32)
    blocks, sides = [], []
    for tile in range(TILES):
        grads = jnp.concatenate(
            [
                jnp.concatenate(
                    [grad_ref[8 * c + 2 * tile + h : 8 * c + 2 * tile + h + 1, :] for h in range(2)],
                    axis=1,
                )
                for c in range(3)
            ],
            axis=0,
        )
        g0, g1, g2 = split(grads, 3)
        blocks += [g0, g1, blank, g0, g2, blank, g0, g1, blank, jnp.zeros((8, 256), F32)]
        zero5 = jnp.zeros((5, 256), F32)
        sides.append(jnp.concatenate([g0, zero5, g1, zero5], axis=0).astype(BF16))
    turned = jnp.transpose(jnp.concatenate(blocks, axis=0)).astype(BF16)

    column = (iota((16, DEPTH), 0).astype(F32) - 7.5) / 128.0
    before = (iota((DEPTH, DEPTH), 0) < iota((DEPTH, DEPTH), 1)).astype(F32).astype(BF16)
    after = (iota((DEPTH, DEPTH), 0) > iota((DEPTH, DEPTH), 1)).astype(F32).astype(BF16)

    def both(ref, tile):
        return jnp.concatenate(
            [ref[pl.ds(2 * tile + h, 32, stride=8), :] for h in range(2)], axis=1
        ).astype(BF16)

    side = [column[8 * g : 8 * g + 8, :128] for g in range(2)]

    def exponents(tile):
        halves = []
        for h in range(2):
            at = 2 * tile + h
            rows = [
                jnp.broadcast_to(coef_scr[8 * i + at : 8 * i + at + 1, :], (8, 128))
                for i in range(6)
            ]
            along = [rows[0] + u * (rows[1] + u * rows[3]) for u in side]
            across = [rows[2] + u * rows[5] for u in side]
            blocks = []
            for i in range(16):
                vpos = (i - 7.5) / 128.0
                bend = vpos * rows[4]
                blocks += [along[g] + vpos * (across[g] + bend) for g in range(2)]
            halves.append(jnp.concatenate(blocks, axis=0))
        return jnp.concatenate(halves, axis=1)

    def front(tile):
        alpha = jnp.exp2(exponents(tile))
        logs = jnp.log(1.0 - alpha)
        l0 = logs.astype(BF16)
        return alpha, l0, (logs - l0.astype(F32)).astype(BF16)

    def middle(tile, alpha, l0, l1):
        weight = alpha * jnp.exp(stacked(l0, l1, before))
        flow = dot(turned[:, 32 * tile : 32 * tile + 32], both(right_scr, tile)) * weight
        s0 = flow.astype(BF16)
        return weight, flow, s0, (flow - s0.astype(F32)).astype(BF16)

    def back(tile, alpha, weight, flow, s0, s1):
        power = flow - stacked(s0, s1, after) * (alpha / (1.0 - alpha))
        w0 = weight.astype(BF16)
        w1 = (weight - w0.astype(F32)).astype(BF16)
        colours = dot(sides[tile], w0)
        colours = colours[0:8] + colours[8:16] + dot(sides[tile], w1)[0:8]

        plain = linear = square = None
        for i in range(8):
            vpos = (7.5 - i) / 128.0
            top, bottom = power[16 * i : 16 * i + 16], power[240 - 16 * i : 256 - 16 * i]
            total, slope = top + bottom, (bottom - top) * vpos
            curve = total * (vpos * vpos)
            plain = total if plain is None else plain + total
            linear = slope if linear is None else linear + slope
            square = curve if square is None else square + curve
        sums = [
            plain,
            plain * column,
            linear,
            plain * (column * column),
            square,
            linear * column,
        ]
        rows = [jnp.sum(v, axis=0, keepdims=True) for v in sums]
        rows += [colours[i : i + 1] for i in range(3)]
        for i, row in enumerate(rows):
            for h in range(2):
                sums_scr[8 * i + 2 * tile + h : 8 * i + 2 * tile + h + 1, :] = row[
                    :, 128 * h : 128 * h + 128
                ]

    for first in range(0, TILES, 2):
        group = (first, first + 1)
        fronts = [front(tile) for tile in group]
        middles = [middle(tile, *fronts[tile - first]) for tile in group]
        for tile in group:
            back(tile, fronts[tile - first][0], *middles[tile - first])

    m0, mu, mv, muu, mvv, muv, red, green, blue = [sums_scr[8 * i : 8 * i + 8, :] for i in range(9)]
    grads = [
        ca * mu + cb * mv - lead_x * m0,
        cc * mv + cb * mu - lead_y * m0,
        -0.5 * (muu - 2.0 * xrel * mu + xrel * xrel * m0),
        -(muv - yrel * mu - xrel * mv + xrel * yrel * m0),
        -0.5 * (mvv - 2.0 * yrel * mv + yrel * yrel * m0),
        jnp.where(shown, m0 / jnp.where(shown, opac, 1.0), 0.0),
        red,
        green,
        blue,
    ]
    grads = [split(grad, 2) for grad in grads]
    column_iota, place_iota = iota((2 * PEERS, 128), 0), iota((CAP // 2, 128), 0)
    column_of, row_of = peer + PEERS * (place & 1), place >> 1
    hots, wides = [], []
    for r in range(8):
        hots.append(one_hot(column_iota, column_of[r : r + 1]))
        mine = place_iota == row_of[r : r + 1]
        wides.append(
            jnp.concatenate(
                [
                    jnp.where(mine, grads[c][part][r : r + 1], 0.0)
                    for part in range(2)
                    for c in range(COMPS)
                ],
                axis=0,
            ).astype(BF16)
        )
    total = dot_t(jnp.concatenate(wides, axis=1), jnp.concatenate(hots, axis=1))
    half = 16 * COMPS
    total = total[:half] + total[half:]
    total = jnp.concatenate(
        [
            total[16 * c : 16 * c + 16, PEERS * bit : PEERS * bit + PEERS]
            for c in range(COMPS)
            for bit in range(2)
        ]
        + [jnp.zeros((96, 128), F32)],
        axis=0,
    )
    for k in range(3):
        out_ref[pl.ds(k, PEERS, stride=3), :] = jnp.transpose(total[128 * k : 128 * k + 128])


def sum_slots(comps, back_ref, high_ref, hot_ref, rows_scr):
    for k in sorted({comp // 4 for comp in comps}):
        block = jnp.concatenate([back_ref[rows, :] for _, rows in peer_blocks(k)], axis=0)
        rows_scr[128 * k : 128 * k + 128, :] = jnp.transpose(block)
    high_iota = iota((HIGH, 256), 0)
    total = None
    for step in range(4):
        wides = []
        for pair in range(4 * step, 4 * step + 4):
            mask = high_iota == pair_row(high_ref, 0, pair)
            both = [split(returned_row(rows_scr, 32 * comp, pair), 2) for comp in comps]
            wides.append(
                jnp.concatenate(
                    [jnp.where(mask, b[part], 0.0) for part in range(2) for b in both], axis=0
                ).astype(BF16)
            )
        term = dot_t(
            jnp.concatenate(wides, axis=1), hot_ref[:, 1024 * step : 1024 * step + 1024]
        )
        total = term if total is None else total + term
    size = 32 * len(comps)
    return total[:size] + total[size:]


def sum_kernel(cam_ref, back_ref, high_ref, hot_ref, out_ref, col_ref, rows_scr):
    total = sum_slots(range(COMPS), back_ref, high_ref, hot_ref, rows_scr)
    for par in range(2):
        out_ref[pl.ds(par, 192, stride=2), :] = total[:192, 128 * par : 128 * par + 128]
        for share in range(4):
            for chan in range(3):
                first = 192 + 32 * chan + 8 * share
                col_ref[pl.ds(PACK * share + 16 * chan + par, 8, stride=2), :] = total[
                    first : first + 8, 128 * par : 128 * par + 128
                ]
    lanes = iota((8, 128), 1)
    row = jnp.zeros((8, 128), F32)
    for i in range(3):
        row = jnp.where(lanes == i, jnp.broadcast_to(cam_ref[0:1, i : i + 1], (8, 128)), row)
    for share in range(4):
        col_ref[PACK * share + 48 : PACK * share + 56, :] = jnp.where(
            lanes == 3, float(share), row
        )


def coeff_kernel(col_ref, pos_ref, rows_ref, out_hbm, rows_hbm, out_scr, unit_scr, sems):
    keep = pltpu.make_async_copy(rows_ref, rows_hbm, sems.at[4])
    keep.start()
    consts = basis_consts()
    share = jnp.max(col_ref[48:49, 3:4]).astype(jnp.int32)
    for i in range(3):
        for at in range(16):
            lanes = pl.ds(pl.multiple_of(share * 2048 + at * 128, 128), 128)
            unit_scr[16 * i + at : 16 * i + at + 1, :] = pos_ref[i : i + 1, lanes]
    place = [unit_scr[16 * i : 16 * i + 16, :] for i in range(3)]
    for image in range(4):
        row = col_ref[PACK * image + 48 : PACK * image + 49, :]
        cam = [jnp.broadcast_to(row[:, i : i + 1], (16, 128)) for i in range(3)]
        for i, term in enumerate(unit_terms(place, cam)):
            at = 112 * image + 16 * i
            unit_scr[at : at + 16, :] = term

    def chunk(step):
        totals = [[None, None] for _ in range(3)]
        for image in range(4):
            halves = basis_halves(
                consts, [repeated(unit_scr, 112 * image + 16 * i + step) for i in range(7)]
            )
            for chan in range(3):
                grad = repeated(col_ref, PACK * image + 16 * chan + step)
                for half in range(2):
                    term = grad * halves[half]
                    old = totals[chan][half]
                    totals[chan][half] = term if old is None else old + term
        for chan in range(3):
            for half in range(2):
                at = 16 * chan + 8 * half
                out_scr[at : at + 8, 128 * step : 128 * step + 128] = totals[chan][half]

    copies = []
    for piece in range(4):
        for step in range(4 * piece, 4 * piece + 4):
            chunk(step)
        lanes = pl.ds(512 * piece, 512)
        copies.append(
            pltpu.make_async_copy(out_scr.at[:, lanes], out_hbm.at[:, lanes], sems.at[piece])
        )
        copies[-1].start()
    keep.wait()
    for copy in copies:
        copy.wait()


VMEM = pl.BlockSpec(memory_space=pltpu.VMEM)
HBM = pl.BlockSpec(memory_space=pltpu.HBM)
PARAMS = pltpu.CompilerParams(vmem_limit_bytes=40 * 1024 * 1024)


def shape(*dims):
    return jax.ShapeDtypeStruct(dims, F32)


def in_hbm(array):
    return pltpu.with_memory_space_constraint(array, pltpu.HBM)


def owner(camera, proj, coeffs, positions, index, count):
    return pl.pallas_call(
        owner_kernel,
        out_shape=(
            shape(384, 128),
            jax.ShapeDtypeStruct((CAP, PEERS), jnp.int32),
            jax.ShapeDtypeStruct((LOW, CAP * PEERS), BF16),
        ),
        in_specs=[HBM] * 6,
        out_specs=[VMEM] * 3,
        scratch_shapes=[
            pltpu.VMEM((1, 3), F32),
            pltpu.VMEM((384, 128), F32),
            pltpu.VMEM((48, 8192), F32),
            pltpu.VMEM((3, 8192), F32),
            pltpu.VMEM((CAP, PEERS), jnp.int32),
            pltpu.VMEM((1, PEERS), jnp.int32),
            pltpu.VMEM((192, 128), F32),
            pltpu.VMEM((CAP, PEERS), jnp.int32),
            pltpu.VMEM((384, 128), F32),
            pltpu.SemaphoreType.DMA((7,)),
        ],
        compiler_params=PARAMS,
        name="owner_rows",
    )(*[in_hbm(x) for x in (camera, proj, coeffs, positions, index, count)])


def render(tile_xy, tile_len, received, tile_list, pixel_grad):
    return pl.pallas_call(
        render_kernel,
        out_shape=shape(384, 128),
        in_specs=[VMEM] * 5,
        out_specs=VMEM,
        scratch_shapes=[
            pltpu.VMEM((384, 128), F32),
            pltpu.VMEM((48, 128), F32),
            pltpu.VMEM((256, 128), F32),
            pltpu.VMEM((72, 128), F32),
        ],
        compiler_params=PARAMS,
        name="render_tiles",
    )(tile_xy, tile_len, received, tile_list, pixel_grad)


def sum_returned(camera, returned, high, low_hot):
    return pl.pallas_call(
        sum_kernel,
        out_shape=(shape(384, 128), shape(4 * PACK, 128)),
        in_specs=[VMEM] * 4,
        out_specs=[VMEM] * 2,
        scratch_shapes=[pltpu.VMEM((384, 128), F32)],
        compiler_params=PARAMS,
        name="owner_sums",
    )(camera, returned, high, low_hot)


def coefficients(colours, positions, rows):
    return pl.pallas_call(
        coeff_kernel,
        out_shape=(shape(48, 2048), shape(384, 128)),
        in_specs=[VMEM] * 3,
        out_specs=[HBM] * 2,
        scratch_shapes=[
            pltpu.VMEM((48, 2048), F32),
            pltpu.VMEM((448, 128), F32),
            pltpu.SemaphoreType.DMA((5,)),
        ],
        compiler_params=PARAMS,
        name="coeff_grads",
    )(colours, positions, rows)


def exchange(rows, axis, peers):
    sent = rows.reshape(peers, 1, -1)
    got = lax.all_to_all(sent, axis, split_axis=0, concat_axis=0, tiled=True)
    return got.reshape(rows.shape)


def on_device(
    proj,
    sh_coeffs,
    positions,
    camera,
    send_index,
    send_count,
    tile_xy,
    tile_list,
    tile_len,
    pixel_grad,
):
    index = send_index.reshape(CAP, PEERS)
    outgoing, high, low_hot = owner(
        camera, proj.reshape(384, 128), sh_coeffs, positions, index, send_count
    )
    received = exchange(outgoing, ORDER, PEERS)
    slot_grads = render(
        tile_xy[0], tile_len, received, tile_list[0], pixel_grad.reshape(24, 128)
    )
    returned = exchange(slot_grads, ORDER, PEERS)
    grad_rows, colours = sum_returned(camera, returned, high, low_hot)
    colours = exchange(colours, "img", 4)
    grad_sh, grad_rows = coefficients(colours, positions, grad_rows)
    return (grad_rows.reshape(proj.shape), grad_sh)


def solution(mesh):
    bits = jax.sharding.Mesh(mesh.devices.reshape((2,) * len(CELL) + (-1,)), CELL + ("img",))
    return jax.shard_map(
        on_device,
        mesh=bits,
        in_specs=(
            P("img", None, CELL),
            P(None, CELL),
            P(None, CELL),
            P("img", None),
            P("img", CELL),
            P("img", CELL),
            P("img", None, CELL),
            P("img", CELL, None),
            P("img", CELL),
            P("img", None, CELL),
        ),
        out_specs=(P("img", None, CELL), P(None, CELL + ("img",))),
        check_vma=False,
    )
```

```python
import functools

import jax
import jax.numpy as jnp
from jax import lax
from jax.experimental import pallas as pl
from jax.experimental.pallas import tpu as pltpu
from jax.sharding import PartitionSpec as P

SH_ZERO = 0.28209479177387814
SH_ONE = 0.4886025119029199
SH_TWO = (
    1.0925484305920792,
    -1.0925484305920792,
    0.31539156525252005,
    -1.0925484305920792,
    0.5462742152960396,
)
SH_THREE = (
    -0.5900435899266435,
    2.890611442640554,
    -0.4570457994644658,
    0.3731763325901154,
    -0.4570457994644658,
    1.445305721320277,
    -0.5900435899266435,
)

F32 = jnp.float32
BF16 = jnp.bfloat16
PEERS = 128
CAP = 32
COMPS = 9
TILES = 4
DEPTH = 256
LOW = 256
HIGH = 32
PACK = 56
NOTHING = -1.0e4
CELL = ("y2", "y1", "y0", "z2", "z1", "z0", "core")
ORDER = ("y0", "y1", "z0", "y2", "z1", "z2", "core")
PEER_ROWS = tuple(
    ((n >> 4) & 1) << 2 | ((n >> 3) & 1) << 3 | ((n >> 2) & 1) << 4 | ((n >> 1) & 1) | (n & 1) << 1
    for n in range(32)
)
LOG2E = 1.4426950408889634
EARLY = 6
LANED = 2
ALONE = 3

LINEAR = (
    (SH_ZERO, 0, 0, 0),
    (0, 0, -SH_ONE, 0),
    (0, 0, 0, SH_ONE),
    (0, -SH_ONE, 0, 0),
    (0, SH_TWO[0], 0, 0),
    (0, 0, SH_TWO[1], 0),
    (SH_TWO[2], 0, 0, 0),
    (0, SH_TWO[3], 0, 0),
    (SH_TWO[4], 0, 0, 0),
    (0, 0, SH_THREE[0], 0),
    (0, SH_THREE[1], 0, 0),
    (0, 0, SH_THREE[2], 0),
    (0, 0, 0, SH_THREE[3]),
    (0, SH_THREE[4], 0, 0),
    (0, 0, 0, SH_THREE[5]),
    (0, SH_THREE[6], 0, 0),
)
QUADRATIC = (
    (1, 0, 0, 0, 0, 0, 0),
    (1, 0, 0, 0, 0, 0, 0),
    (1, 0, 0, 0, 0, 0, 0),
    (1, 0, 0, 0, 0, 0, 0),
    (0, 1, 0, 0, 0, 0, 0),
    (0, 0, 1, 0, 0, 0, 0),
    (0, 0, 0, -1, -1, 2, 0),
    (0, 0, 1, 0, 0, 0, 0),
    (0, 0, 0, 1, -1, 0, 0),
    (0, 0, 0, 3, -1, 0, 0),
    (0, 0, 0, 0, 0, 0, 1),
    (0, 0, 0, -1, -1, 4, 0),
    (0, 0, 0, -3, -3, 2, 0),
    (0, 0, 0, -1, -1, 4, 0),
    (0, 0, 0, 1, -1, 0, 0),
    (0, 0, 0, 1, -3, 0, 0),
)


def dot(left, right):
    return lax.dot_general(left, right, (((1,), (0,)), ((), ())), preferred_element_type=F32)


def dot_t(left, right):
    return lax.dot_general(left, right, (((1,), (1,)), ((), ())), preferred_element_type=F32)


def one_hot(rows, index):
    same = rows.astype(jnp.int16) == index.astype(jnp.int16)
    return jnp.where(same, jnp.ones((), BF16), jnp.zeros((), BF16))


def stacked(first, second, right):
    both = dot(jnp.concatenate([first, second], axis=0), right)
    return both[: first.shape[0]] + both[first.shape[0] :]


def iota(shape, axis):
    return lax.broadcasted_iota(jnp.int32, shape, axis)


def split(value, parts):
    out = []
    for _ in range(parts - 1):
        head = value.astype(BF16).astype(F32)
        out.append(head)
        value = value - head
    out.append(value.astype(BF16).astype(F32))
    return out


def column_consts(table, half):
    rows = iota((8, 128), 0)
    out = []
    for col in range(len(table[0])):
        vals = [float(table[8 * half + i][col]) for i in range(8)]
        if not any(vals):
            out.append(None)
            continue
        acc = jnp.zeros((8, 128), F32)
        for i, val in enumerate(vals):
            if val:
                acc = jnp.where(rows == i, val, acc)
        out.append(acc)
    return out


def form(consts, values):
    total = None
    for const, value in zip(consts, values):
        if const is None:
            continue
        term = const if value is None else const * value
        total = term if total is None else total + term
    return total


def basis_consts():
    return [(column_consts(LINEAR, half), column_consts(QUADRATIC, half)) for half in range(2)]


def unit_terms(place, cam):
    offs = [at - centre for at, centre in zip(place, cam)]
    inv = lax.rsqrt(offs[0] * offs[0] + offs[1] * offs[1] + offs[2] * offs[2])
    xpos, ypos, zpos = [off * inv for off in offs]
    return xpos, ypos, zpos, xpos * xpos, ypos * ypos, zpos * zpos, ypos * zpos


def basis_halves(consts, terms):
    xpos, ypos, zpos, xsq, ysq, zsq, yz = terms
    return [
        form(lin, (None, xpos, ypos, zpos)) * form(quad, (None, ypos, zpos, xsq, ysq, zsq, yz))
        for lin, quad in consts
    ]


def repeated(ref, row):
    return jnp.broadcast_to(ref[row : row + 1, :], (8, 128))


def column_sums(blocks):
    rows = iota((8, 128), 0)
    low = rows < 4
    blocks = [
        jnp.where(low, blocks[i], blocks[i + 4])
        + pltpu.roll(jnp.where(low, blocks[i + 4], blocks[i]), 4, 0)
        for i in range(4)
    ]
    for step in (2, 1):
        low = (rows & step) == 0
        blocks = [
            jnp.where(low, blocks[i], blocks[i + step])
            + jnp.where(
                low, pltpu.roll(blocks[i], 8 - step, 0), pltpu.roll(blocks[i + step], step, 0)
            )
            for i in range(step)
        ]
    return blocks[0]


def flipped(value, bits):
    out = jnp.zeros_like(value)
    for i in range(bits):
        out = out | (((value >> i) & 1) << (bits - 1 - i))
    return out


def rank_of(peer):
    out = jnp.zeros_like(peer)
    for place, name in enumerate(ORDER):
        bit = len(CELL) - 1 - CELL.index(name)
        out = out | (((peer >> bit) & 1) << (len(ORDER) - 1 - place))
    return out


def peer_of(place):
    return (flipped(place >> 2, 3) << 2) | flipped(place & 3, 2)


def slot_index(idx_ref, cnt_ref, low_scr, high_scr):
    rows = [idx_ref[row : row + 1, :] for row in PEER_ROWS]
    turned = jnp.concatenate(rows, axis=0)
    turned = jnp.transpose(turned.astype(F32)).astype(jnp.int32)
    slots = jnp.concatenate([turned[32 * i : 32 * i + 32] for i in range(4)], axis=1)
    rows, cols = iota((PEERS, PEERS), 0), iota((PEERS, PEERS), 1)
    perm = (rows == 4 * peer_of(cols & 31) + (cols >> 5)).astype(F32).astype(BF16)
    counts = jnp.broadcast_to(cnt_ref[...], (8, PEERS)).astype(F32).astype(BF16)
    counts = dot(counts, perm)[0:1].astype(jnp.int32)
    live = iota((CAP, PEERS), 0) < counts
    low_scr[...] = slots & (LOW - 1)
    high_scr[...] = jnp.where(live, slots >> 8, -1)


def peer_blocks(k):
    for part in range(4):
        for group in range(4):
            rank = (group << 5) | ((part >> 1) << 4) | (part & 1)
            yield 32 * part + 8 * group, pl.ds(3 * rank + k, 8, stride=6)


def pair_row(ref, base, pair):
    first = ref[pl.ds(base + 2 * pair, 1), :]
    second = ref[pl.ds(base + 2 * pair + 1, 1), :]
    return jnp.concatenate([first, second], axis=1)


def returned_row(ref, base, pair):
    first = ref[pl.ds(base + pair, 1), :]
    second = ref[pl.ds(base + CAP // 2 + pair, 1), :]
    return jnp.concatenate([first, second], axis=1)


def owner_kernel(
    cam_hbm,
    proj_hbm,
    sh_hbm,
    pos_hbm,
    idx_hbm,
    cnt_hbm,
    out_ref,
    high_scr,
    hot_ref,
    cam_ref,
    proj_ref,
    sh_ref,
    pos_ref,
    idx_ref,
    cnt_ref,
    col_scr,
    low_scr,
    rows_scr,
    sems,
):
    copies = [
        pltpu.make_async_copy(src, dst, sems.at[i])
        for i, (src, dst) in enumerate(
            (
                (idx_hbm, idx_ref),
                (cnt_hbm, cnt_ref),
                (proj_hbm, proj_ref),
                (cam_hbm, cam_ref),
                (pos_hbm, pos_ref),
                (sh_hbm.at[:, pl.ds(0, 4096)], sh_ref.at[:, pl.ds(0, 4096)]),
                (sh_hbm.at[:, pl.ds(4096, 4096)], sh_ref.at[:, pl.ds(4096, 4096)]),
            )
        )
    ]
    for copy in copies:
        copy.start()
    consts = basis_consts()
    for copy in copies[:2]:
        copy.wait()
    slot_index(idx_ref, cnt_ref, low_scr, high_scr)
    low_iota = iota((LOW, 256), 0)
    high_iota = iota((HIGH, 256), 0)

    def table(ref, comps):
        return jnp.concatenate(
            [ref[pl.ds(par, 32 * comps, stride=2), :] for par in range(2)], axis=1
        )

    partial = {}

    def pick(wide, mask, base, comps, pair):
        for comp in range(base, base + comps):
            at = 32 * (comp - base)
            kept = jnp.where(mask, wide[at : at + 32], 0.0)
            kept = (kept[0:8] + kept[8:16]) + (kept[16:24] + kept[24:32])
            for h in range(2):
                partial[comp, 2 * pair + h] = kept[:, 128 * h : 128 * h + 128]
            first = 8 * (pair // 4)
            if all((comp, first + i) in partial for i in range(8)):
                rows_scr[32 * comp + first : 32 * comp + first + 8, :] = column_sums(
                    [partial.pop((comp, first + i)) for i in range(8)]
                )

    def shade(chunk):
        lanes = slice(128 * chunk, 128 * chunk + 128)
        place = [jnp.broadcast_to(pos_ref[i : i + 1, lanes], (8, 128)) for i in range(3)]
        first, second = basis_halves(consts, unit_terms(place, cam))
        for chan in range(3):
            terms = sh_ref[16 * chan : 16 * chan + 8, lanes] * first
            partial["shade", chan, chunk] = (
                terms + sh_ref[16 * chan + 8 : 16 * chan + 16, lanes] * second
            )
            if chunk % 8 == 7:
                at = 64 * chan + chunk - 7
                col_scr[at : at + 8, :] = 0.5 + column_sums(
                    [partial.pop(("shade", chan, chunk - 7 + i)) for i in range(8)]
                )

    def hots(pair):
        hot = one_hot(low_iota, pair_row(low_scr, 0, pair))
        hot_ref[:, 256 * pair : 256 * pair + 256] = hot
        return hot

    def mask(pair):
        return high_iota == pair_row(high_scr, 0, pair)

    copies[2].wait()
    rows = split(table(proj_ref, 6)[32 * LANED :], 3)
    size = 192 - 32 * LANED
    exact = size - 32
    rows = jnp.concatenate([rows[0], rows[1], rows[2][:exact]], axis=0).astype(BF16)
    both = 2 * size + exact

    def sum_rows(wide):
        first = wide[:exact] + wide[size : size + exact] + wide[2 * size : both]
        return jnp.concatenate([first, wide[exact:size] + wide[size + exact : 2 * size]], axis=0)

    lanes_of = [(high_scr[8 * b : 8 * b + 8, :] << 1) | (low_scr[8 * b : 8 * b + 8, :] >> 7) for b in range(4)]
    dead = [high_scr[8 * b : 8 * b + 8, :] < 0 for b in range(4)]
    lanes_of = [jnp.where(d, -1, v) for d, v in zip(dead, lanes_of)]
    within = [low_scr[8 * b : 8 * b + 8, :] & 127 for b in range(4)]
    found = [[jnp.zeros((8, 128), F32) for _ in range(4)] for _ in range(LANED)]

    def lane_gather(block):
        mine = [v == block for v in lanes_of]
        for comp in range(LANED):
            at = 64 * comp + block
            row = jnp.broadcast_to(proj_ref[at : at + 1, :], (8, 128))
            for b in range(4):
                value = jnp.take_along_axis(row, within[b], axis=1)
                found[comp][b] = jnp.where(mine[b], value, found[comp][b])

    cam, chunk = None, 0
    for pair in range(EARLY):
        hot = hots(pair)
        pick(sum_rows(dot(rows, hot)), mask(pair), LANED, 6 - LANED, pair)
        for block in range(4 * pair, 4 * pair + 4):
            lane_gather(block)
        if pair == ALONE - 1:
            for copy in copies[3:6]:
                copy.wait()
            cam = [jnp.broadcast_to(cam_ref[0:1, i : i + 1], (8, 128)) for i in range(3)]
        if pair >= ALONE:
            for _ in range(-(-64 // (EARLY - ALONE))):
                if chunk == 32:
                    copies[6].wait()
                if chunk < 64:
                    shade(chunk)
                    chunk += 1
    tints = jnp.concatenate(split(table(col_scr, 3), 2), axis=0).astype(BF16)
    everything = jnp.concatenate([rows, tints], axis=0)
    for pair in range(EARLY, CAP // 2):
        wide = dot(everything, hots(pair))
        pick(sum_rows(wide), mask(pair), LANED, 6 - LANED, pair)
        pick(wide[both : both + 96] + wide[both + 96 :], mask(pair), 6, 3, pair)
        for block in range(4 * pair, 4 * pair + 4):
            lane_gather(block)
    for pair in range(EARLY):
        wide = dot(tints, hot_ref[:, 256 * pair : 256 * pair + 256])
        pick(wide[:96] + wide[96:], mask(pair), 6, 3, pair)

    for comp in range(LANED):
        for b in range(4):
            rows_scr[32 * comp + 8 * b : 32 * comp + 8 * b + 8, :] = found[comp][b]
    rows_scr[32 * COMPS :, :] = jnp.zeros((96, 128), F32)
    for k in range(3):
        turned = jnp.transpose(rows_scr[128 * k : 128 * k + 128, :])
        for at, rows in peer_blocks(k):
            out_ref[rows, :] = turned[at : at + 8]


def render_kernel(
    xy_ref, len_ref, recv_ref, list_ref, grad_ref, out_ref, table_scr, coef_scr, right_scr, sums_scr
):
    for k in range(3):
        table_scr[128 * k : 128 * k + 128, :] = jnp.transpose(
            recv_ref[pl.ds(k, PEERS, stride=3), :]
        )

    slots = jnp.concatenate(
        [list_ref[t : t + 1, 128 * h : 128 * h + 128] for t in range(TILES) for h in range(2)],
        axis=0,
    )
    peer, place = rank_of(slots >> 5), slots & (CAP - 1)
    row_iota = iota((8, 128), 0)

    def by_tile(ref, row):
        out = jnp.zeros((8, 128), jnp.int32)
        for t in range(TILES):
            out = jnp.where(
                row_iota >> 1 == t, jnp.broadcast_to(ref[row : row + 1, t : t + 1], (8, 128)), out
            )
        return out

    centre_x = (by_tile(xy_ref, 0).astype(F32) * 16.0 + 8.0) / 128.0
    centre_y = (by_tile(xy_ref, 1).astype(F32) * 16.0 + 8.0) / 128.0
    inside = (row_iota & 1) * 128 + iota((8, 128), 1) < by_tile(len_ref, 0)

    vals = [jnp.zeros((8, 128), F32) for _ in range(COMPS)]
    for q in range(CAP):
        mine = place == q
        for c in range(COMPS):
            row = jnp.broadcast_to(table_scr[32 * c + q : 32 * c + q + 1, :], (8, 128))
            vals[c] = jnp.where(mine, jnp.take_along_axis(row, peer, axis=1), vals[c])

    mean_x, mean_y, ca, cb, cc, opac = vals[:6]
    xrel, yrel = mean_x - centre_x, mean_y - centre_y
    shown = opac > 0.0
    lead_x = ca * xrel + cb * yrel
    lead_y = cc * yrel + cb * xrel
    const = -0.5 * (xrel * lead_x + yrel * lead_y) + jnp.log(jnp.where(shown, opac, 1.0))
    const = jnp.where(shown & inside, const, NOTHING)
    for i, value in enumerate((const, lead_x, lead_y, -0.5 * ca, -0.5 * cc, -cb)):
        coef_scr[8 * i : 8 * i + 8, :] = LOG2E * value
    tint = [split(v, 3) for v in vals[6:9]]
    for block, (one, two) in enumerate(((0, 0), (1, 0), (2, 1))):
        for c in range(3):
            right_scr[64 * block + 8 * c : 64 * block + 8 * c + 8, :] = tint[c][one]
            right_scr[64 * block + 24 + 8 * c : 64 * block + 32 + 8 * c, :] = tint[c][two]
        right_scr[64 * block + 48 : 64 * block + 64, :] = jnp.zeros((16, 128), F32)
    right_scr[192:256, :] = jnp.zeros((64, 128), F32)

    blank = jnp.zeros((2, 256), F32)
    blocks, sides = [], []
    for tile in range(TILES):
        grads = jnp.concatenate(
            [
                jnp.concatenate(
                    [grad_ref[8 * c + 2 * tile + h : 8 * c + 2 * tile + h + 1, :] for h in range(2)],
                    axis=1,
                )
                for c in range(3)
            ],
            axis=0,
        )
        g0, g1, g2 = split(grads, 3)
        blocks += [g0, g1, blank, g0, g2, blank, g0, g1, blank, jnp.zeros((8, 256), F32)]
        zero5 = jnp.zeros((5, 256), F32)
        sides.append(jnp.concatenate([g0, zero5, g1, zero5], axis=0).astype(BF16))
    turned = jnp.transpose(jnp.concatenate(blocks, axis=0)).astype(BF16)

    column = (iota((16, DEPTH), 0).astype(F32) - 7.5) / 128.0
    before = (iota((DEPTH, DEPTH), 0) < iota((DEPTH, DEPTH), 1)).astype(F32).astype(BF16)
    after = (iota((DEPTH, DEPTH), 0) > iota((DEPTH, DEPTH), 1)).astype(F32).astype(BF16)

    def both(ref, tile):
        return jnp.concatenate(
            [ref[pl.ds(2 * tile + h, 32, stride=8), :] for h in range(2)], axis=1
        ).astype(BF16)

    side = [column[8 * g : 8 * g + 8, :128] for g in range(2)]

    def exponents(tile):
        halves = []
        for h in range(2):
            at = 2 * tile + h
            rows = [
                jnp.broadcast_to(coef_scr[8 * i + at : 8 * i + at + 1, :], (8, 128))
                for i in range(6)
            ]
            along = [rows[0] + u * (rows[1] + u * rows[3]) for u in side]
            across = [rows[2] + u * rows[5] for u in side]
            blocks = []
            for i in range(16):
                vpos = (i - 7.5) / 128.0
                bend = vpos * rows[4]
                blocks += [along[g] + vpos * (across[g] + bend) for g in range(2)]
            halves.append(jnp.concatenate(blocks, axis=0))
        return jnp.concatenate(halves, axis=1)

    def front(tile):
        alpha = jnp.exp2(exponents(tile))
        logs = jnp.log(1.0 - alpha)
        l0 = logs.astype(BF16)
        return alpha, l0, (logs - l0.astype(F32)).astype(BF16)

    def middle(tile, alpha, l0, l1):
        weight = alpha * jnp.exp(stacked(l0, l1, before))
        flow = dot(turned[:, 32 * tile : 32 * tile + 32], both(right_scr, tile)) * weight
        s0 = flow.astype(BF16)
        return weight, flow, s0, (flow - s0.astype(F32)).astype(BF16)

    def back(tile, alpha, weight, flow, s0, s1):
        power = flow - stacked(s0, s1, after) * (alpha / (1.0 - alpha))
        w0 = weight.astype(BF16)
        w1 = (weight - w0.astype(F32)).astype(BF16)
        colours = dot(sides[tile], w0)
        colours = colours[0:8] + colours[8:16] + dot(sides[tile], w1)[0:8]

        plain = linear = square = None
        for i in range(8):
            vpos = (7.5 - i) / 128.0
            top, bottom = power[16 * i : 16 * i + 16], power[240 - 16 * i : 256 - 16 * i]
            total, slope = top + bottom, (bottom - top) * vpos
            curve = total * (vpos * vpos)
            plain = total if plain is None else plain + total
            linear = slope if linear is None else linear + slope
            square = curve if square is None else square + curve
        sums = [
            plain,
            plain * column,
            linear,
            plain * (column * column),
            square,
            linear * column,
        ]
        rows = [jnp.sum(v, axis=0, keepdims=True) for v in sums]
        rows += [colours[i : i + 1] for i in range(3)]
        for i, row in enumerate(rows):
            for h in range(2):
                sums_scr[8 * i + 2 * tile + h : 8 * i + 2 * tile + h + 1, :] = row[
                    :, 128 * h : 128 * h + 128
                ]

    for first in range(0, TILES, 2):
        group = (first, first + 1)
        fronts = [front(tile) for tile in group]
        middles = [middle(tile, *fronts[tile - first]) for tile in group]
        for tile in group:
            back(tile, fronts[tile - first][0], *middles[tile - first])

    m0, mu, mv, muu, mvv, muv, red, green, blue = [sums_scr[8 * i : 8 * i + 8, :] for i in range(9)]
    grads = [
        ca * mu + cb * mv - lead_x * m0,
        cc * mv + cb * mu - lead_y * m0,
        -0.5 * (muu - 2.0 * xrel * mu + xrel * xrel * m0),
        -(muv - yrel * mu - xrel * mv + xrel * yrel * m0),
        -0.5 * (mvv - 2.0 * yrel * mv + yrel * yrel * m0),
        jnp.where(shown, m0 / jnp.where(shown, opac, 1.0), 0.0),
        red,
        green,
        blue,
    ]
    grads = [split(grad, 2) for grad in grads]
    column_iota, place_iota = iota((2 * PEERS, 128), 0), iota((CAP // 2, 128), 0)
    column_of, row_of = peer + PEERS * (place & 1), place >> 1
    hots, wides = [], []
    for r in range(8):
        hots.append(one_hot(column_iota, column_of[r : r + 1]))
        mine = place_iota == row_of[r : r + 1]
        wides.append(
            jnp.concatenate(
                [
                    jnp.where(mine, grads[c][part][r : r + 1], 0.0)
                    for part in range(2)
                    for c in range(COMPS)
                ],
                axis=0,
            ).astype(BF16)
        )
    total = dot_t(jnp.concatenate(wides, axis=1), jnp.concatenate(hots, axis=1))
    half = 16 * COMPS
    total = total[:half] + total[half:]
    total = jnp.concatenate(
        [
            total[16 * c : 16 * c + 16, PEERS * bit : PEERS * bit + PEERS]
            for c in range(COMPS)
            for bit in range(2)
        ]
        + [jnp.zeros((96, 128), F32)],
        axis=0,
    )
    for k in range(3):
        out_ref[pl.ds(k, PEERS, stride=3), :] = jnp.transpose(total[128 * k : 128 * k + 128])


def sum_slots(comps, back_ref, high_ref, hot_ref, rows_scr):
    for k in sorted({comp // 4 for comp in comps}):
        block = jnp.concatenate([back_ref[rows, :] for _, rows in peer_blocks(k)], axis=0)
        rows_scr[128 * k : 128 * k + 128, :] = jnp.transpose(block)
    high_iota = iota((HIGH, 256), 0)
    total = None
    for step in range(4):
        wides = []
        for pair in range(4 * step, 4 * step + 4):
            mask = high_iota == pair_row(high_ref, 0, pair)
            both = [split(returned_row(rows_scr, 32 * comp, pair), 2) for comp in comps]
            wides.append(
                jnp.concatenate(
                    [jnp.where(mask, b[part], 0.0) for part in range(2) for b in both], axis=0
                ).astype(BF16)
            )
        term = dot_t(
            jnp.concatenate(wides, axis=1), hot_ref[:, 1024 * step : 1024 * step + 1024]
        )
        total = term if total is None else total + term
    size = 32 * len(comps)
    return total[:size] + total[size:]


def sum_kernel(cam_ref, back_ref, high_ref, hot_ref, out_ref, col_ref, rows_scr):
    total = sum_slots(range(COMPS), back_ref, high_ref, hot_ref, rows_scr)
    for par in range(2):
        out_ref[pl.ds(par, 192, stride=2), :] = total[:192, 128 * par : 128 * par + 128]
        for share in range(4):
            for chan in range(3):
                first = 192 + 32 * chan + 8 * share
                col_ref[pl.ds(PACK * share + 16 * chan + par, 8, stride=2), :] = total[
                    first : first + 8, 128 * par : 128 * par + 128
                ]
    lanes = iota((8, 128), 1)
    row = jnp.zeros((8, 128), F32)
    for i in range(3):
        row = jnp.where(lanes == i, jnp.broadcast_to(cam_ref[0:1, i : i + 1], (8, 128)), row)
    for share in range(4):
        col_ref[PACK * share + 48 : PACK * share + 56, :] = jnp.where(
            lanes == 3, float(share), row
        )


def coeff_kernel(col_ref, pos_ref, rows_ref, out_hbm, rows_hbm, out_scr, unit_scr, sems):
    keep = pltpu.make_async_copy(rows_ref, rows_hbm, sems.at[4])
    keep.start()
    consts = basis_consts()
    share = jnp.max(col_ref[48:49, 3:4]).astype(jnp.int32)
    for i in range(3):
        for at in range(16):
            lanes = pl.ds(pl.multiple_of(share * 2048 + at * 128, 128), 128)
            unit_scr[16 * i + at : 16 * i + at + 1, :] = pos_ref[i : i + 1, lanes]
    place = [unit_scr[16 * i : 16 * i + 16, :] for i in range(3)]
    for image in range(4):
        row = col_ref[PACK * image + 48 : PACK * image + 49, :]
        cam = [jnp.broadcast_to(row[:, i : i + 1], (16, 128)) for i in range(3)]
        for i, term in enumerate(unit_terms(place, cam)):
            at = 112 * image + 16 * i
            unit_scr[at : at + 16, :] = term

    def chunk(step):
        totals = [[None, None] for _ in range(3)]
        for image in range(4):
            halves = basis_halves(
                consts, [repeated(unit_scr, 112 * image + 16 * i + step) for i in range(7)]
            )
            for chan in range(3):
                grad = repeated(col_ref, PACK * image + 16 * chan + step)
                for half in range(2):
                    term = grad * halves[half]
                    old = totals[chan][half]
                    totals[chan][half] = term if old is None else old + term
        for chan in range(3):
            for half in range(2):
                at = 16 * chan + 8 * half
                out_scr[at : at + 8, 128 * step : 128 * step + 128] = totals[chan][half]

    copies = []
    for piece in range(4):
        for step in range(4 * piece, 4 * piece + 4):
            chunk(step)
        lanes = pl.ds(512 * piece, 512)
        copies.append(
            pltpu.make_async_copy(out_scr.at[:, lanes], out_hbm.at[:, lanes], sems.at[piece])
        )
        copies[-1].start()
    keep.wait()
    for copy in copies:
        copy.wait()


VMEM = pl.BlockSpec(memory_space=pltpu.VMEM)
HBM = pl.BlockSpec(memory_space=pltpu.HBM)
PARAMS = pltpu.CompilerParams(vmem_limit_bytes=40 * 1024 * 1024)


def shape(*dims):
    return jax.ShapeDtypeStruct(dims, F32)


def in_hbm(array):
    return pltpu.with_memory_space_constraint(array, pltpu.HBM)


def owner(camera, proj, coeffs, positions, index, count):
    return pl.pallas_call(
        owner_kernel,
        out_shape=(
            shape(384, 128),
            jax.ShapeDtypeStruct((CAP, PEERS), jnp.int32),
            jax.ShapeDtypeStruct((LOW, CAP * PEERS), BF16),
        ),
        in_specs=[HBM] * 6,
        out_specs=[VMEM] * 3,
        scratch_shapes=[
            pltpu.VMEM((1, 3), F32),
            pltpu.VMEM((384, 128), F32),
            pltpu.VMEM((48, 8192), F32),
            pltpu.VMEM((3, 8192), F32),
            pltpu.VMEM((CAP, PEERS), jnp.int32),
            pltpu.VMEM((1, PEERS), jnp.int32),
            pltpu.VMEM((192, 128), F32),
            pltpu.VMEM((CAP, PEERS), jnp.int32),
            pltpu.VMEM((384, 128), F32),
            pltpu.SemaphoreType.DMA((7,)),
        ],
        compiler_params=PARAMS,
        name="owner_rows",
    )(*[in_hbm(x) for x in (camera, proj, coeffs, positions, index, count)])


def render(tile_xy, tile_len, received, tile_list, pixel_grad):
    return pl.pallas_call(
        render_kernel,
        out_shape=shape(384, 128),
        in_specs=[VMEM] * 5,
        out_specs=VMEM,
        scratch_shapes=[
            pltpu.VMEM((384, 128), F32),
            pltpu.VMEM((48, 128), F32),
            pltpu.VMEM((256, 128), F32),
            pltpu.VMEM((72, 128), F32),
        ],
        compiler_params=PARAMS,
        name="render_tiles",
    )(tile_xy, tile_len, received, tile_list, pixel_grad)


def sum_returned(camera, returned, high, low_hot):
    return pl.pallas_call(
        sum_kernel,
        out_shape=(shape(384, 128), shape(4 * PACK, 128)),
        in_specs=[VMEM] * 4,
        out_specs=[VMEM] * 2,
        scratch_shapes=[pltpu.VMEM((384, 128), F32)],
        compiler_params=PARAMS,
        name="owner_sums",
    )(camera, returned, high, low_hot)


def coefficients(colours, positions, rows):
    return pl.pallas_call(
        coeff_kernel,
        out_shape=(shape(48, 2048), shape(384, 128)),
        in_specs=[VMEM] * 3,
        out_specs=[HBM] * 2,
        scratch_shapes=[
            pltpu.VMEM((48, 2048), F32),
            pltpu.VMEM((448, 128), F32),
            pltpu.SemaphoreType.DMA((5,)),
        ],
        compiler_params=PARAMS,
        name="coeff_grads",
    )(colours, positions, rows)


def exchange(rows, axis, peers):
    sent = rows.reshape(peers, 1, -1)
    got = lax.all_to_all(sent, axis, split_axis=0, concat_axis=0, tiled=True)
    return got.reshape(rows.shape)


def on_device(
    proj,
    sh_coeffs,
    positions,
    camera,
    send_index,
    send_count,
    tile_xy,
    tile_list,
    tile_len,
    pixel_grad,
):
    index = send_index.reshape(CAP, PEERS)
    outgoing, high, low_hot = owner(
        camera, proj.reshape(384, 128), sh_coeffs, positions, index, send_count
    )
    received = exchange(outgoing, ORDER, PEERS)
    slot_grads = render(
        tile_xy[0], tile_len, received, tile_list[0], pixel_grad.reshape(24, 128)
    )
    returned = exchange(slot_grads, ORDER, PEERS)
    grad_rows, colours = sum_returned(camera, returned, high, low_hot)
    colours = exchange(colours, "img", 4)
    grad_sh, grad_rows = coefficients(colours, positions, grad_rows)
    return (grad_rows.reshape(proj.shape), grad_sh)


def solution(mesh):
    bits = jax.sharding.Mesh(mesh.devices.reshape((2,) * len(CELL) + (-1,)), CELL + ("img",))
    return jax.shard_map(
        on_device,
        mesh=bits,
        in_specs=(
            P("img", None, CELL),
            P(None, CELL),
            P(None, CELL),
            P("img", None),
            P("img", CELL),
            P("img", CELL),
            P("img", None, CELL),
            P("img", CELL, None),
            P("img", CELL),
            P("img", None, CELL),
        ),
        out_specs=(P("img", None, CELL), P(None, CELL + ("img",))),
        check_vma=False,
    )
```

```python
import functools

import jax
import jax.numpy as jnp
from jax import lax
from jax.experimental import pallas as pl
from jax.experimental.pallas import tpu as pltpu
from jax.sharding import PartitionSpec as P

SH_ZERO = 0.28209479177387814
SH_ONE = 0.4886025119029199
SH_TWO = (
    1.0925484305920792,
    -1.0925484305920792,
    0.31539156525252005,
    -1.0925484305920792,
    0.5462742152960396,
)
SH_THREE = (
    -0.5900435899266435,
    2.890611442640554,
    -0.4570457994644658,
    0.3731763325901154,
    -0.4570457994644658,
    1.445305721320277,
    -0.5900435899266435,
)

F32 = jnp.float32
BF16 = jnp.bfloat16
PEERS = 128
CAP = 32
COMPS = 9
TILES = 4
DEPTH = 256
LOW = 256
HIGH = 32
PACK = 56
NOTHING = -1.0e4
CELL = ("y2", "y1", "y0", "z2", "z1", "z0", "core")
ORDER = ("y0", "y1", "y2", "z0", "z2", "z1", "core")
LOG2E = 1.4426950408889634
EARLY = 6
LANED = 2
ALONE = 3

LINEAR = (
    (SH_ZERO, 0, 0, 0),
    (0, 0, -SH_ONE, 0),
    (0, 0, 0, SH_ONE),
    (0, -SH_ONE, 0, 0),
    (0, SH_TWO[0], 0, 0),
    (0, 0, SH_TWO[1], 0),
    (SH_TWO[2], 0, 0, 0),
    (0, SH_TWO[3], 0, 0),
    (SH_TWO[4], 0, 0, 0),
    (0, 0, SH_THREE[0], 0),
    (0, SH_THREE[1], 0, 0),
    (0, 0, SH_THREE[2], 0),
    (0, 0, 0, SH_THREE[3]),
    (0, SH_THREE[4], 0, 0),
    (0, 0, 0, SH_THREE[5]),
    (0, SH_THREE[6], 0, 0),
)
QUADRATIC = (
    (1, 0, 0, 0, 0, 0, 0),
    (1, 0, 0, 0, 0, 0, 0),
    (1, 0, 0, 0, 0, 0, 0),
    (1, 0, 0, 0, 0, 0, 0),
    (0, 1, 0, 0, 0, 0, 0),
    (0, 0, 1, 0, 0, 0, 0),
    (0, 0, 0, -1, -1, 2, 0),
    (0, 0, 1, 0, 0, 0, 0),
    (0, 0, 0, 1, -1, 0, 0),
    (0, 0, 0, 3, -1, 0, 0),
    (0, 0, 0, 0, 0, 0, 1),
    (0, 0, 0, -1, -1, 4, 0),
    (0, 0, 0, -3, -3, 2, 0),
    (0, 0, 0, -1, -1, 4, 0),
    (0, 0, 0, 1, -1, 0, 0),
    (0, 0, 0, 1, -3, 0, 0),
)


def dot(left, right):
    return lax.dot_general(left, right, (((1,), (0,)), ((), ())), preferred_element_type=F32)


def dot_t(left, right):
    return lax.dot_general(left, right, (((1,), (1,)), ((), ())), preferred_element_type=F32)


def one_hot(rows, index):
    same = rows.astype(jnp.int16) == index.astype(jnp.int16)
    return jnp.where(same, jnp.ones((), BF16), jnp.zeros((), BF16))


def stacked(first, second, right):
    both = dot(jnp.concatenate([first, second], axis=0), right)
    return both[: first.shape[0]] + both[first.shape[0] :]


def iota(shape, axis):
    return lax.broadcasted_iota(jnp.int32, shape, axis)


def split(value, parts):
    out = []
    for _ in range(parts - 1):
        head = value.astype(BF16).astype(F32)
        out.append(head)
        value = value - head
    out.append(value.astype(BF16).astype(F32))
    return out


def column_consts(table, half):
    rows = iota((8, 128), 0)
    out = []
    for col in range(len(table[0])):
        vals = [float(table[8 * half + i][col]) for i in range(8)]
        if not any(vals):
            out.append(None)
            continue
        acc = jnp.zeros((8, 128), F32)
        for i, val in enumerate(vals):
            if val:
                acc = jnp.where(rows == i, val, acc)
        out.append(acc)
    return out


def form(consts, values):
    total = None
    for const, value in zip(consts, values):
        if const is None:
            continue
        term = const if value is None else const * value
        total = term if total is None else total + term
    return total


def basis_consts():
    return [(column_consts(LINEAR, half), column_consts(QUADRATIC, half)) for half in range(2)]


def unit_terms(place, cam):
    offs = [at - centre for at, centre in zip(place, cam)]
    inv = lax.rsqrt(offs[0] * offs[0] + offs[1] * offs[1] + offs[2] * offs[2])
    xpos, ypos, zpos = [off * inv for off in offs]
    return xpos, ypos, zpos, xpos * xpos, ypos * ypos, zpos * zpos, ypos * zpos


def basis_halves(consts, terms):
    xpos, ypos, zpos, xsq, ysq, zsq, yz = terms
    return [
        form(lin, (None, xpos, ypos, zpos)) * form(quad, (None, ypos, zpos, xsq, ysq, zsq, yz))
        for lin, quad in consts
    ]


def repeated(ref, row):
    return jnp.broadcast_to(ref[row : row + 1, :], (8, 128))


def column_sums(blocks):
    rows = iota((8, 128), 0)
    low = rows < 4
    blocks = [
        jnp.where(low, blocks[i], blocks[i + 4])
        + pltpu.roll(jnp.where(low, blocks[i + 4], blocks[i]), 4, 0)
        for i in range(4)
    ]
    for step in (2, 1):
        low = (rows & step) == 0
        blocks = [
            jnp.where(low, blocks[i], blocks[i + step])
            + jnp.where(
                low, pltpu.roll(blocks[i], 8 - step, 0), pltpu.roll(blocks[i + step], step, 0)
            )
            for i in range(step)
        ]
    return blocks[0]


def flipped(value, bits):
    out = jnp.zeros_like(value)
    for i in range(bits):
        out = out | (((value >> i) & 1) << (bits - 1 - i))
    return out


def rank_of(peer):
    low = ((peer >> 1) & 1) << 3 | ((peer >> 3) & 1) << 2 | ((peer >> 2) & 1) << 1 | (peer & 1)
    return (flipped(peer >> 4, 3) << 4) | low


def slot_index(idx_ref, cnt_ref, low_scr, high_scr):
    order = [int(f"{row:05b}"[::-1], 2) for row in range(32)]
    turned = jnp.concatenate([idx_ref[row : row + 1, :] for row in order], axis=0)
    turned = jnp.transpose(turned.astype(F32)).astype(jnp.int32)
    slots = jnp.concatenate([turned[32 * i : 32 * i + 32] for i in range(4)], axis=1)
    rows, cols = iota((PEERS, PEERS), 0), iota((PEERS, PEERS), 1)
    perm = (rows == 4 * flipped(cols & 31, 5) + (cols >> 5)).astype(F32).astype(BF16)
    counts = jnp.broadcast_to(cnt_ref[...], (8, PEERS)).astype(F32).astype(BF16)
    counts = dot(counts, perm)[0:1].astype(jnp.int32)
    live = iota((CAP, PEERS), 0) < counts
    low_scr[...] = slots & (LOW - 1)
    high_scr[...] = jnp.where(live, slots >> 8, -1)


def peer_blocks(k):
    for part in range(4):
        for group in range(4):
            rank = ((part >> 1) << 3) | ((group & 1) << 2) | ((group >> 1) << 1) | (part & 1)
            yield 32 * part + 8 * group, pl.ds(3 * rank + k, 8, stride=48)


def pair_row(ref, base, pair):
    first = ref[pl.ds(base + 2 * pair, 1), :]
    second = ref[pl.ds(base + 2 * pair + 1, 1), :]
    return jnp.concatenate([first, second], axis=1)


def returned_row(ref, base, pair):
    first = ref[pl.ds(base + pair, 1), :]
    second = ref[pl.ds(base + CAP // 2 + pair, 1), :]
    return jnp.concatenate([first, second], axis=1)


def owner_kernel(
    cam_hbm,
    proj_hbm,
    sh_hbm,
    pos_hbm,
    idx_hbm,
    cnt_hbm,
    out_ref,
    high_scr,
    hot_ref,
    cam_ref,
    proj_ref,
    sh_ref,
    pos_ref,
    idx_ref,
    cnt_ref,
    col_scr,
    low_scr,
    rows_scr,
    sems,
):
    copies = [
        pltpu.make_async_copy(src, dst, sems.at[i])
        for i, (src, dst) in enumerate(
            (
                (idx_hbm, idx_ref),
                (cnt_hbm, cnt_ref),
                (proj_hbm, proj_ref),
                (cam_hbm, cam_ref),
                (pos_hbm, pos_ref),
                (sh_hbm.at[:, pl.ds(0, 4096)], sh_ref.at[:, pl.ds(0, 4096)]),
                (sh_hbm.at[:, pl.ds(4096, 4096)], sh_ref.at[:, pl.ds(4096, 4096)]),
            )
        )
    ]
    for copy in copies:
        copy.start()
    consts = basis_consts()
    for copy in copies[:2]:
        copy.wait()
    slot_index(idx_ref, cnt_ref, low_scr, high_scr)
    low_iota = iota((LOW, 256), 0)
    high_iota = iota((HIGH, 256), 0)

    def table(ref, comps):
        return jnp.concatenate(
            [ref[pl.ds(par, 32 * comps, stride=2), :] for par in range(2)], axis=1
        )

    partial = {}

    def pick(wide, mask, base, comps, pair):
        for comp in range(base, base + comps):
            at = 32 * (comp - base)
            kept = jnp.where(mask, wide[at : at + 32], 0.0)
            kept = (kept[0:8] + kept[8:16]) + (kept[16:24] + kept[24:32])
            for h in range(2):
                partial[comp, 2 * pair + h] = kept[:, 128 * h : 128 * h + 128]
            first = 8 * (pair // 4)
            if all((comp, first + i) in partial for i in range(8)):
                rows_scr[32 * comp + first : 32 * comp + first + 8, :] = column_sums(
                    [partial.pop((comp, first + i)) for i in range(8)]
                )

    def shade(chunk):
        lanes = slice(128 * chunk, 128 * chunk + 128)
        place = [jnp.broadcast_to(pos_ref[i : i + 1, lanes], (8, 128)) for i in range(3)]
        first, second = basis_halves(consts, unit_terms(place, cam))
        for chan in range(3):
            terms = sh_ref[16 * chan : 16 * chan + 8, lanes] * first
            partial["shade", chan, chunk] = (
                terms + sh_ref[16 * chan + 8 : 16 * chan + 16, lanes] * second
            )
            if chunk % 8 == 7:
                at = 64 * chan + chunk - 7
                col_scr[at : at + 8, :] = 0.5 + column_sums(
                    [partial.pop(("shade", chan, chunk - 7 + i)) for i in range(8)]
                )

    def hots(pair):
        hot = one_hot(low_iota, pair_row(low_scr, 0, pair))
        hot_ref[:, 256 * pair : 256 * pair + 256] = hot
        return hot

    def mask(pair):
        return high_iota == pair_row(high_scr, 0, pair)

    copies[2].wait()
    rows = split(table(proj_ref, 6)[32 * LANED :], 3)
    size = 192 - 32 * LANED
    exact = size - 32
    rows = jnp.concatenate([rows[0], rows[1], rows[2][:exact]], axis=0).astype(BF16)
    both = 2 * size + exact

    def sum_rows(wide):
        first = wide[:exact] + wide[size : size + exact] + wide[2 * size : both]
        return jnp.concatenate([first, wide[exact:size] + wide[size + exact : 2 * size]], axis=0)

    lanes_of = [(high_scr[8 * b : 8 * b + 8, :] << 1) | (low_scr[8 * b : 8 * b + 8, :] >> 7) for b in range(4)]
    dead = [high_scr[8 * b : 8 * b + 8, :] < 0 for b in range(4)]
    lanes_of = [jnp.where(d, -1, v) for d, v in zip(dead, lanes_of)]
    within = [low_scr[8 * b : 8 * b + 8, :] & 127 for b in range(4)]
    found = [[jnp.zeros((8, 128), F32) for _ in range(4)] for _ in range(LANED)]

    def lane_gather(block):
        mine = [v == block for v in lanes_of]
        for comp in range(LANED):
            at = 64 * comp + block
            row = jnp.broadcast_to(proj_ref[at : at + 1, :], (8, 128))
            for b in range(4):
                value = jnp.take_along_axis(row, within[b], axis=1)
                found[comp][b] = jnp.where(mine[b], value, found[comp][b])

    cam, chunk = None, 0
    for pair in range(EARLY):
        hot = hots(pair)
        pick(sum_rows(dot(rows, hot)), mask(pair), LANED, 6 - LANED, pair)
        for block in range(4 * pair, 4 * pair + 4):
            lane_gather(block)
        if pair == ALONE - 1:
            for copy in copies[3:6]:
                copy.wait()
            cam = [jnp.broadcast_to(cam_ref[0:1, i : i + 1], (8, 128)) for i in range(3)]
        if pair >= ALONE:
            for _ in range(-(-64 // (EARLY - ALONE))):
                if chunk == 32:
                    copies[6].wait()
                if chunk < 64:
                    shade(chunk)
                    chunk += 1
    tints = jnp.concatenate(split(table(col_scr, 3), 2), axis=0).astype(BF16)
    everything = jnp.concatenate([rows, tints], axis=0)
    for pair in range(EARLY, CAP // 2):
        wide = dot(everything, hots(pair))
        pick(sum_rows(wide), mask(pair), LANED, 6 - LANED, pair)
        pick(wide[both : both + 96] + wide[both + 96 :], mask(pair), 6, 3, pair)
        for block in range(4 * pair, 4 * pair + 4):
            lane_gather(block)
    for pair in range(EARLY):
        wide = dot(tints, hot_ref[:, 256 * pair : 256 * pair + 256])
        pick(wide[:96] + wide[96:], mask(pair), 6, 3, pair)

    for comp in range(LANED):
        for b in range(4):
            rows_scr[32 * comp + 8 * b : 32 * comp + 8 * b + 8, :] = found[comp][b]
    rows_scr[32 * COMPS :, :] = jnp.zeros((96, 128), F32)
    for k in range(3):
        turned = jnp.transpose(rows_scr[128 * k : 128 * k + 128, :])
        for at, rows in peer_blocks(k):
            out_ref[rows, :] = turned[at : at + 8]


def render_kernel(
    xy_ref, len_ref, recv_ref, list_ref, grad_ref, out_ref, table_scr, coef_scr, right_scr, sums_scr
):
    for k in range(3):
        table_scr[128 * k : 128 * k + 128, :] = jnp.transpose(
            recv_ref[pl.ds(k, PEERS, stride=3), :]
        )

    slots = jnp.concatenate(
        [list_ref[t : t + 1, 128 * h : 128 * h + 128] for t in range(TILES) for h in range(2)],
        axis=0,
    )
    peer, place = rank_of(slots >> 5), slots & (CAP - 1)
    row_iota = iota((8, 128), 0)

    def by_tile(ref, row):
        out = jnp.zeros((8, 128), jnp.int32)
        for t in range(TILES):
            out = jnp.where(
                row_iota >> 1 == t, jnp.broadcast_to(ref[row : row + 1, t : t + 1], (8, 128)), out
            )
        return out

    centre_x = (by_tile(xy_ref, 0).astype(F32) * 16.0 + 8.0) / 128.0
    centre_y = (by_tile(xy_ref, 1).astype(F32) * 16.0 + 8.0) / 128.0
    inside = (row_iota & 1) * 128 + iota((8, 128), 1) < by_tile(len_ref, 0)

    vals = [jnp.zeros((8, 128), F32) for _ in range(COMPS)]
    for q in range(CAP):
        mine = place == q
        for c in range(COMPS):
            row = jnp.broadcast_to(table_scr[32 * c + q : 32 * c + q + 1, :], (8, 128))
            vals[c] = jnp.where(mine, jnp.take_along_axis(row, peer, axis=1), vals[c])

    mean_x, mean_y, ca, cb, cc, opac = vals[:6]
    xrel, yrel = mean_x - centre_x, mean_y - centre_y
    shown = opac > 0.0
    lead_x = ca * xrel + cb * yrel
    lead_y = cc * yrel + cb * xrel
    const = -0.5 * (xrel * lead_x + yrel * lead_y) + jnp.log(jnp.where(shown, opac, 1.0))
    const = jnp.where(shown & inside, const, NOTHING)
    for i, value in enumerate((const, lead_x, lead_y, -0.5 * ca, -0.5 * cc, -cb)):
        coef_scr[8 * i : 8 * i + 8, :] = LOG2E * value
    tint = [split(v, 3) for v in vals[6:9]]
    for block, (one, two) in enumerate(((0, 0), (1, 0), (2, 1))):
        for c in range(3):
            right_scr[64 * block + 8 * c : 64 * block + 8 * c + 8, :] = tint[c][one]
            right_scr[64 * block + 24 + 8 * c : 64 * block + 32 + 8 * c, :] = tint[c][two]
        right_scr[64 * block + 48 : 64 * block + 64, :] = jnp.zeros((16, 128), F32)
    right_scr[192:256, :] = jnp.zeros((64, 128), F32)

    blank = jnp.zeros((2, 256), F32)
    blocks, sides = [], []
    for tile in range(TILES):
        grads = jnp.concatenate(
            [
                jnp.concatenate(
                    [grad_ref[8 * c + 2 * tile + h : 8 * c + 2 * tile + h + 1, :] for h in range(2)],
                    axis=1,
                )
                for c in range(3)
            ],
            axis=0,
        )
        g0, g1, g2 = split(grads, 3)
        blocks += [g0, g1, blank, g0, g2, blank, g0, g1, blank, jnp.zeros((8, 256), F32)]
        zero5 = jnp.zeros((5, 256), F32)
        sides.append(jnp.concatenate([g0, zero5, g1, zero5], axis=0).astype(BF16))
    turned = jnp.transpose(jnp.concatenate(blocks, axis=0)).astype(BF16)

    column = (iota((16, DEPTH), 0).astype(F32) - 7.5) / 128.0
    before = (iota((DEPTH, DEPTH), 0) < iota((DEPTH, DEPTH), 1)).astype(F32).astype(BF16)
    after = (iota((DEPTH, DEPTH), 0) > iota((DEPTH, DEPTH), 1)).astype(F32).astype(BF16)

    def both(ref, tile):
        return jnp.concatenate(
            [ref[pl.ds(2 * tile + h, 32, stride=8), :] for h in range(2)], axis=1
        ).astype(BF16)

    side = [column[8 * g : 8 * g + 8, :128] for g in range(2)]

    def exponents(tile):
        halves = []
        for h in range(2):
            at = 2 * tile + h
            rows = [
                jnp.broadcast_to(coef_scr[8 * i + at : 8 * i + at + 1, :], (8, 128))
                for i in range(6)
            ]
            along = [rows[0] + u * (rows[1] + u * rows[3]) for u in side]
            across = [rows[2] + u * rows[5] for u in side]
            blocks = []
            for i in range(16):
                vpos = (i - 7.5) / 128.0
                bend = vpos * rows[4]
                blocks += [along[g] + vpos * (across[g] + bend) for g in range(2)]
            halves.append(jnp.concatenate(blocks, axis=0))
        return jnp.concatenate(halves, axis=1)

    def front(tile):
        alpha = jnp.exp2(exponents(tile))
        logs = jnp.log(1.0 - alpha)
        l0 = logs.astype(BF16)
        return alpha, l0, (logs - l0.astype(F32)).astype(BF16)

    def middle(tile, alpha, l0, l1):
        weight = alpha * jnp.exp(stacked(l0, l1, before))
        flow = dot(turned[:, 32 * tile : 32 * tile + 32], both(right_scr, tile)) * weight
        s0 = flow.astype(BF16)
        return weight, flow, s0, (flow - s0.astype(F32)).astype(BF16)

    def back(tile, alpha, weight, flow, s0, s1):
        power = flow - stacked(s0, s1, after) * (alpha / (1.0 - alpha))
        w0 = weight.astype(BF16)
        w1 = (weight - w0.astype(F32)).astype(BF16)
        colours = dot(sides[tile], w0)
        colours = colours[0:8] + colours[8:16] + dot(sides[tile], w1)[0:8]

        plain = linear = square = None
        for i in range(8):
            vpos = (7.5 - i) / 128.0
            top, bottom = power[16 * i : 16 * i + 16], power[240 - 16 * i : 256 - 16 * i]
            total, slope = top + bottom, (bottom - top) * vpos
            curve = total * (vpos * vpos)
            plain = total if plain is None else plain + total
            linear = slope if linear is None else linear + slope
            square = curve if square is None else square + curve
        sums = [
            plain,
            plain * column,
            linear,
            plain * (column * column),
            square,
            linear * column,
        ]
        rows = [jnp.sum(v, axis=0, keepdims=True) for v in sums]
        rows += [colours[i : i + 1] for i in range(3)]
        for i, row in enumerate(rows):
            for h in range(2):
                sums_scr[8 * i + 2 * tile + h : 8 * i + 2 * tile + h + 1, :] = row[
                    :, 128 * h : 128 * h + 128
                ]

    for first in range(0, TILES, 2):
        group = (first, first + 1)
        fronts = [front(tile) for tile in group]
        middles = [middle(tile, *fronts[tile - first]) for tile in group]
        for tile in group:
            back(tile, fronts[tile - first][0], *middles[tile - first])

    m0, mu, mv, muu, mvv, muv, red, green, blue = [sums_scr[8 * i : 8 * i + 8, :] for i in range(9)]
    grads = [
        ca * mu + cb * mv - lead_x * m0,
        cc * mv + cb * mu - lead_y * m0,
        -0.5 * (muu - 2.0 * xrel * mu + xrel * xrel * m0),
        -(muv - yrel * mu - xrel * mv + xrel * yrel * m0),
        -0.5 * (mvv - 2.0 * yrel * mv + yrel * yrel * m0),
        jnp.where(shown, m0 / jnp.where(shown, opac, 1.0), 0.0),
        red,
        green,
        blue,
    ]
    grads = [split(grad, 2) for grad in grads]
    column_iota, place_iota = iota((2 * PEERS, 128), 0), iota((CAP // 2, 128), 0)
    column_of, row_of = peer + PEERS * (place & 1), place >> 1
    hots, wides = [], []
    for r in range(8):
        hots.append(one_hot(column_iota, column_of[r : r + 1]))
        mine = place_iota == row_of[r : r + 1]
        wides.append(
            jnp.concatenate(
                [
                    jnp.where(mine, grads[c][part][r : r + 1], 0.0)
                    for part in range(2)
                    for c in range(COMPS)
                ],
                axis=0,
            ).astype(BF16)
        )
    total = dot_t(jnp.concatenate(wides, axis=1), jnp.concatenate(hots, axis=1))
    half = 16 * COMPS
    total = total[:half] + total[half:]
    total = jnp.concatenate(
        [
            total[16 * c : 16 * c + 16, PEERS * bit : PEERS * bit + PEERS]
            for c in range(COMPS)
            for bit in range(2)
        ]
        + [jnp.zeros((96, 128), F32)],
        axis=0,
    )
    for k in range(3):
        out_ref[pl.ds(k, PEERS, stride=3), :] = jnp.transpose(total[128 * k : 128 * k + 128])


def sum_slots(comps, back_ref, high_ref, hot_ref, rows_scr):
    for k in sorted({comp // 4 for comp in comps}):
        block = jnp.concatenate([back_ref[rows, :] for _, rows in peer_blocks(k)], axis=0)
        rows_scr[128 * k : 128 * k + 128, :] = jnp.transpose(block)
    high_iota = iota((HIGH, 256), 0)
    total = None
    for step in range(4):
        wides = []
        for pair in range(4 * step, 4 * step + 4):
            mask = high_iota == pair_row(high_ref, 0, pair)
            both = [split(returned_row(rows_scr, 32 * comp, pair), 2) for comp in comps]
            wides.append(
                jnp.concatenate(
                    [jnp.where(mask, b[part], 0.0) for part in range(2) for b in both], axis=0
                ).astype(BF16)
            )
        term = dot_t(
            jnp.concatenate(wides, axis=1), hot_ref[:, 1024 * step : 1024 * step + 1024]
        )
        total = term if total is None else total + term
    size = 32 * len(comps)
    return total[:size] + total[size:]


def sum_kernel(cam_ref, back_ref, high_ref, hot_ref, out_ref, col_ref, rows_scr):
    total = sum_slots(range(COMPS), back_ref, high_ref, hot_ref, rows_scr)
    for par in range(2):
        out_ref[pl.ds(par, 192, stride=2), :] = total[:192, 128 * par : 128 * par + 128]
        for share in range(4):
            for chan in range(3):
                first = 192 + 32 * chan + 8 * share
                col_ref[pl.ds(PACK * share + 16 * chan + par, 8, stride=2), :] = total[
                    first : first + 8, 128 * par : 128 * par + 128
                ]
    lanes = iota((8, 128), 1)
    row = jnp.zeros((8, 128), F32)
    for i in range(3):
        row = jnp.where(lanes == i, jnp.broadcast_to(cam_ref[0:1, i : i + 1], (8, 128)), row)
    for share in range(4):
        col_ref[PACK * share + 48 : PACK * share + 56, :] = jnp.where(
            lanes == 3, float(share), row
        )


def coeff_kernel(col_ref, pos_ref, rows_ref, out_hbm, rows_hbm, out_scr, unit_scr, sems):
    keep = pltpu.make_async_copy(rows_ref, rows_hbm, sems.at[4])
    keep.start()
    consts = basis_consts()
    share = jnp.max(col_ref[48:49, 3:4]).astype(jnp.int32)
    for i in range(3):
        for at in range(16):
            lanes = pl.ds(pl.multiple_of(share * 2048 + at * 128, 128), 128)
            unit_scr[16 * i + at : 16 * i + at + 1, :] = pos_ref[i : i + 1, lanes]
    place = [unit_scr[16 * i : 16 * i + 16, :] for i in range(3)]
    for image in range(4):
        row = col_ref[PACK * image + 48 : PACK * image + 49, :]
        cam = [jnp.broadcast_to(row[:, i : i + 1], (16, 128)) for i in range(3)]
        for i, term in enumerate(unit_terms(place, cam)):
            at = 112 * image + 16 * i
            unit_scr[at : at + 16, :] = term

    def chunk(step):
        totals = [[None, None] for _ in range(3)]
        for image in range(4):
            halves = basis_halves(
                consts, [repeated(unit_scr, 112 * image + 16 * i + step) for i in range(7)]
            )
            for chan in range(3):
                grad = repeated(col_ref, PACK * image + 16 * chan + step)
                for half in range(2):
                    term = grad * halves[half]
                    old = totals[chan][half]
                    totals[chan][half] = term if old is None else old + term
        for chan in range(3):
            for half in range(2):
                at = 16 * chan + 8 * half
                out_scr[at : at + 8, 128 * step : 128 * step + 128] = totals[chan][half]

    copies = []
    for piece in range(4):
        for step in range(4 * piece, 4 * piece + 4):
            chunk(step)
        lanes = pl.ds(512 * piece, 512)
        copies.append(
            pltpu.make_async_copy(out_scr.at[:, lanes], out_hbm.at[:, lanes], sems.at[piece])
        )
        copies[-1].start()
    keep.wait()
    for copy in copies:
        copy.wait()


VMEM = pl.BlockSpec(memory_space=pltpu.VMEM)
HBM = pl.BlockSpec(memory_space=pltpu.HBM)
PARAMS = pltpu.CompilerParams(vmem_limit_bytes=40 * 1024 * 1024)


def shape(*dims):
    return jax.ShapeDtypeStruct(dims, F32)


def in_hbm(array):
    return pltpu.with_memory_space_constraint(array, pltpu.HBM)


def owner(camera, proj, coeffs, positions, index, count):
    return pl.pallas_call(
        owner_kernel,
        out_shape=(
            shape(384, 128),
            jax.ShapeDtypeStruct((CAP, PEERS), jnp.int32),
            jax.ShapeDtypeStruct((LOW, CAP * PEERS), BF16),
        ),
        in_specs=[HBM] * 6,
        out_specs=[VMEM] * 3,
        scratch_shapes=[
            pltpu.VMEM((1, 3), F32),
            pltpu.VMEM((384, 128), F32),
            pltpu.VMEM((48, 8192), F32),
            pltpu.VMEM((3, 8192), F32),
            pltpu.VMEM((CAP, PEERS), jnp.int32),
            pltpu.VMEM((1, PEERS), jnp.int32),
            pltpu.VMEM((192, 128), F32),
            pltpu.VMEM((CAP, PEERS), jnp.int32),
            pltpu.VMEM((384, 128), F32),
            pltpu.SemaphoreType.DMA((7,)),
        ],
        compiler_params=PARAMS,
        name="owner_rows",
    )(*[in_hbm(x) for x in (camera, proj, coeffs, positions, index, count)])


def render(tile_xy, tile_len, received, tile_list, pixel_grad):
    return pl.pallas_call(
        render_kernel,
        out_shape=shape(384, 128),
        in_specs=[VMEM] * 5,
        out_specs=VMEM,
        scratch_shapes=[
            pltpu.VMEM((384, 128), F32),
            pltpu.VMEM((48, 128), F32),
            pltpu.VMEM((256, 128), F32),
            pltpu.VMEM((72, 128), F32),
        ],
        compiler_params=PARAMS,
        name="render_tiles",
    )(tile_xy, tile_len, received, tile_list, pixel_grad)


def sum_returned(camera, returned, high, low_hot):
    return pl.pallas_call(
        sum_kernel,
        out_shape=(shape(384, 128), shape(4 * PACK, 128)),
        in_specs=[VMEM] * 4,
        out_specs=[VMEM] * 2,
        scratch_shapes=[pltpu.VMEM((384, 128), F32)],
        compiler_params=PARAMS,
        name="owner_sums",
    )(camera, returned, high, low_hot)


def coefficients(colours, positions, rows):
    return pl.pallas_call(
        coeff_kernel,
        out_shape=(shape(48, 2048), shape(384, 128)),
        in_specs=[VMEM] * 3,
        out_specs=[HBM] * 2,
        scratch_shapes=[
            pltpu.VMEM((48, 2048), F32),
            pltpu.VMEM((448, 128), F32),
            pltpu.SemaphoreType.DMA((5,)),
        ],
        compiler_params=PARAMS,
        name="coeff_grads",
    )(colours, positions, rows)


def exchange(rows, axis, peers):
    sent = rows.reshape(peers, 1, -1)
    got = lax.all_to_all(sent, axis, split_axis=0, concat_axis=0, tiled=True)
    return got.reshape(rows.shape)


def on_device(
    proj,
    sh_coeffs,
    positions,
    camera,
    send_index,
    send_count,
    tile_xy,
    tile_list,
    tile_len,
    pixel_grad,
):
    index = send_index.reshape(CAP, PEERS)
    outgoing, high, low_hot = owner(
        camera, proj.reshape(384, 128), sh_coeffs, positions, index, send_count
    )
    received = exchange(outgoing, ORDER, PEERS)
    slot_grads = render(
        tile_xy[0], tile_len, received, tile_list[0], pixel_grad.reshape(24, 128)
    )
    returned = exchange(slot_grads, ORDER, PEERS)
    grad_rows, colours = sum_returned(camera, returned, high, low_hot)
    colours = exchange(colours, "img", 4)
    grad_sh, grad_rows = coefficients(colours, positions, grad_rows)
    return (grad_rows.reshape(proj.shape), grad_sh)


def solution(mesh):
    bits = jax.sharding.Mesh(mesh.devices.reshape((2,) * len(CELL) + (-1,)), CELL + ("img",))
    return jax.shard_map(
        on_device,
        mesh=bits,
        in_specs=(
            P("img", None, CELL),
            P(None, CELL),
            P(None, CELL),
            P("img", None),
            P("img", CELL),
            P("img", CELL),
            P("img", None, CELL),
            P("img", CELL, None),
            P("img", CELL),
            P("img", None, CELL),
        ),
        out_specs=(P("img", None, CELL), P(None, CELL + ("img",))),
        check_vma=False,
    )
```
